32 devices in a mesh: tile: 8 (over z, y), freq: 4 (over x, core).
Axes of the slice: x: 2, y: 2, z: 4, core: 2. Of those that a mesh axis runs over, the one named last changes fastest.
Arguments:
- source_field: float32 [2, 8, 192, 1024], P(None, 'freq', 'tile'), may hold values from -6 to 6
- receiver_field: float32 [2, 8, 192, 1024], P(None, 'freq', 'tile'), may hold values from -6 to 6
- slowness: float32 [2, 192, 1024], P(None, 'tile', 'freq'), may hold values from 0.5 to 1
- frequency: float32 [8], P('freq'), may hold values from 0.5 to 2
- order_table: int32 [2, 8], P(None, 'freq'), may hold values from 2 to 4, as said below
- filter_coeffs: float32 [2, 5, 3], replicated, may hold values from -2 to 2
- aperture: int32 [8], replicated, may hold values from 8 to 24, as said below
Outputs:
- image_out: float32 [2, 192, 1024], P(None, 'tile', 'freq')
- receiver_out: float32 [2, 8, 192, 1024], P(None, 'freq', 'tile')
The draws below stay inside these ranges and needn't reach their ends.
Inputs may be any that keep to these rules, and one draw needn't show every extreme that they name: Tile t holds aperture[t] grid rows; the entries sum to 128, and some tile holds exactly 24. `order_table`: the order 4 occurs in every draw.
All inputs are finite; a program needn't handle non-finite values.
Results may differ from the reference program's by a relative error of at most 0.0003.
Values sent between devices are 32-bit elements; how exact they have to be, the bound alone decides.
No kernel may reach another device: no remote copies, remote signals or barrier semaphores. Data moves between devices by JAX's collectives and lax.ppermute only.
A program may use at most 64 MiB of HBM per device.

```python
import math
import jax
import jax.numpy as jnp
from jax import lax

ROWS = 16
NY = 1024
ORDER = 4
POWERS = 3
NDEPTH = 2
CAP = 24
NX = 128
FREQS = 8
N_TILE = 8


def draw_aperture(key, part):
    tile_count = NX // ROWS
    half_rows = ROWS // 2
    shifts = jax.random.randint(key, (tile_count,), 0, half_rows + 1)
    shifts = shifts.at[0].set(half_rows).at[1].set(0)
    return (ROWS + shifts - jnp.roll(shifts, -1)).astype(jnp.int32)


def draw_order_table(key, part):
    order_draw = jax.random.randint(key, (NDEPTH, FREQS), 2, ORDER + 1)
    order_draw = order_draw.at[0, 0].set(ORDER).at[NDEPTH - 1, FREQS - 1].set(2)
    return order_draw.astype(jnp.int32)


def block_levels(own_key, extent, cuts, smallest, high):
    def one(axis_at, parts):
        heights = jax.random.uniform(jax.random.fold_in(jax.random.fold_in(own_key, 6), axis_at), (parts,), jnp.float32, smallest / len(cuts), high / len(cuts))
        return jnp.repeat(jnp.exp(heights), extent[axis_at] // parts).reshape((-1,) + (1,) * (len(extent) - axis_at - 1))

    factor_of = one(*cuts[0])
    for cut in cuts[1:]:
        factor_of = factor_of * one(*cut)
    return factor_of


def scatter_about(key, extent, scale, reach, shards=(), held_as=jnp.bfloat16):
    gain = block_levels(key, extent, shards, -0.22, 0.18) if shards else 1.0
    array = jax.random.normal(key, extent, jnp.float32) * scale * gain
    return jnp.minimum(jnp.maximum(array, -reach), reach).astype(held_as)


def setup_inputs(seed: int = 0) -> dict:
    arg_keys = jax.random.split(jax.random.key(seed), 8)
    source_field = scatter_about(arg_keys[0], (2, FREQS, N_TILE * CAP, NY), 1.0, 6.0, ((1, 4), (2, 8)), jnp.float32)
    receiver_field = scatter_about(arg_keys[1], (2, FREQS, N_TILE * CAP, NY), 1.0, 6.0, ((1, 4), (2, 8)), jnp.float32)
    slowness = jnp.clip(jnp.exp(math.log(1.0) - 0.6931472 * jax.random.uniform(arg_keys[2], (NDEPTH, N_TILE * CAP, NY), jnp.float32) ** block_levels(arg_keys[2], (NDEPTH, N_TILE * CAP, NY), ((1, 8), (2, 4)), -0.2, 0.2)), 0.5, 1.0)
    frequency = jnp.clip(jnp.exp(math.log(2.0) - 1.3862944 * jax.random.uniform(arg_keys[3], (FREQS,), jnp.float32) ** block_levels(arg_keys[3], (FREQS,), ((0, 4),), -0.2, 0.2)), 0.5, 2.0)
    order_table = draw_order_table(jax.random.fold_in(arg_keys[7], 71), 0)
    filter_coeffs = scatter_about(arg_keys[5], (2, ORDER + 1, POWERS), 0.15, 2.0, (), jnp.float32)
    aperture = draw_aperture(jax.random.fold_in(arg_keys[7], 71), 0)
    return {"source_field": source_field, "receiver_field": receiver_field, "slowness": slowness, "frequency": frequency, "order_table": order_table, "filter_coeffs": filter_coeffs, "aperture": aperture}


def mcclellan(values):
    lead = [(0, 0)] * (values.ndim - 2)
    padded_x = jnp.pad(values, lead + [(1, 1), (0, 0)])
    blur_rows = 0.25 * (padded_x[..., :-2, :] + padded_x[..., 2:, :]) + 0.5 * values
    padded_cols = jnp.pad(blur_rows, lead + [(0, 0), (1, 1)])
    blur_cols = 0.25 * (padded_cols[..., :-2] + padded_cols[..., 2:]) + 0.5 * blur_rows
    return 2.0 * blur_cols - values


def weighted(term_index, cheb_term, wavenumber, coeffs, active):
    powers = coeffs.shape[2]
    coef_re = coeffs[0, term_index, powers - 1] + 0.0 * wavenumber
    coef_im = coeffs[1, term_index, powers - 1] + 0.0 * wavenumber
    for power_index in range(powers - 2, -1, -1):
        coef_re = coef_re * wavenumber + coeffs[0, term_index, power_index]
        coef_im = coef_im * wavenumber + coeffs[1, term_index, power_index]
    coef_re = coef_re * active
    coef_im = coef_im * active
    src_re = coef_re * cheb_term[0, 0] + coef_im * cheb_term[0, 1]
    src_im = coef_re * cheb_term[0, 1] - coef_im * cheb_term[0, 0]
    rec_re = coef_re * cheb_term[1, 0] - coef_im * cheb_term[1, 1]
    rec_im = coef_re * cheb_term[1, 1] + coef_im * cheb_term[1, 0]
    return jnp.stack([jnp.stack([src_re, src_im]), jnp.stack([rec_re, rec_im])])


def reference(source_field, receiver_field, slowness, frequency, order_table, filter_coeffs, aperture):
    starts = (jnp.cumsum(aperture) - aperture).astype(jnp.int32)
    global_row = jnp.arange(NX, dtype=jnp.int32)
    owner_tile = jnp.sum((global_row[:, None] >= starts[None, 1:]).astype(jnp.int32), axis=1).astype(jnp.int32)
    slot_index = (owner_tile * CAP + global_row - starts[owner_tile]).astype(jnp.int32)
    fields = jnp.stack([source_field[:, :, slot_index, :], receiver_field[:, :, slot_index, :]])
    fields = jnp.transpose(fields, (2, 0, 1, 3, 4))
    planes = slowness[:, slot_index, :]
    orders = jnp.transpose(order_table, (1, 0))

    def one_frequency(inputs):
        state, angular, order_column = inputs
        images = []
        for depth_index in range(NDEPTH):
            wavenumber = angular * planes[depth_index]
            previous = state
            current = mcclellan(state)
            result = weighted(0, previous, wavenumber, filter_coeffs, (order_column[depth_index] >= 0).astype(jnp.float32))
            result = result + weighted(1, current, wavenumber, filter_coeffs, (order_column[depth_index] >= 1).astype(jnp.float32))
            for term_index in range(2, ORDER + 1):
                following = 2.0 * mcclellan(current) - previous
                result = result + weighted(term_index, following, wavenumber, filter_coeffs, (order_column[depth_index] >= term_index).astype(jnp.float32))
                previous, current = current, following
            state = result
            images.append(state[0, 0] * state[1, 0] + state[0, 1] * state[1, 1])
        return jnp.stack(images), state[1]

    image_terms, receivers = lax.map(one_frequency, (fields, frequency, orders))
    image_sum = jnp.sum(image_terms, axis=0)
    stored = N_TILE * CAP
    image_out = jnp.zeros((NDEPTH, stored, NY), jnp.float32).at[:, slot_index, :].set(image_sum)
    receivers = jnp.transpose(receivers, (1, 0, 2, 3))
    receiver_out = jnp.zeros((2, receivers.shape[1], stored, NY), jnp.float32).at[:, :, slot_index, :].set(receivers)
    return image_out, receiver_out
```

```python
import jax
import jax.numpy as jnp
from jax import lax
from jax.experimental import pallas as pl
from jax.experimental.pallas import tpu as pltpu
from jax.sharding import PartitionSpec as P

ORDER = 4
NDEPTH = 2
HALO = ORDER * NDEPTH
PAD = 10
F32 = jnp.float32
VMEM = pl.BlockSpec(memory_space=pltpu.VMEM)
SMEM = pl.BlockSpec(memory_space=pltpu.SMEM)


def to_rows(flat, load_tile, row_tiles):
    for i in range(row_tiles):
        for j in range(8):
            flat[pl.ds((i * 8 + j) * 8, 8), :] = load_tile(i, j)


def row_of(flat, row):
    start = (row // 8) * 64 + row % 8
    return flat[pl.ds(start, 8, stride=8), :]


def pack_kernel(aperture, source, receiver, planes, ahead, behind, *flats):
    width = aperture[lax.axis_index("tile")]
    row_tiles = source.shape[2] // 8
    plane = 0
    for field in (source, receiver):
        for part in range(2):
            for freq in range(source.shape[1]):
                flat = flats[plane]
                to_rows(
                    flat,
                    lambda i, j: field[part, freq, pl.ds(8 * i, 8), pl.ds(128 * j, 128)],
                    row_tiles,
                )
                for k in range(HALO):
                    ahead[plane * HALO + k] = row_of(flat, width - HALO + k)
                    behind[plane * HALO + k] = row_of(flat, k)
                plane += 1
    flat = flats[plane]
    to_rows(
        flat,
        lambda i, j: planes[j // 2, 0, pl.ds(8 * i, 8), pl.ds(128 * (j % 2), 128)],
        row_tiles,
    )
    for k in range(ORDER):
        ahead[plane * HALO + k] = row_of(flat, width - ORDER + k)
        behind[plane * HALO + k] = row_of(flat, k)


def spread(above, here, below, before, masks):
    first_lane, last_lane, first_cell, last_cell = masks
    rows = (above + below) + (here + here)
    from_left = pltpu.roll(rows, 1, 1)
    from_right = pltpu.roll(rows, 127, 1)
    wrap_left = pltpu.roll(from_left, 1, 0)
    wrap_right = pltpu.roll(from_right, 7, 0)
    left = jnp.where(first_lane, jnp.where(first_cell, 0.0, wrap_left), from_left)
    right = jnp.where(last_lane, jnp.where(last_cell, 0.0, wrap_right), from_right)
    blurred = (left + right) + (rows + rows)
    if before is None:
        return 0.125 * blurred - here
    return (0.25 * blurred - (here + here)) - before


def main_kernel(
    aperture, frequency, order_table, filter_coeffs,
    source, receiver, planes, from_before, from_after,
    image_out, receiver_out,
    flat, slow, weights, images, *buffers,
):
    tile = lax.axis_index("tile")
    last_tile = lax.axis_size("tile") - 1
    width = aperture[tile]
    freqs = source.shape[1]
    stored = source.shape[2]
    row_tiles = stored // 8
    count = 4 * freqs
    start, middle = buffers[:count], buffers[count : 2 * count]
    terms = [buffers[(2 + n) * count : (3 + n) * count] for n in range(ORDER)]

    lane = lax.broadcasted_iota(jnp.int32, (8, 128), 1)
    sub = lax.broadcasted_iota(jnp.int32, (8, 128), 0)
    first_lane, last_lane = lane == 0, lane == 127
    masks = (first_lane, last_lane, sub == 0, sub == 7)

    base = PAD + HALO
    plane = 0
    for field in (source, receiver):
        for part in range(2):
            for freq in range(freqs):
                to_rows(
                    flat.at[plane % 2],
                    lambda i, j: field[part, freq, pl.ds(8 * i, 8), pl.ds(128 * j, 128)],
                    row_tiles,
                )
                for r in range(stored):
                    start[plane][base + r] = row_of(flat.at[plane % 2], r)
                for k in range(HALO):
                    start[plane][PAD + k] = from_before[plane * HALO + k]
                    start[plane][base + width + k] = from_after[plane * HALO + k]
                plane += 1
    for depth in range(NDEPTH):
        to_rows(
            flat.at[depth],
            lambda i, j: planes[j // 2, depth, pl.ds(8 * i, 8), pl.ds(128 * (j % 2), 128)],
            row_tiles,
        )
        for r in range(stored):
            slow[depth, base + r] = row_of(flat.at[depth], r)
    for k in range(ORDER):
        slow[0, base - ORDER + k] = from_before[count * HALO + k]
        slow[0, base + width + k] = from_after[count * HALO + k]

    @pl.when(tile == 0)
    def _():
        for p in range(count):
            start[p][base - 1] = jnp.zeros((8, 128), F32)
            for k in range(1, HALO):
                start[p][base - 1 - k] = -start[p][base + k - 1]
        slow[0, base - 1] = slow[0, base]
        for k in range(1, ORDER):
            slow[0, base - 1 - k] = slow[0, base + k - 1]

    @pl.when(tile == last_tile)
    def _():
        for p in range(count):
            start[p][base + width] = jnp.zeros((8, 128), F32)
            for k in range(1, HALO):
                start[p][base + width + k] = -start[p][base + width - k]
        slow[0, base + width] = slow[0, base + width - 1]
        for k in range(1, ORDER):
            slow[0, base + width + k] = slow[0, base + width - k]

    powers = filter_coeffs.shape[2]
    for depth in range(NDEPTH):
        for freq in range(freqs):
            for n in range(ORDER + 1):
                active = jnp.where(order_table[depth, freq] >= n, 1.0, 0.0)
                for c in range(2):
                    for m in range(powers):
                        weights[depth, freq, (n * 2 + c) * powers + m] = jnp.full(
                            (8, 128), filter_coeffs[c, n, m] * active, F32
                        )

    def weigh(depth, freq, row, slow_row, fields):
        wavenumber = frequency[freq] * slow[depth, slow_row]
        out = [None] * 4
        for n in range(ORDER + 1):
            def poly(c):
                at = (n * 2 + c) * powers
                value = weights[depth, freq, at + powers - 1]
                for m in range(powers - 2, -1, -1):
                    value = value * wavenumber + weights[depth, freq, at + m]
                return value

            re, im = poly(0), poly(1)
            level = fields if n == 0 else terms[n - 1]
            src_re, src_im, rec_re, rec_im = (level[q * freqs + freq][row] for q in range(4))
            part = (
                re * src_re + im * src_im,
                re * src_im - im * src_re,
                re * rec_re - im * rec_im,
                re * rec_im + im * rec_re,
            )
            out = part if n == 0 else tuple(a + b for a, b in zip(out, part))
        return out

    def sweep(depth, fields, results, rows, slow_shift):
        def step(i, carry):
            row = i - (2 * ORDER - 1)
            total = None
            for freq in range(freqs):
                out = weigh(depth, freq, row, row + slow_shift, fields)
                for q in range(4):
                    results[q * freqs + freq][row - ORDER] = out[q]
                term = out[0] * out[2] + out[1] * out[3]
                total = term if total is None else total + term
            images[depth, row - ORDER] = total
            for n in range(ORDER, 0, -1):
                row = i - 2 * (n - 1)
                level = fields if n == 1 else terms[n - 2]
                older = None if n == 1 else (fields if n == 2 else terms[n - 3])
                for p in range(count):
                    terms[n - 1][p][row] = spread(
                        level[p][row - 1], level[p][row], level[p][row + 1],
                        None if n == 1 else older[p][row], masks,
                    )
            return carry

        lax.fori_loop(PAD + 1, PAD + rows + ORDER - 1, step, 0)

    total_rows = stored + 2 * HALO
    sweep(0, start, middle, total_rows, 0)
    sweep(1, middle, start, total_rows - 2 * ORDER, ORDER)

    for depth in range(NDEPTH):
        shift = PAD + HALO - ORDER * (depth + 1)
        for r in range(stored):
            value = jnp.where(r < width, images[depth, shift + r], 0.0)
            image_out[pl.ds(depth * stored + r, 8, stride=NDEPTH * stored), :] = value
    for part in range(2):
        for freq in range(freqs):
            p = (2 + part) * freqs + freq
            for r in range(stored):
                at = (r // 8) * 64 + r % 8
                flat[p % 2, pl.ds(at, 8, stride=8), :] = jnp.where(
                    r < width, start[p][PAD + r], 0.0
                )
            for i in range(row_tiles):
                for j in range(8):
                    receiver_out[part, freq, pl.ds(8 * i, 8), pl.ds(128 * j, 128)] = flat[
                        p % 2, pl.ds((i * 8 + j) * 8, 8), :
                    ]


def image_kernel(parts, out):
    senders = 4
    depths, stored = out.shape[0], out.shape[1]
    size = parts.shape[0] // senders
    for j in range(size // (depths * stored)):
        for depth in range(depths):
            total = None
            for s in range(senders):
                at = s * size + (j * depths + depth) * stored
                term = parts[pl.ds(at, stored), :]
                total = term if total is None else total + term
            out[depth, :, pl.ds(128 * j, 128)] = total


def passed_along(value, axis, steps):
    count = lax.axis_size(axis)
    initial, last = (max(0, -steps), min(count, count - steps))
    return lax.ppermute(value, axis, [(source, source + steps) for source in range(initial, last)])


def shards(source_field, receiver_field, slowness, frequency, order_table, filter_coeffs, aperture):
    freqs, stored = source_field.shape[1:3]
    count = 4 * freqs
    planes = lax.all_gather(slowness, "freq", axis=0)
    halo = jax.ShapeDtypeStruct((count * HALO + ORDER, 8, 128), F32)
    ahead, behind = pl.pallas_call(
        pack_kernel,
        out_shape=(halo, halo),
        in_specs=[SMEM] + [VMEM] * 3,
        out_specs=(VMEM, VMEM),
        scratch_shapes=[pltpu.VMEM((stored * 8, 128), F32)] * (count + 1),
        compiler_params=pltpu.CompilerParams(vmem_limit_bytes=32 << 20),
        name="pack",
    )(aperture, source_field, receiver_field, planes)
    from_before = passed_along(ahead, "tile", 1)
    from_after = passed_along(behind, "tile", -1)
    rows = PAD + stored + 2 * HALO + PAD
    image_parts, receiver_out = pl.pallas_call(
        main_kernel,
        out_shape=(
            jax.ShapeDtypeStruct((8 * NDEPTH * stored, 128), F32),
            jax.ShapeDtypeStruct(receiver_field.shape, F32),
        ),
        in_specs=[SMEM] * 4 + [VMEM] * 5,
        out_specs=(VMEM, VMEM),
        scratch_shapes=[
            pltpu.VMEM((2, stored * 8, 128), F32),
            pltpu.VMEM((NDEPTH, rows, 8, 128), F32),
            pltpu.VMEM((NDEPTH, freqs, 2 * (ORDER + 1) * filter_coeffs.shape[2], 8, 128), F32),
            pltpu.VMEM((NDEPTH, rows, 8, 128), F32),
        ]
        + [pltpu.VMEM((rows, 8, 128), F32)] * (count * (2 + ORDER)),
        compiler_params=pltpu.CompilerParams(vmem_limit_bytes=48 << 20),
        name="migrate",
    )(
        aperture, frequency, order_table, filter_coeffs,
        source_field, receiver_field, planes, from_before, from_after,
    )
    exchanged = lax.all_to_all(image_parts, "freq", 0, 0, tiled=True)
    image_out = pl.pallas_call(
        image_kernel,
        out_shape=jax.ShapeDtypeStruct(slowness.shape, F32),
        in_specs=[VMEM],
        out_specs=VMEM,
        name="image",
    )(exchanged)
    return image_out, receiver_out


def solution(mesh):
    placed = (
        P(None, "freq", "tile", None),
        P(None, "freq", "tile", None),
        P(None, "tile", "freq"),
        P("freq"),
        P(None, "freq"),
        P(),
        P(),
    )
    return jax.shard_map(
        shards,
        mesh=mesh,
        in_specs=placed,
        out_specs=(P(None, "tile", "freq"), P(None, "freq", "tile", None)),
        check_vma=False,
    )
```

```python
import jax
import jax.numpy as jnp
from jax import lax
from jax.experimental import pallas as pl
from jax.experimental.pallas import tpu as pltpu
from jax.sharding import PartitionSpec as P

ORDER = 4
NDEPTH = 2
HALO = ORDER * NDEPTH
PAD = 10
F32 = jnp.float32
VMEM = pl.BlockSpec(memory_space=pltpu.VMEM)
SMEM = pl.BlockSpec(memory_space=pltpu.SMEM)


def to_rows(flat, load_tile, row_tiles):
    for i in range(row_tiles):
        for j in range(8):
            flat[pl.ds((i * 8 + j) * 8, 8), :] = load_tile(i, j)


def row_of(flat, row):
    start = (row // 8) * 64 + row % 8
    return flat[pl.ds(start, 8, stride=8), :]


def pack_kernel(aperture, source, receiver, planes, ahead, behind, *flats):
    width = aperture[lax.axis_index("tile")]
    row_tiles = source.shape[2] // 8
    plane = 0
    for field in (source, receiver):
        for part in range(2):
            for freq in range(source.shape[1]):
                flat = flats[plane]
                to_rows(
                    flat,
                    lambda i, j: field[part, freq, pl.ds(8 * i, 8), pl.ds(128 * j, 128)],
                    row_tiles,
                )
                for k in range(HALO):
                    ahead[plane * HALO + k] = row_of(flat, width - HALO + k)
                    behind[plane * HALO + k] = row_of(flat, k)
                plane += 1
    flat = flats[plane]
    to_rows(
        flat,
        lambda i, j: planes[j // 2, 0, pl.ds(8 * i, 8), pl.ds(128 * (j % 2), 128)],
        row_tiles,
    )
    for k in range(ORDER):
        ahead[plane * HALO + k] = row_of(flat, width - ORDER + k)
        behind[plane * HALO + k] = row_of(flat, k)


def spread(above, here, below, before, masks):
    first_lane, last_lane, first_cell, last_cell = masks
    rows = (above + below) + (here + here)
    from_left = pltpu.roll(rows, 1, 1)
    from_right = pltpu.roll(rows, 127, 1)
    wrap_left = pltpu.roll(from_left, 1, 0)
    wrap_right = pltpu.roll(from_right, 7, 0)
    left = jnp.where(first_lane, jnp.where(first_cell, 0.0, wrap_left), from_left)
    right = jnp.where(last_lane, jnp.where(last_cell, 0.0, wrap_right), from_right)
    blurred = (left + right) + (rows + rows)
    if before is None:
        return 0.125 * blurred - here
    return (0.25 * blurred - (here + here)) - before


def main_kernel(
    aperture, frequency, order_table, filter_coeffs,
    source, receiver, planes, from_before, from_after,
    image_out, receiver_out,
    flat, slow, weights, images, *buffers,
):
    tile = lax.axis_index("tile")
    last_tile = lax.axis_size("tile") - 1
    width = aperture[tile]
    freqs = source.shape[1]
    stored = source.shape[2]
    row_tiles = stored // 8
    count = 4 * freqs
    start, middle = buffers[:count], buffers[count : 2 * count]
    terms = [buffers[(2 + n) * count : (3 + n) * count] for n in range(ORDER)]

    lane = lax.broadcasted_iota(jnp.int32, (8, 128), 1)
    sub = lax.broadcasted_iota(jnp.int32, (8, 128), 0)
    first_lane, last_lane = lane == 0, lane == 127
    masks = (first_lane, last_lane, sub == 0, sub == 7)

    base = PAD + HALO
    plane = 0
    for field in (source, receiver):
        for part in range(2):
            for freq in range(freqs):
                to_rows(
                    flat.at[plane % 2],
                    lambda i, j: field[part, freq, pl.ds(8 * i, 8), pl.ds(128 * j, 128)],
                    row_tiles,
                )
                for r in range(stored):
                    start[plane][base + r] = row_of(flat.at[plane % 2], r)
                for k in range(HALO):
                    start[plane][PAD + k] = from_before[plane * HALO + k]
                    start[plane][base + width + k] = from_after[plane * HALO + k]
                plane += 1
    for depth in range(NDEPTH):
        to_rows(
            flat.at[depth],
            lambda i, j: planes[j // 2, depth, pl.ds(8 * i, 8), pl.ds(128 * (j % 2), 128)],
            row_tiles,
        )
        for r in range(stored):
            slow[depth, base + r] = row_of(flat.at[depth], r)
    for k in range(ORDER):
        slow[0, base - ORDER + k] = from_before[count * HALO + k]
        slow[0, base + width + k] = from_after[count * HALO + k]

    @pl.when(tile == 0)
    def _():
        for p in range(count):
            start[p][base - 1] = jnp.zeros((8, 128), F32)
            for k in range(1, HALO):
                start[p][base - 1 - k] = -start[p][base + k - 1]
        slow[0, base - 1] = slow[0, base]
        for k in range(1, ORDER):
            slow[0, base - 1 - k] = slow[0, base + k - 1]

    @pl.when(tile == last_tile)
    def _():
        for p in range(count):
            start[p][base + width] = jnp.zeros((8, 128), F32)
            for k in range(1, HALO):
                start[p][base + width + k] = -start[p][base + width - k]
        slow[0, base + width] = slow[0, base + width - 1]
        for k in range(1, ORDER):
            slow[0, base + width + k] = slow[0, base + width - k]

    powers = filter_coeffs.shape[2]
    for depth in range(NDEPTH):
        for freq in range(freqs):
            for n in range(ORDER + 1):
                active = jnp.where(order_table[depth, freq] >= n, 1.0, 0.0)
                for c in range(2):
                    for m in range(powers):
                        weights[depth, freq, (n * 2 + c) * powers + m] = jnp.full(
                            (8, 128), filter_coeffs[c, n, m] * active, F32
                        )

    def weigh(depth, freq, row, slow_row, fields):
        wavenumber = frequency[freq] * slow[depth, slow_row]
        out = [None] * 4
        for n in range(ORDER + 1):
            def poly(c):
                at = (n * 2 + c) * powers
                value = weights[depth, freq, at + powers - 1]
                for m in range(powers - 2, -1, -1):
                    value = value * wavenumber + weights[depth, freq, at + m]
                return value

            re, im = poly(0), poly(1)
            level = fields if n == 0 else terms[n - 1]
            src_re, src_im, rec_re, rec_im = (level[q * freqs + freq][row] for q in range(4))
            part = (
                re * src_re + im * src_im,
                re * src_im - im * src_re,
                re * rec_re - im * rec_im,
                re * rec_im + im * rec_re,
            )
            out = part if n == 0 else tuple(a + b for a, b in zip(out, part))
        return out

    def sweep(depth, fields, results, rows, slow_shift):
        def step(i, carry):
            row = i - (2 * ORDER - 1)
            total = None
            for freq in range(freqs):
                out = weigh(depth, freq, row, row + slow_shift, fields)
                for q in range(4):
                    results[q * freqs + freq][row - ORDER] = out[q]
                term = out[0] * out[2] + out[1] * out[3]
                total = term if total is None else total + term
            images[depth, row - ORDER] = total
            for n in range(ORDER, 0, -1):
                row = i - 2 * (n - 1)
                level = fields if n == 1 else terms[n - 2]
                older = None if n == 1 else (fields if n == 2 else terms[n - 3])
                for p in range(count):
                    terms[n - 1][p][row] = spread(
                        level[p][row - 1], level[p][row], level[p][row + 1],
                        None if n == 1 else older[p][row], masks,
                    )
            return carry

        lax.fori_loop(PAD + 1, PAD + rows + ORDER - 1, step, 0)

    total_rows = stored + 2 * HALO
    sweep(0, start, middle, total_rows, 0)
    sweep(1, middle, start, total_rows - 2 * ORDER, ORDER)

    columns = image_out.shape[3]
    for depth in range(NDEPTH):
        shift = PAD + HALO - ORDER * (depth + 1)
        for r in range(stored):
            at = (r // 8) * 64 + r % 8
            flat[depth, pl.ds(at, 8, stride=8), :] = jnp.where(
                r < width, images[depth, shift + r], 0.0
            )
        for i in range(row_tiles):
            for j in range(8):
                owner, column = (128 * j) // columns, (128 * j) % columns
                image_out[owner, depth, pl.ds(8 * i, 8), pl.ds(column, 128)] = flat[
                    depth, pl.ds((i * 8 + j) * 8, 8), :
                ]
    for part in range(2):
        for freq in range(freqs):
            p = (2 + part) * freqs + freq
            for r in range(stored):
                at = (r // 8) * 64 + r % 8
                flat[p % 2, pl.ds(at, 8, stride=8), :] = jnp.where(
                    r < width, start[p][PAD + r], 0.0
                )
            for i in range(row_tiles):
                for j in range(8):
                    receiver_out[part, freq, pl.ds(8 * i, 8), pl.ds(128 * j, 128)] = flat[
                        p % 2, pl.ds((i * 8 + j) * 8, 8), :
                    ]


def passed_along(value, axis, steps):
    count = lax.axis_size(axis)
    initial, last = (max(0, -steps), min(count, count - steps))
    return lax.ppermute(value, axis, [(source, source + steps) for source in range(initial, last)])


def shards(source_field, receiver_field, slowness, frequency, order_table, filter_coeffs, aperture):
    freqs, stored = source_field.shape[1:3]
    count = 4 * freqs
    planes = lax.all_gather(slowness, "freq", axis=0)
    halo = jax.ShapeDtypeStruct((count * HALO + ORDER, 8, 128), F32)
    ahead, behind = pl.pallas_call(
        pack_kernel,
        out_shape=(halo, halo),
        in_specs=[SMEM] + [VMEM] * 3,
        out_specs=(VMEM, VMEM),
        scratch_shapes=[pltpu.VMEM((stored * 8, 128), F32)] * (count + 1),
        compiler_params=pltpu.CompilerParams(vmem_limit_bytes=32 << 20),
        name="pack",
    )(aperture, source_field, receiver_field, planes)
    from_before = passed_along(ahead, "tile", 1)
    from_after = passed_along(behind, "tile", -1)
    rows = PAD + stored + 2 * HALO + PAD
    image_parts, receiver_out = pl.pallas_call(
        main_kernel,
        out_shape=(
            jax.ShapeDtypeStruct((lax.axis_size("freq"),) + slowness.shape, F32),
            jax.ShapeDtypeStruct(receiver_field.shape, F32),
        ),
        in_specs=[SMEM] * 4 + [VMEM] * 5,
        out_specs=(VMEM, VMEM),
        scratch_shapes=[
            pltpu.VMEM((2, stored * 8, 128), F32),
            pltpu.VMEM((NDEPTH, rows, 8, 128), F32),
            pltpu.VMEM((NDEPTH, freqs, 2 * (ORDER + 1) * filter_coeffs.shape[2], 8, 128), F32),
            pltpu.VMEM((NDEPTH, rows, 8, 128), F32),
        ]
        + [pltpu.VMEM((rows, 8, 128), F32)] * (count * (2 + ORDER)),
        compiler_params=pltpu.CompilerParams(vmem_limit_bytes=48 << 20),
        name="migrate",
    )(
        aperture, frequency, order_table, filter_coeffs,
        source_field, receiver_field, planes, from_before, from_after,
    )
    image_out = lax.psum_scatter(image_parts, "freq", scatter_dimension=0)
    return image_out, receiver_out


def solution(mesh):
    placed = (
        P(None, "freq", "tile", None),
        P(None, "freq", "tile", None),
        P(None, "tile", "freq"),
        P("freq"),
        P(None, "freq"),
        P(),
        P(),
    )
    return jax.shard_map(
        shards,
        mesh=mesh,
        in_specs=placed,
        out_specs=(P(None, "tile", "freq"), P(None, "freq", "tile", None)),
        check_vma=False,
    )
```

```python
from math import comb

import jax
import jax.numpy as jnp
import numpy as np
from jax import lax
from jax.experimental import pallas as pl
from jax.experimental.pallas import tpu as pltpu
from jax.sharding import PartitionSpec as P

ORDER = 4
NDEPTH = 2
HALO = ORDER * NDEPTH
F32 = jnp.float32
BF16 = jnp.bfloat16
VMEM = pl.BlockSpec(memory_space=pltpu.VMEM)
SMEM = pl.BlockSpec(memory_space=pltpu.SMEM)

SHIFTED = ((1,), (-1, 2), (1, -8, 8), (-1, 18, -48, 32), (1, -32, 160, -256, 128))


def y_weights():
    out = np.zeros((256, ORDER * 128), np.float32)

    def add(k, column, sign):
        for m in range(1, ORDER + 1):
            for lane in range(max(0, column - m), min(128, column + m + 1)):
                out[k, (m - 1) * 128 + lane] += sign * comb(2 * m, m + lane - column) / 16.0**m

    for lane in range(128):
        add(lane, lane, 1)
    for lane in range(4):
        add(128 + lane, 128 + lane, 1)
        add(128 + 124 + lane, lane - 4, 1)
    for k in range(3):
        add(128 + 8 + k, -2 - k, -1)
        add(128 + 5 + k, 131 - k, -1)
    return out


def seam(values):
    lane = lax.broadcasted_iota(jnp.int32, (1, 8, 128), 2)
    sub = lax.broadcasted_iota(jnp.int32, (1, 8, 128), 1)
    inner = ((lane < 4) & (sub < 7)) | ((lane >= 124) & (sub > 0))
    edge = ((sub == 0) & (lane >= 8) & (lane <= 10)) | ((sub == 7) & (lane >= 5) & (lane <= 7))
    beside = jnp.where(lane < 64, pltpu.roll(values, 7, 1), pltpu.roll(values, 1, 1))
    return jnp.where(inner, beside, jnp.where(edge, pltpu.roll(values, 8, 2), 0.0))


def y_powers(values, weights):
    rows = values.shape[0]

    def halves(x):
        x = x.reshape(rows * 8, 128)
        high = x.astype(BF16)
        return high, (x - high.astype(F32)).astype(BF16)

    high, low = halves(values)
    seam_high, seam_low = halves(seam(values))
    left = jnp.concatenate([high, seam_high, low, seam_low], axis=1)
    right = jnp.concatenate([weights, weights], axis=0)
    out = jnp.dot(left, right, preferred_element_type=F32)
    return [out[:, m * 128 : (m + 1) * 128].reshape(rows, 8, 128) for m in range(ORDER)]


def to_rows(flat, load_tile, row_tiles):
    for i in range(row_tiles):
        for j in range(8):
            flat[pl.ds((i * 8 + j) * 8, 8), :] = load_tile(i, j)


def row_of(flat, row):
    start = (row // 8) * 64 + row % 8
    return flat[pl.ds(start, 8, stride=8), :]


def planes_of(source, receiver):
    for field in (source, receiver):
        for part in range(2):
            for freq in range(source.shape[1]):
                yield lambda i, j: field[part, freq, pl.ds(8 * i, 8), pl.ds(128 * j, 128)]


def ahead_kernel(aperture, source, receiver, slowness, ahead, slowness_out, *flats):
    width = aperture[lax.axis_index("tile")]
    row_tiles = source.shape[2] // 8
    for plane, load in enumerate(planes_of(source, receiver)):
        to_rows(flats[plane], load, row_tiles)
        for k in range(HALO):
            ahead[plane * HALO + k] = row_of(flats[plane], width - HALO + k)
    slowness_out[...] = slowness[...]


def slow_tile(planes, depth):
    columns = planes.shape[3]
    return lambda i, j: planes[
        128 * j // columns, depth, pl.ds(8 * i, 8), pl.ds(128 * j % columns, 128)
    ]


def behind_kernel(aperture, source, receiver, planes, behind, slow_ahead, *flats):
    width = aperture[lax.axis_index("tile")]
    row_tiles = source.shape[2] // 8
    count = 4 * source.shape[1]
    for plane, load in enumerate(planes_of(source, receiver)):
        to_rows(flats[plane], load, HALO // 8)
        for k in range(HALO):
            behind[plane * HALO + k] = row_of(flats[plane], k)
    to_rows(flats[count], slow_tile(planes, 0), row_tiles)
    for k in range(ORDER):
        slow_ahead[k] = row_of(flats[count], width - ORDER + k)
        behind[count * HALO + k] = row_of(flats[count], k)


def coefficients(weights, freq, slow_row, store):
    powers = weights.shape[1] // (2 * (ORDER + 1))
    for part in range(2 * (ORDER + 1)):
        value = weights[freq, part * powers + powers - 1]
        for power in range(powers - 2, -1, -1):
            value = value * slow_row + weights[freq, part * powers + power]
        store(part, value)


def own_kernel(
    frequency, order_table, filter_coeffs, source, receiver, planes, y_matrix,
    rows_out, powers_out, slow_out, weights_out, later_out, flat, later_weights,
):
    freqs, stored = source.shape[1:3]
    row_tiles = stored // 8
    powers = filter_coeffs.shape[2]
    for plane, load in enumerate(planes_of(source, receiver)):
        to_rows(flat.at[plane % 2], load, row_tiles)
        for r in range(stored):
            rows_out[plane, r] = row_of(flat.at[plane % 2], r)
    for depth in range(NDEPTH):
        to_rows(flat.at[depth], slow_tile(planes, depth), row_tiles)
        for r in range(stored):
            slow_out[depth, r] = row_of(flat.at[depth], r)

    for depth, weights in enumerate((weights_out, later_weights)):
        for freq in range(freqs):
            omega = frequency[freq]
            active = [jnp.where(order_table[depth, freq] >= n, 1.0, 0.0) for n in range(ORDER + 1)]
            for c in range(2):
                scale = None
                for j in range(powers):
                    scaled = [filter_coeffs[c, n, j] * active[n] for n in range(ORDER + 1)]
                    for m in range(ORDER + 1):
                        total = None
                        for n in range(m, ORDER + 1):
                            term = scaled[n] * float(SHIFTED[n][m])
                            total = term if total is None else total + term
                        if scale is not None:
                            total = total * scale
                        weights[freq, (m * 2 + c) * powers + j] = jnp.full((8, 128), total, F32)
                    scale = omega if scale is None else scale * omega

    def later(r, carry):
        for freq in range(freqs):
            def store(part, value):
                later_out[freq, part, r] = value

            coefficients(later_weights, freq, slow_out[1, r], store)
        return carry

    lax.fori_loop(0, stored, later, 0)

    matrix = y_matrix[...]

    def spread(plane, carry):
        for m, value in enumerate(y_powers(rows_out[plane], matrix)):
            powers_out[plane, m] = value
        return carry

    lax.fori_loop(0, 4 * freqs, spread, 0)


def main_kernel(
    aperture, rows_in, powers_in, slow_in, weights, later, y_matrix,
    from_before, slow_before, from_after,
    image_out, receiver_out,
    flat, edges, start, middle, powers, slow, first, images,
):
    tile = lax.axis_index("tile")
    width = aperture[tile]
    count, stored = rows_in.shape[:2]
    freqs = count // 4
    row_tiles = stored // 8
    rows_one = stored + 2 * ORDER
    matrix = y_matrix[...]

    for p in range(count):
        start[p, pl.ds(HALO, stored)] = rows_in[p]
        for m in range(ORDER):
            powers[p, m, pl.ds(HALO, stored)] = powers_in[p, m]
    slow[pl.ds(ORDER, stored)] = slow_in[0]

    @pl.when(tile == 0)
    def _():
        for p in range(count):
            edges[p, HALO - 1] = jnp.zeros((8, 128), F32)
            for k in range(1, HALO):
                edges[p, HALO - 1 - k] = -rows_in[p, k - 1]
        slow[ORDER - 1] = slow_in[0, 0]
        for k in range(1, ORDER):
            slow[ORDER - 1 - k] = slow_in[0, k - 1]

    @pl.when(tile > 0)
    def _():
        for p in range(count):
            edges[p, pl.ds(0, HALO)] = from_before[pl.ds(p * HALO, HALO)]
        slow[pl.ds(0, ORDER)] = slow_before[...]

    @pl.when(tile == lax.axis_size("tile") - 1)
    def _():
        for p in range(count):
            edges[p, HALO] = jnp.zeros((8, 128), F32)
            for k in range(1, HALO):
                edges[p, HALO + k] = -rows_in[p, width - k]
        slow[ORDER + width] = slow_in[0, width - 1]
        for k in range(1, ORDER):
            slow[ORDER + width + k] = slow_in[0, width - k]

    @pl.when(tile < lax.axis_size("tile") - 1)
    def _():
        for p in range(count):
            edges[p, pl.ds(HALO, HALO)] = from_after[pl.ds(p * HALO, HALO)]
        slow[pl.ds(ORDER + width, ORDER)] = from_after[pl.ds(count * HALO, ORDER)]

    def spread_edges(p, carry):
        values = edges[p]
        start[p, pl.ds(0, HALO)] = values[:HALO]
        start[p, pl.ds(HALO + width, HALO)] = values[HALO:]
        for m, value in enumerate(y_powers(values, matrix)):
            powers[p, m, pl.ds(0, HALO)] = value[:HALO]
            powers[p, m, pl.ds(HALO + width, HALO)] = value[HALO:]
        return carry

    lax.fori_loop(0, count, spread_edges, 0)

    def first_row(r, carry):
        for freq in range(freqs):
            def store(part, value):
                first[freq, part, r] = value

            coefficients(weights, freq, slow[r], store)
        return carry

    lax.fori_loop(0, rows_one, first_row, 0)

    def sweep(depth, fields, results, coefs, rows):
        def feed(held, value):
            kept = []
            for last in held:
                kept.append(value)
                value = value + last
            return kept, value

        for freq in range(freqs):
            for field in range(2):
                pair = [(2 * field + part) * freqs + freq for part in range(2)]
                held = []
                for p in pair:
                    for m in range(1, ORDER + 1):
                        chain = []
                        for k in range(2 * m):
                            value = powers[p, m - 1, ORDER - m + k]
                            chain, value = feed(chain, value)
                            chain.append(value)
                        held.append(chain)

                def step(o, held, freq=freq, field=field, pair=pair):
                    totals, kept = [], []
                    for at, p in enumerate(pair):
                        sums = [fields[p, o + ORDER]]
                        for m in range(1, ORDER + 1):
                            chain, value = feed(
                                held[at * ORDER + m - 1], powers[p, m - 1, o + ORDER + m]
                            )
                            kept.append(chain)
                            sums.append(value)
                        totals.append(sums)
                    re = im = None
                    for m in range(ORDER + 1):
                        g_re, g_im = coefs[freq, 2 * m, o], coefs[freq, 2 * m + 1, o]
                        v_re, v_im = totals[0][m], totals[1][m]
                        if field == 0:
                            part_re, part_im = g_re * v_re + g_im * v_im, g_re * v_im - g_im * v_re
                        else:
                            part_re, part_im = g_re * v_re - g_im * v_im, g_re * v_im + g_im * v_re
                        re = part_re if re is None else re + part_re
                        im = part_im if im is None else im + part_im
                    results[pair[0], o] = re
                    results[pair[1], o] = im
                    if field == 1:
                        term = re * results[freq, o] + im * results[freqs + freq, o]
                        images[depth, o] = term if freq == 0 else images[depth, o] + term
                    return kept

                lax.fori_loop(0, rows, step, held, unroll=8)

    sweep(0, start, middle, first, rows_one)

    def spread_middle(p, carry):
        for m, value in enumerate(y_powers(middle[p], matrix)):
            powers[p, m, pl.ds(0, rows_one)] = value
        return carry

    lax.fori_loop(0, count, spread_middle, 0)
    sweep(1, middle, start, later, stored)

    def put(slot, load_row, store_tile):
        for r in range(stored):
            at = (r // 8) * 64 + r % 8
            flat[slot, pl.ds(at, 8, stride=8), :] = jnp.where(r < width, load_row(r), 0.0)
        for i in range(row_tiles):
            for j in range(8):
                store_tile(i, j, flat[slot, pl.ds((i * 8 + j) * 8, 8), :])

    columns = image_out.shape[3]
    for depth in range(NDEPTH):
        def store_image(i, j, value):
            image_out[
                128 * j // columns, depth, pl.ds(8 * i, 8), pl.ds(128 * j % columns, 128)
            ] = value

        put(depth, lambda r: images[depth, r + ORDER * (1 - depth)], store_image)
    for part in range(2):
        for freq in range(freqs):
            def store_receiver(i, j, value):
                receiver_out[part, freq, pl.ds(8 * i, 8), pl.ds(128 * j, 128)] = value

            p = (2 + part) * freqs + freq
            put(p % 2, lambda r: start[p, r], store_receiver)


def passed_along(value, axis, steps):
    count = lax.axis_size(axis)
    initial, last = (max(0, -steps), min(count, count - steps))
    return lax.ppermute(value, axis, [(source, source + steps) for source in range(initial, last)])


def kernel(body, out_shape, in_specs, scratch, name, cost):
    return pl.pallas_call(
        body,
        out_shape=out_shape,
        in_specs=in_specs,
        out_specs=jax.tree.map(lambda _: VMEM, out_shape),
        scratch_shapes=scratch,
        compiler_params=pltpu.CompilerParams(vmem_limit_bytes=28 << 20),
        cost_estimate=pl.CostEstimate(flops=cost, bytes_accessed=cost // 100, transcendentals=0),
        name=name,
    )


def shards(source_field, receiver_field, slowness, frequency, order_table, filter_coeffs, aperture):
    freqs, stored = source_field.shape[1:3]
    count = 4 * freqs
    parts = 2 * (ORDER + 1)
    rows_one, rows_all = stored + 2 * ORDER, stored + 2 * HALO

    def rows(*lead):
        return jax.ShapeDtypeStruct(lead + (8, 128), F32)

    def scratch(*lead):
        return pltpu.VMEM(lead + (8, 128), F32)

    flat = pltpu.VMEM((stored * 8, 128), F32)
    ahead, slowness = kernel(
        ahead_kernel,
        (rows(count * HALO), jax.ShapeDtypeStruct(slowness.shape, F32)),
        [SMEM] + [VMEM] * 3,
        [flat] * count,
        "ahead",
        1 << 20,
    )(aperture, source_field, receiver_field, slowness)
    from_before = passed_along(ahead, "tile", 1)
    planes = lax.all_gather(slowness, "freq", axis=0)
    behind, slow_ahead = kernel(
        behind_kernel,
        (rows(count * HALO + ORDER), rows(ORDER)),
        [SMEM] + [VMEM] * 3,
        [flat] * (count + 1),
        "behind",
        1 << 20,
    )(aperture, source_field, receiver_field, planes)
    from_after = passed_along(behind, "tile", -1)
    slow_before = passed_along(slow_ahead, "tile", 1)

    y_matrix = jnp.asarray(y_weights(), BF16)
    powers = filter_coeffs.shape[2]
    own = kernel(
        own_kernel,
        (
            rows(count, stored),
            rows(count, ORDER, stored),
            rows(NDEPTH, stored),
            rows(freqs, parts * powers),
            rows(freqs, parts, stored),
        ),
        [SMEM] * 3 + [VMEM] * 4,
        [pltpu.VMEM((2, stored * 8, 128), F32), scratch(freqs, parts * powers)],
        "own",
        1 << 30,
    )(frequency, order_table, filter_coeffs, source_field, receiver_field, planes, y_matrix)
    image_parts, receiver_out = kernel(
        main_kernel,
        (
            jax.ShapeDtypeStruct((lax.axis_size("freq"),) + slowness.shape, F32),
            jax.ShapeDtypeStruct(receiver_field.shape, F32),
        ),
        [SMEM] + [VMEM] * 9,
        [
            pltpu.VMEM((2, stored * 8, 128), F32),
            scratch(count, 2 * HALO),
            scratch(count, rows_all),
            scratch(count, rows_one),
            scratch(count, ORDER, rows_all),
            scratch(rows_one),
            scratch(freqs, parts, rows_one),
            scratch(NDEPTH, rows_one),
        ],
        "migrate",
        1 << 30,
    )(aperture, *own, y_matrix, from_before, slow_before, from_after)
    exchanged = lax.all_to_all(image_parts, "freq", 0, 0)
    return jnp.sum(exchanged, axis=0), receiver_out


def solution(mesh):
    placed = (
        P(None, "freq", "tile", None),
        P(None, "freq", "tile", None),
        P(None, "tile", "freq"),
        P("freq"),
        P(None, "freq"),
        P(),
        P(),
    )
    return jax.shard_map(
        shards,
        mesh=mesh,
        in_specs=placed,
        out_specs=(P(None, "tile", "freq"), P(None, "freq", "tile", None)),
        check_vma=False,
    )
```

```python
from math import comb

import jax
import jax.numpy as jnp
import numpy as np
from jax import lax
from jax.experimental import pallas as pl
from jax.experimental.pallas import tpu as pltpu
from jax.sharding import PartitionSpec as P

ORDER = 4
NDEPTH = 2
HALO = ORDER * NDEPTH
F32 = jnp.float32
BF16 = jnp.bfloat16
VMEM = pl.BlockSpec(memory_space=pltpu.VMEM)
HBM = pl.BlockSpec(memory_space=pltpu.HBM)

SHIFTED = ((1,), (-1, 2), (1, -8, 8), (-1, 18, -48, 32), (1, -32, 160, -256, 128))


def y_weights():
    out = np.zeros((256, ORDER * 128), np.float32)

    def add(k, column, sign):
        for m in range(1, ORDER + 1):
            for lane in range(max(0, column - m), min(128, column + m + 1)):
                out[k, (m - 1) * 128 + lane] += sign * comb(2 * m, m + lane - column) / 16.0**m

    for lane in range(128):
        add(lane, lane, 1)
    for lane in range(4):
        add(128 + lane, 128 + lane, 1)
        add(128 + 124 + lane, lane - 4, 1)
    for k in range(3):
        add(128 + 8 + k, -2 - k, -1)
        add(128 + 5 + k, 131 - k, -1)
    return out


def seam(values):
    lane = lax.broadcasted_iota(jnp.int32, (1, 8, 128), 2)
    sub = lax.broadcasted_iota(jnp.int32, (1, 8, 128), 1)
    inner = ((lane < 4) & (sub < 7)) | ((lane >= 124) & (sub > 0))
    edge = ((sub == 0) & (lane >= 8) & (lane <= 10)) | ((sub == 7) & (lane >= 5) & (lane <= 7))
    beside = jnp.where(lane < 64, pltpu.roll(values, 7, 1), pltpu.roll(values, 1, 1))
    return jnp.where(inner, beside, jnp.where(edge, pltpu.roll(values, 8, 2), 0.0))


def split_rows(values, left, at):
    rows = values.shape[0]
    for column, x in enumerate((values, seam(values))):
        x = x.reshape(rows * 8, 128)
        high = x.astype(BF16)
        left[pl.ds(at, rows * 8), pl.ds(128 * column, 128)] = high
        left[pl.ds(at, rows * 8), pl.ds(256 + 128 * column, 128)] = (x - high.astype(F32)).astype(BF16)


def multiply(left, rows, y_matrix):
    matrix = y_matrix[...]
    right = jnp.concatenate([matrix, matrix], axis=0)
    return jnp.dot(left[pl.ds(0, rows), :], right, preferred_element_type=F32)


def fetch(sems, *pairs):
    copies = [pltpu.make_async_copy(a, b, sems.at[k]) for k, (a, b) in enumerate(pairs)]
    for copy in copies:
        copy.start()
    for copy in copies:
        copy.wait()


def to_rows(flat, load_tile, row_tiles):
    for i in range(row_tiles):
        for j in range(8):
            flat[pl.ds((i * 8 + j) * 8, 8), :] = load_tile(i, j)


def row_of(flat, row):
    start = (row // 8) * 64 + row % 8
    return flat[pl.ds(start, 8, stride=8), :]


def planes_of(source, receiver):
    for field in (source, receiver):
        for part in range(2):
            for freq in range(source.shape[1]):
                yield lambda i, j: field[part, freq, pl.ds(8 * i, 8), pl.ds(128 * j, 128)]


def ahead_kernel(
    aperture_hbm, source_hbm, receiver_hbm, slowness_hbm, ahead, slowness_out,
    aperture, source, receiver, sems, *flats,
):
    fetch(
        sems,
        (aperture_hbm, aperture),
        (source_hbm, source),
        (receiver_hbm, receiver),
        (slowness_hbm, slowness_out),
    )
    width = aperture[lax.axis_index("tile")]
    row_tiles = source.shape[2] // 8
    for plane, load in enumerate(planes_of(source, receiver)):
        to_rows(flats[plane], load, row_tiles)
        for k in range(HALO):
            ahead[plane * HALO + k] = row_of(flats[plane], width - HALO + k)


def slow_tile(planes, depth):
    columns = planes.shape[3]
    return lambda i, j: planes[
        128 * j // columns, depth, pl.ds(8 * i, 8), pl.ds(128 * j % columns, 128)
    ]


def behind_kernel(
    aperture_hbm, source_hbm, receiver_hbm, planes, behind, slow_ahead,
    aperture, source, receiver, sems, *flats,
):
    top = pl.ds(0, HALO)
    fetch(
        sems,
        (aperture_hbm, aperture),
        (source_hbm.at[:, :, top, :], source),
        (receiver_hbm.at[:, :, top, :], receiver),
    )
    width = aperture[lax.axis_index("tile")]
    count = 4 * source.shape[1]
    for plane, load in enumerate(planes_of(source, receiver)):
        to_rows(flats[plane], load, HALO // 8)
        for k in range(HALO):
            behind[plane * HALO + k] = row_of(flats[plane], k)
    to_rows(flats[count], slow_tile(planes, 0), planes.shape[2] // 8)
    for k in range(ORDER):
        slow_ahead[k] = row_of(flats[count], width - ORDER + k)
        behind[count * HALO + k] = row_of(flats[count], k)


def coefficients(weights, freq, slow_row, store):
    powers = weights.shape[1] // (2 * (ORDER + 1))
    for part in range(2 * (ORDER + 1)):
        value = weights[freq, part * powers + powers - 1]
        for power in range(powers - 2, -1, -1):
            value = value * slow_row + weights[freq, part * powers + power]
        store(part, value)


def own_kernel(
    frequency_hbm, order_hbm, coeffs_hbm, source_hbm, receiver_hbm, planes, y_matrix_hbm,
    rows_out, powers_out, slow_out, weights_out, later_out,
    frequency, order_table, filter_coeffs, source, receiver, y_matrix, sems,
    flat, left, later_weights,
):
    fetch(
        sems,
        (frequency_hbm, frequency),
        (order_hbm, order_table),
        (coeffs_hbm, filter_coeffs),
        (source_hbm, source),
        (receiver_hbm, receiver),
        (y_matrix_hbm, y_matrix),
    )
    freqs, stored = source.shape[1:3]
    row_tiles = stored // 8
    powers = filter_coeffs.shape[0]
    for plane, load in enumerate(planes_of(source, receiver)):
        to_rows(flat.at[plane], load, row_tiles)
        for r in range(stored):
            rows_out[plane, r] = row_of(flat.at[plane], r)
    for plane in range(4 * freqs):
        split_rows(rows_out[plane], left, plane * stored * 8)
    powers_out[...] = multiply(left, 4 * freqs * stored * 8, y_matrix)

    for depth in range(NDEPTH):
        to_rows(flat.at[depth], slow_tile(planes, depth), row_tiles)
        for r in range(stored):
            slow_out[depth, r] = row_of(flat.at[depth], r)

    for depth, weights in enumerate((weights_out, later_weights)):
        for freq in range(freqs):
            omega = jnp.full((8, 128), frequency[freq], F32)
            active = [
                jnp.full((8, 128), jnp.where(order_table[depth, freq] >= n, 1.0, 0.0), F32)
                for n in range(ORDER + 1)
            ]
            for c in range(2):
                scale = None
                for j in range(powers):
                    scaled = [filter_coeffs[j, c, n] * active[n] for n in range(ORDER + 1)]
                    for m in range(ORDER + 1):
                        total = None
                        for n in range(m, ORDER + 1):
                            term = scaled[n] * float(SHIFTED[n][m])
                            total = term if total is None else total + term
                        if scale is not None:
                            total = total * scale
                        weights[freq, (m * 2 + c) * powers + j] = total
                    scale = omega if scale is None else scale * omega

    def later(r, carry):
        for freq in range(freqs):
            def store(part, value):
                later_out[freq, part, r] = value

            coefficients(later_weights, freq, slow_out[1, r], store)
        return carry

    lax.fori_loop(0, stored, later, 0, unroll=4)


def main_kernel(
    aperture_hbm, rows_in, powers_in, slow_in, weights, later, y_matrix_hbm,
    from_before, slow_before, from_after,
    image_out, receiver_out,
    aperture, y_matrix, sems,
    flat, edges, start, middle, left, powers, slow, first, images, partial,
):
    fetch(sems, (aperture_hbm, aperture), (y_matrix_hbm, y_matrix))
    tile = lax.axis_index("tile")
    width = aperture[tile]
    count, stored = rows_in.shape[:2]
    freqs = count // 4
    row_tiles = stored // 8
    rows_one = stored + 2 * ORDER

    for p in range(count):
        start[p, pl.ds(HALO, stored)] = rows_in[p]
        powers[p, pl.ds(8 * HALO, 8 * stored), :] = powers_in[pl.ds(p * stored * 8, stored * 8), :]
    slow[pl.ds(ORDER, stored)] = slow_in[0]

    @pl.when(tile == 0)
    def _():
        for p in range(count):
            edges[p, HALO - 1] = jnp.zeros((8, 128), F32)
            for k in range(1, HALO):
                edges[p, HALO - 1 - k] = -rows_in[p, k - 1]
        slow[ORDER - 1] = slow_in[0, 0]
        for k in range(1, ORDER):
            slow[ORDER - 1 - k] = slow_in[0, k - 1]

    @pl.when(tile > 0)
    def _():
        for p in range(count):
            edges[p, pl.ds(0, HALO)] = from_before[pl.ds(p * HALO, HALO)]
        slow[pl.ds(0, ORDER)] = slow_before[...]

    @pl.when(tile == lax.axis_size("tile") - 1)
    def _():
        for p in range(count):
            edges[p, HALO] = jnp.zeros((8, 128), F32)
            for k in range(1, HALO):
                edges[p, HALO + k] = -rows_in[p, width - k]
        slow[ORDER + width] = slow_in[0, width - 1]
        for k in range(1, ORDER):
            slow[ORDER + width + k] = slow_in[0, width - k]

    @pl.when(tile < lax.axis_size("tile") - 1)
    def _():
        for p in range(count):
            edges[p, pl.ds(HALO, HALO)] = from_after[pl.ds(p * HALO, HALO)]
        slow[pl.ds(ORDER + width, ORDER)] = from_after[pl.ds(count * HALO, ORDER)]

    for p in range(count):
        values = edges[p]
        start[p, pl.ds(0, HALO)] = values[:HALO]
        start[p, pl.ds(HALO + width, HALO)] = values[HALO:]
        split_rows(values, left, p * 2 * HALO * 8)
    product = multiply(left, count * 2 * HALO * 8, y_matrix)
    after = pl.multiple_of(8 * (HALO + width), 8)
    for p in range(count):
        at = p * 2 * HALO * 8
        powers[p, pl.ds(0, 8 * HALO), :] = product[at : at + 8 * HALO]
        powers[p, pl.ds(after, 8 * HALO), :] = product[at + 8 * HALO : at + 16 * HALO]

    def first_row(r, carry):
        for freq in range(freqs):
            def store(part, value):
                first[freq, part, r] = value

            coefficients(weights, freq, slow[r], store)
        return carry

    lax.fori_loop(0, rows_one, first_row, 0, unroll=4)

    def sweep(depth, fields, results, coefs, rows):
        def feed(held, value):
            kept = []
            for last in held:
                kept.append(value)
                value = value + last
            return kept, value

        def power(p, m, row):
            return powers[p, pl.ds(pl.multiple_of(8 * row, 8), 8), pl.ds(128 * (m - 1), 128)]

        for freq in range(freqs):
            for field in range(2):
                for part in range(2):
                    p = (2 * field + part) * freqs + freq
                    held = []
                    for m in range(1, ORDER + 1):
                        chain = []
                        for k in range(2 * m):
                            value = power(p, m, ORDER - m + k)
                            chain, value = feed(chain, value)
                            chain.append(value)
                        held.append(chain)

                    def step(o, held, freq=freq, field=field, part=part, p=p):
                        kept, by_re, by_im = [], None, None
                        for m in range(ORDER + 1):
                            if m == 0:
                                value = fields[p, o + ORDER]
                            else:
                                chain, value = feed(held[m - 1], power(p, m, o + ORDER + m))
                                kept.append(chain)
                            re = coefs[freq, 2 * m, o] * value
                            im = coefs[freq, 2 * m + 1, o] * value
                            by_re = re if by_re is None else by_re + re
                            by_im = im if by_im is None else by_im + im
                        if part == 0:
                            partial[0, o] = by_re
                            partial[1, o] = by_im
                            return kept
                        if field == 0:
                            re, im = partial[0, o] + by_im, by_re - partial[1, o]
                        else:
                            re, im = partial[0, o] - by_im, by_re + partial[1, o]
                            term = re * results[freq, o] + im * results[freqs + freq, o]
                            images[depth, o] = term if freq == 0 else images[depth, o] + term
                        results[p - freqs, o] = re
                        results[p, o] = im
                        return kept

                    lax.fori_loop(0, rows, step, held, unroll=8)

    sweep(0, start, middle, first, rows_one)

    for p in range(count):
        split_rows(middle[p], left, p * rows_one * 8)
    product = multiply(left, count * rows_one * 8, y_matrix)
    for p in range(count):
        at = p * rows_one * 8
        powers[p, pl.ds(0, 8 * rows_one), :] = product[at : at + 8 * rows_one]
    sweep(1, middle, start, later, stored)

    def put(slot, load_row, store_tile):
        for r in range(stored):
            at = (r // 8) * 64 + r % 8
            flat[slot, pl.ds(at, 8, stride=8), :] = jnp.where(r < width, load_row(r), 0.0)
        for i in range(row_tiles):
            for j in range(8):
                store_tile(i, j, flat[slot, pl.ds((i * 8 + j) * 8, 8), :])

    columns = image_out.shape[3]
    for depth in range(NDEPTH):
        def store_image(i, j, value):
            image_out[
                128 * j // columns, depth, pl.ds(8 * i, 8), pl.ds(128 * j % columns, 128)
            ] = value

        put(depth, lambda r: images[depth, r + ORDER * (1 - depth)], store_image)
    for part in range(2):
        for freq in range(freqs):
            def store_receiver(i, j, value):
                receiver_out[part, freq, pl.ds(8 * i, 8), pl.ds(128 * j, 128)] = value

            p = (2 + part) * freqs + freq
            put(p % 2, lambda r: start[p, r], store_receiver)


def passed_along(value, axis, steps):
    count = lax.axis_size(axis)
    initial, last = (max(0, -steps), min(count, count - steps))
    return lax.ppermute(value, axis, [(source, source + steps) for source in range(initial, last)])


def kernel(body, out_shape, in_specs, scratch, name):
    return pl.pallas_call(
        body,
        out_shape=out_shape,
        in_specs=in_specs,
        out_specs=jax.tree.map(lambda _: VMEM, out_shape),
        scratch_shapes=scratch,
        compiler_params=pltpu.CompilerParams(vmem_limit_bytes=32 << 20),
        cost_estimate=pl.CostEstimate(flops=1000, bytes_accessed=1000, transcendentals=0),
        name=name,
    )


def shards(source_field, receiver_field, slowness, frequency, order_table, filter_coeffs, aperture):
    freqs, stored = source_field.shape[1:3]
    count = 4 * freqs
    parts = 2 * (ORDER + 1)
    rows_one, rows_all = stored + 2 * ORDER, stored + 2 * HALO

    def rows(*lead):
        return jax.ShapeDtypeStruct(lead + (8, 128), F32)

    def scratch(*lead):
        return pltpu.VMEM(lead + (8, 128), F32)

    def same(value):
        return pltpu.VMEM(value.shape, value.dtype)

    def scalars(value):
        return pltpu.SMEM(value.shape, value.dtype)

    flat = pltpu.VMEM((stored * 8, 128), F32)
    ahead, slowness = kernel(
        ahead_kernel,
        (rows(count * HALO), jax.ShapeDtypeStruct(slowness.shape, F32)),
        [HBM] * 4,
        [scalars(aperture), same(source_field), same(receiver_field), pltpu.SemaphoreType.DMA((4,))]
        + [flat] * count,
        "ahead",
    )(aperture, source_field, receiver_field, slowness)
    from_before = passed_along(ahead, "tile", 1)
    planes = lax.all_gather(slowness, "freq", axis=0)
    top = pltpu.VMEM(source_field.shape[:2] + (HALO,) + source_field.shape[3:], F32)
    behind, slow_ahead = kernel(
        behind_kernel,
        (rows(count * HALO + ORDER), rows(ORDER)),
        [HBM] * 3 + [VMEM],
        [scalars(aperture), top, top, pltpu.SemaphoreType.DMA((3,))] + [flat] * (count + 1),
        "behind",
    )(aperture, source_field, receiver_field, planes)
    from_after = passed_along(behind, "tile", -1)
    slow_before = passed_along(slow_ahead, "tile", 1)

    y_matrix = jnp.asarray(y_weights(), BF16)
    coeffs = jnp.transpose(filter_coeffs, (2, 0, 1))
    powers = coeffs.shape[0]
    own = kernel(
        own_kernel,
        (
            rows(count, stored),
            jax.ShapeDtypeStruct((count * stored * 8, ORDER * 128), F32),
            rows(NDEPTH, stored),
            rows(freqs, parts * powers),
            rows(freqs, parts, stored),
        ),
        [HBM] * 5 + [VMEM, HBM],
        [
            scalars(frequency),
            scalars(order_table),
            scalars(coeffs),
            same(source_field),
            same(receiver_field),
            same(y_matrix),
            pltpu.SemaphoreType.DMA((6,)),
            pltpu.VMEM((count, stored * 8, 128), F32),
            pltpu.VMEM((count * stored * 8, 512), BF16),
            scratch(freqs, parts * powers),
        ],
        "own",
    )(frequency, order_table, coeffs, source_field, receiver_field, planes, y_matrix)
    image_parts, receiver_out = kernel(
        main_kernel,
        (
            jax.ShapeDtypeStruct((lax.axis_size("freq"),) + slowness.shape, F32),
            jax.ShapeDtypeStruct(receiver_field.shape, F32),
        ),
        [HBM] + [VMEM] * 5 + [HBM] + [VMEM] * 3,
        [
            scalars(aperture),
            same(y_matrix),
            pltpu.SemaphoreType.DMA((2,)),
            pltpu.VMEM((2, stored * 8, 128), F32),
            scratch(count, 2 * HALO),
            scratch(count, rows_all),
            scratch(count, rows_one),
            pltpu.VMEM((count * rows_one * 8, 512), BF16),
            pltpu.VMEM((count, rows_all * 8, ORDER * 128), F32),
            scratch(rows_one),
            scratch(freqs, parts, rows_one),
            scratch(NDEPTH, rows_one),
            scratch(2, rows_one),
        ],
        "migrate",
    )(aperture, *own, y_matrix, from_before, slow_before, from_after)
    exchanged = lax.all_to_all(image_parts, "freq", 0, 0)
    return jnp.sum(exchanged, axis=0), receiver_out


def solution(mesh):
    placed = (
        P(None, "freq", "tile", None),
        P(None, "freq", "tile", None),
        P(None, "tile", "freq"),
        P("freq"),
        P(None, "freq"),
        P(),
        P(),
    )
    return jax.shard_map(
        shards,
        mesh=mesh,
        in_specs=placed,
        out_specs=(P(None, "tile", "freq"), P(None, "freq", "tile", None)),
        check_vma=False,
    )
```

```python
from math import comb

import jax
import jax.numpy as jnp
import numpy as np
from jax import lax
from jax.experimental import pallas as pl
from jax.experimental.pallas import tpu as pltpu
from jax.sharding import PartitionSpec as P

ORDER = 4
NDEPTH = 2
HALO = ORDER * NDEPTH
EXTRA = 8
F32 = jnp.float32
BF16 = jnp.bfloat16
VMEM = pl.BlockSpec(memory_space=pltpu.VMEM)
HBM = pl.BlockSpec(memory_space=pltpu.HBM)

SHIFTED = ((1,), (-1, 2), (1, -8, 8), (-1, 18, -48, 32), (1, -32, 160, -256, 128))


def y_weights():
    out = np.zeros((256, ORDER * 128), np.float32)

    def add(k, column, sign):
        for m in range(1, ORDER + 1):
            for lane in range(max(0, column - m), min(128, column + m + 1)):
                out[k, (m - 1) * 128 + lane] += sign * comb(2 * m, m + lane - column) / 16.0**m

    for lane in range(128):
        add(lane, lane, 1)
    for lane in range(4):
        add(128 + lane, 128 + lane, 1)
        add(128 + 124 + lane, lane - 4, 1)
    for k in range(3):
        add(128 + 8 + k, -2 - k, -1)
        add(128 + 5 + k, 131 - k, -1)
    return out


def seam(values):
    lane = lax.broadcasted_iota(jnp.int32, (1, 8, 128), 2)
    sub = lax.broadcasted_iota(jnp.int32, (1, 8, 128), 1)
    inner = ((lane < 4) & (sub < 7)) | ((lane >= 124) & (sub > 0))
    edge = ((sub == 0) & (lane >= 8) & (lane <= 10)) | ((sub == 7) & (lane >= 5) & (lane <= 7))
    beside = jnp.where(lane < 64, pltpu.roll(values, 7, 1), pltpu.roll(values, 1, 1))
    return jnp.where(inner, beside, jnp.where(edge, pltpu.roll(values, 8, 2), 0.0))


def split_rows(values, left, at):
    rows = values.shape[0]
    for column, x in enumerate((values, seam(values))):
        x = x.reshape(rows * 8, 128)
        high = x.astype(BF16)
        left[pl.ds(at, rows * 8), pl.ds(128 * column, 128)] = high
        left[pl.ds(at, rows * 8), pl.ds(256 + 128 * column, 128)] = (x - high.astype(F32)).astype(BF16)


def multiply(left, rows, y_matrix):
    matrix = y_matrix[...]
    right = jnp.concatenate([matrix, matrix], axis=0)
    return jnp.dot(left[pl.ds(0, rows), :], right, preferred_element_type=F32)


def begin(sems, *pairs):
    copies = [pltpu.make_async_copy(a, b, sems.at[k]) for k, (a, b) in enumerate(pairs)]
    for copy in copies:
        copy.start()
    return copies


def finish(copies):
    for copy in copies:
        copy.wait()


def fetch(sems, *pairs):
    finish(begin(sems, *pairs))


def to_rows(flat, load_tile, row_tiles):
    for i in range(row_tiles):
        for j in range(8):
            flat[pl.ds((i * 8 + j) * 8, 8), :] = load_tile(i, j)


def row_of(flat, row):
    start = (row // 8) * 64 + row % 8
    return flat[pl.ds(start, 8, stride=8), :]


def planes_of(source, receiver):
    for field in (source, receiver):
        for part in range(2):
            for freq in range(source.shape[1]):
                yield lambda i, j: field[part, freq, pl.ds(8 * i, 8), pl.ds(128 * j, 128)]


def ahead_kernel(
    aperture_hbm, source_hbm, receiver_hbm, ahead, aperture, source, receiver, sems, *flats
):
    fetch(
        sems,
        (aperture_hbm, aperture),
        (source_hbm, source),
        (receiver_hbm, receiver),
    )
    width = aperture[lax.axis_index("tile")]
    row_tiles = source.shape[2] // 8
    for plane, load in enumerate(planes_of(source, receiver)):
        to_rows(flats[plane], load, row_tiles)
        for k in range(HALO):
            ahead[plane * HALO + k] = row_of(flats[plane], width - HALO + k)
    used = 4 * source.shape[1] * HALO
    ahead[pl.ds(used, EXTRA)] = jnp.zeros((EXTRA, 8, 128), F32)


def slow_tile(planes, depth):
    columns = planes.shape[3]
    return lambda i, j: planes[
        128 * j // columns, depth, pl.ds(8 * i, 8), pl.ds(128 * j % columns, 128)
    ]


def behind_kernel(
    aperture_hbm, source_hbm, receiver_hbm, planes_hbm, behind, slow_ahead,
    aperture, source, receiver, planes, sems, *flats,
):
    top = pl.ds(0, HALO)
    fetch(
        sems,
        (aperture_hbm, aperture),
        (source_hbm.at[:, :, top, :], source),
        (receiver_hbm.at[:, :, top, :], receiver),
        (planes_hbm.at[:, pl.ds(0, 1)], planes),
    )
    width = aperture[lax.axis_index("tile")]
    count = 4 * source.shape[1]
    for plane, load in enumerate(planes_of(source, receiver)):
        to_rows(flats[plane], load, HALO // 8)
        for k in range(HALO):
            behind[plane * HALO + k] = row_of(flats[plane], k)
    to_rows(flats[count], slow_tile(planes, 0), planes.shape[2] // 8)
    for k in range(ORDER):
        slow_ahead[k] = row_of(flats[count], width - ORDER + k)
        behind[count * HALO + k] = row_of(flats[count], k)


def coefficients(weights, freq, slow_row, store):
    powers = weights.shape[1] // (2 * (ORDER + 1))
    for part in range(2 * (ORDER + 1)):
        value = weights[freq, part * powers + powers - 1]
        for power in range(powers - 2, -1, -1):
            value = value * slow_row + weights[freq, part * powers + power]
        store(part, value)


def own_kernel(
    frequency_hbm, order_hbm, coeffs_hbm, source_hbm, receiver_hbm, planes_hbm, y_matrix_hbm,
    rows_hbm, powers_hbm, slow_hbm, weights_hbm, later_hbm,
    frequency, order_table, filter_coeffs, source, receiver, planes, y_matrix,
    rows_out, powers_out, slow_out, weights_out, later_out, sems, sent,
    flat, left, later_weights,
):
    fetch(
        sems,
        (frequency_hbm, frequency),
        (order_hbm, order_table),
        (coeffs_hbm, filter_coeffs),
        (source_hbm, source),
        (receiver_hbm, receiver),
        (planes_hbm, planes),
        (y_matrix_hbm, y_matrix),
    )
    freqs, stored = source.shape[1:3]
    row_tiles = stored // 8
    powers = filter_coeffs.shape[0]
    for plane, load in enumerate(planes_of(source, receiver)):
        to_rows(flat.at[plane], load, row_tiles)
        for r in range(stored):
            rows_out[plane, r] = row_of(flat.at[plane], r)
    copies = begin(sent.at[pl.ds(0, 1)], (rows_out, rows_hbm))
    for plane in range(4 * freqs):
        split_rows(rows_out[plane], left, plane * stored * 8)
    product = multiply(left, 4 * freqs * stored * 8, y_matrix)
    powers_out[...] = product.reshape(powers_out.shape)
    copies += begin(sent.at[pl.ds(1, 1)], (powers_out, powers_hbm))

    for depth in range(NDEPTH):
        to_rows(flat.at[depth], slow_tile(planes, depth), row_tiles)
        for r in range(stored):
            slow_out[depth, r] = row_of(flat.at[depth], r)

    for depth, weights in enumerate((weights_out, later_weights)):
        for freq in range(freqs):
            omega = jnp.full((8, 128), frequency[freq], F32)
            active = [
                jnp.full((8, 128), jnp.where(order_table[depth, freq] >= n, 1.0, 0.0), F32)
                for n in range(ORDER + 1)
            ]
            for c in range(2):
                scale = None
                for j in range(powers):
                    scaled = [filter_coeffs[j, c, n] * active[n] for n in range(ORDER + 1)]
                    for m in range(ORDER + 1):
                        total = None
                        for n in range(m, ORDER + 1):
                            term = scaled[n] * float(SHIFTED[n][m])
                            total = term if total is None else total + term
                        if scale is not None:
                            total = total * scale
                        weights[freq, (m * 2 + c) * powers + j] = total
                    scale = omega if scale is None else scale * omega

    def later(r, carry):
        for freq in range(freqs):
            def store(part, value):
                later_out[freq, part, r] = value

            coefficients(later_weights, freq, slow_out[1, r], store)
        return carry

    lax.fori_loop(0, stored, later, 0, unroll=4)
    copies += begin(
        sent.at[pl.ds(2, 3)],
        (slow_out, slow_hbm),
        (weights_out, weights_hbm),
        (later_out, later_hbm),
    )
    finish(copies)


def main_kernel(
    aperture_hbm, rows_hbm, powers_hbm, slow_hbm, weights_hbm, later_hbm, y_matrix_hbm,
    before_hbm, slow_before_hbm, after_hbm,
    image_out, receiver_out,
    aperture, weights, later, y_matrix, from_before, from_after, sems,
    flat, edges, start, middle, left, powers, slow, slow_before, first, images, partial,
):
    count, stored = rows_hbm.shape[:2]
    freqs = count // 4
    row_tiles = stored // 8
    rows_one = stored + 2 * ORDER

    copies = begin(
        sems,
        (aperture_hbm, aperture),
        (before_hbm.at[pl.ds(0, count * HALO)], from_before),
        (after_hbm, from_after),
        (slow_before_hbm, slow_before),
        (rows_hbm, start.at[:, pl.ds(HALO, stored)]),
        (slow_hbm.at[0], slow.at[pl.ds(ORDER, stored)]),
        (y_matrix_hbm, y_matrix),
        (weights_hbm, weights),
        (powers_hbm, powers.at[:, pl.ds(8 * HALO, 8 * stored), :]),
        (later_hbm, later),
    )
    finish(copies[:8])
    tile = lax.axis_index("tile")
    width = aperture[tile]

    @pl.when(tile == 0)
    def _():
        for p in range(count):
            edges[p, HALO - 1] = jnp.zeros((8, 128), F32)
            for k in range(1, HALO):
                edges[p, HALO - 1 - k] = -start[p, HALO + k - 1]
        slow[ORDER - 1] = slow[ORDER]
        for k in range(1, ORDER):
            slow[ORDER - 1 - k] = slow[ORDER + k - 1]

    @pl.when(tile > 0)
    def _():
        for p in range(count):
            edges[p, pl.ds(0, HALO)] = from_before[pl.ds(p * HALO, HALO)]
        slow[pl.ds(0, ORDER)] = slow_before[...]

    @pl.when(tile == lax.axis_size("tile") - 1)
    def _():
        for p in range(count):
            edges[p, HALO] = jnp.zeros((8, 128), F32)
            for k in range(1, HALO):
                edges[p, HALO + k] = -start[p, HALO + width - k]
        slow[ORDER + width] = slow[ORDER + width - 1]
        for k in range(1, ORDER):
            slow[ORDER + width + k] = slow[ORDER + width - k]

    @pl.when(tile < lax.axis_size("tile") - 1)
    def _():
        for p in range(count):
            edges[p, pl.ds(HALO, HALO)] = from_after[pl.ds(p * HALO, HALO)]
        slow[pl.ds(ORDER + width, ORDER)] = from_after[pl.ds(count * HALO, ORDER)]

    for p in range(count):
        values = edges[p]
        start[p, pl.ds(0, HALO)] = values[:HALO]
        start[p, pl.ds(HALO + width, HALO)] = values[HALO:]
        split_rows(values, left, p * 2 * HALO * 8)
    product = multiply(left, count * 2 * HALO * 8, y_matrix)
    finish(copies[8:])
    after = pl.multiple_of(8 * (HALO + width), 8)
    for p in range(count):
        at = p * 2 * HALO * 8
        powers[p, pl.ds(0, 8 * HALO), :] = product[at : at + 8 * HALO]
        powers[p, pl.ds(after, 8 * HALO), :] = product[at + 8 * HALO : at + 16 * HALO]

    def first_row(r, carry):
        for freq in range(freqs):
            def store(part, value):
                first[freq, part, r] = value

            coefficients(weights, freq, slow[r], store)
        return carry

    lax.fori_loop(0, rows_one, first_row, 0, unroll=4)

    def sweep(depth, fields, results, coefs, rows):
        def feed(held, value):
            kept = []
            for last in held:
                kept.append(value)
                value = value + last
            return kept, value

        def power(p, m, row):
            return powers[p, pl.ds(pl.multiple_of(8 * row, 8), 8), pl.ds(128 * (m - 1), 128)]

        for freq in range(freqs):
            for field in range(2):
                for part in range(2):
                    p = (2 * field + part) * freqs + freq
                    held = []
                    for m in range(1, ORDER + 1):
                        chain = []
                        for k in range(2 * m):
                            value = power(p, m, ORDER - m + k)
                            chain, value = feed(chain, value)
                            chain.append(value)
                        held.append(chain)

                    def step(o, held, freq=freq, field=field, part=part, p=p):
                        kept, by_re, by_im = [], None, None
                        for m in range(ORDER + 1):
                            if m == 0:
                                value = fields[p, o + ORDER]
                            else:
                                chain, value = feed(held[m - 1], power(p, m, o + ORDER + m))
                                kept.append(chain)
                            re = coefs[freq, 2 * m, o] * value
                            im = coefs[freq, 2 * m + 1, o] * value
                            by_re = re if by_re is None else by_re + re
                            by_im = im if by_im is None else by_im + im
                        if part == 0:
                            partial[0, o] = by_re
                            partial[1, o] = by_im
                            return kept
                        if field == 0:
                            re, im = partial[0, o] + by_im, by_re - partial[1, o]
                        else:
                            re, im = partial[0, o] - by_im, by_re + partial[1, o]
                            term = re * results[freq, o] + im * results[freqs + freq, o]
                            images[depth, o] = term if freq == 0 else images[depth, o] + term
                        results[p - freqs, o] = re
                        results[p, o] = im
                        return kept

                    lax.fori_loop(0, rows, step, held, unroll=8)

    sweep(0, start, middle, first, rows_one)

    for p in range(count):
        split_rows(middle[p], left, p * rows_one * 8)
    product = multiply(left, count * rows_one * 8, y_matrix)
    for p in range(count):
        at = p * rows_one * 8
        powers[p, pl.ds(0, 8 * rows_one), :] = product[at : at + 8 * rows_one]
    sweep(1, middle, start, later, stored)

    def put(slot, load_row, store_tile):
        for r in range(stored):
            at = (r // 8) * 64 + r % 8
            flat[slot, pl.ds(at, 8, stride=8), :] = jnp.where(r < width, load_row(r), 0.0)
        for i in range(row_tiles):
            for j in range(8):
                store_tile(i, j, flat[slot, pl.ds((i * 8 + j) * 8, 8), :])

    columns = image_out.shape[3]
    for depth in range(NDEPTH):
        def store_image(i, j, value):
            image_out[
                128 * j // columns, depth, pl.ds(8 * i, 8), pl.ds(128 * j % columns, 128)
            ] = value

        put(depth, lambda r: images[depth, r + ORDER * (1 - depth)], store_image)
    for part in range(2):
        for freq in range(freqs):
            def store_receiver(i, j, value):
                receiver_out[part, freq, pl.ds(8 * i, 8), pl.ds(128 * j, 128)] = value

            p = (2 + part) * freqs + freq
            put(p % 2, lambda r: start[p, r], store_receiver)


def passed_along(value, axis, steps):
    count = lax.axis_size(axis)
    initial, last = (max(0, -steps), min(count, count - steps))
    return lax.ppermute(value, axis, [(source, source + steps) for source in range(initial, last)])


def kernel(body, out_shape, out_specs, operands, scratch, name):
    return pl.pallas_call(
        body,
        out_shape=out_shape,
        in_specs=[HBM] * len(operands),
        out_specs=out_specs,
        scratch_shapes=scratch,
        compiler_params=pltpu.CompilerParams(vmem_limit_bytes=60 << 20),
        cost_estimate=pl.CostEstimate(flops=1000, bytes_accessed=1000, transcendentals=0),
        name=name,
    )(*operands)


def shards(source_field, receiver_field, slowness, frequency, order_table, filter_coeffs, aperture):
    freqs, stored = source_field.shape[1:3]
    count = 4 * freqs
    parts = 2 * (ORDER + 1)
    rows_one, rows_all = stored + 2 * ORDER, stored + 2 * HALO

    def shape(*dims):
        return jax.ShapeDtypeStruct(dims, F32)

    def rows(*lead):
        return shape(*lead, 8, 128)

    def same(value):
        return pltpu.VMEM(value.shape, value.dtype)

    def scratch(*lead):
        return same(rows(*lead))

    def scalars(value):
        return pltpu.SMEM(value.shape, value.dtype)

    def copies(number):
        return pltpu.SemaphoreType.DMA((number,))

    flat = pltpu.VMEM((stored * 8, 128), F32)
    ahead = kernel(
        ahead_kernel,
        rows(count * HALO + EXTRA),
        VMEM,
        (aperture, source_field, receiver_field),
        [scalars(aperture), same(source_field), same(receiver_field), copies(3)] + [flat] * count,
        "ahead",
    )
    from_before = passed_along(ahead, "tile", 1)
    planes = lax.all_gather(slowness, "freq", axis=0)
    top = pltpu.VMEM(source_field.shape[:2] + (HALO,) + source_field.shape[3:], F32)
    behind, slow_ahead = kernel(
        behind_kernel,
        (rows(count * HALO + ORDER), rows(ORDER)),
        (VMEM, VMEM),
        (aperture, source_field, receiver_field, planes),
        [scalars(aperture), top, top, pltpu.VMEM((planes.shape[0], 1) + planes.shape[2:], F32)]
        + [copies(4)]
        + [flat] * (count + 1),
        "behind",
    )
    from_after = passed_along(behind, "tile", -1)
    slow_before = passed_along(slow_ahead, "tile", 1)

    y_matrix = jnp.asarray(y_weights(), BF16)
    coeffs = jnp.transpose(filter_coeffs, (2, 0, 1))
    weights = parts * coeffs.shape[0]
    results = (
        rows(count, stored),
        shape(count, stored * 8, ORDER * 128),
        rows(NDEPTH, stored),
        rows(freqs, weights),
        rows(freqs, parts, stored),
    )
    tables = (frequency, order_table, coeffs)
    arrays = (source_field, receiver_field, planes, y_matrix)
    own = kernel(
        own_kernel,
        results,
        (HBM,) * len(results),
        tables + arrays,
        [scalars(value) for value in tables]
        + [same(value) for value in arrays + results]
        + [copies(len(tables + arrays)), copies(len(results))]
        + [
            pltpu.VMEM((count, stored * 8, 128), F32),
            pltpu.VMEM((count * stored * 8, 512), BF16),
            scratch(freqs, weights),
        ],
        "own",
    )
    image_parts, receiver_out = kernel(
        main_kernel,
        (shape(lax.axis_size("freq"), *slowness.shape), shape(*receiver_field.shape)),
        (VMEM, VMEM),
        (aperture, *own, y_matrix, from_before, slow_before, from_after),
        [
            scalars(aperture),
            scratch(freqs, weights),
            scratch(freqs, parts, stored),
            same(y_matrix),
            scratch(count * HALO),
            same(from_after),
            copies(10),
            pltpu.VMEM((2, stored * 8, 128), F32),
            scratch(count, 2 * HALO),
            scratch(count, rows_all),
            scratch(count, rows_one),
            pltpu.VMEM((count * rows_one * 8, 512), BF16),
            pltpu.VMEM((count, rows_all * 8, ORDER * 128), F32),
            scratch(rows_one),
            scratch(ORDER),
            scratch(freqs, parts, rows_one),
            scratch(NDEPTH, rows_one),
            scratch(2, rows_one),
        ],
        "migrate",
    )
    exchanged = lax.all_to_all(image_parts, "freq", 0, 0)
    return jnp.sum(exchanged, axis=0), receiver_out


def solution(mesh):
    placed = (
        P(None, "freq", "tile", None),
        P(None, "freq", "tile", None),
        P(None, "tile", "freq"),
        P("freq"),
        P(None, "freq"),
        P(),
        P(),
    )
    return jax.shard_map(
        shards,
        mesh=mesh,
        in_specs=placed,
        out_specs=(P(None, "tile", "freq"), P(None, "freq", "tile", None)),
        check_vma=False,
    )
```

```python
from math import comb

import jax
import jax.numpy as jnp
import numpy as np
from jax import lax
from jax.experimental import pallas as pl
from jax.experimental.pallas import tpu as pltpu
from jax.sharding import PartitionSpec as P

ORDER = 4
NDEPTH = 2
HALO = ORDER * NDEPTH
F32 = jnp.float32
BF16 = jnp.bfloat16
VMEM = pl.BlockSpec(memory_space=pltpu.VMEM)
HBM = pl.BlockSpec(memory_space=pltpu.HBM)
SMEM = pl.BlockSpec(memory_space=pltpu.SMEM)

SHIFTED = ((1,), (-1, 2), (1, -8, 8), (-1, 18, -48, 32), (1, -32, 160, -256, 128))


def y_weights():
    out = np.zeros((256, ORDER * 128), np.float32)

    def add(k, column, sign):
        for m in range(1, ORDER + 1):
            for lane in range(max(0, column - m), min(128, column + m + 1)):
                out[k, (m - 1) * 128 + lane] += sign * comb(2 * m, m + lane - column) / 16.0**m

    for lane in range(128):
        add(lane, lane, 1)
    for lane in range(4):
        add(128 + lane, 128 + lane, 1)
        add(128 + 124 + lane, lane - 4, 1)
    for k in range(3):
        add(128 + 8 + k, -2 - k, -1)
        add(128 + 5 + k, 131 - k, -1)
    return out


def seam(values):
    lane = lax.broadcasted_iota(jnp.int32, (1, 8, 128), 2)
    sub = lax.broadcasted_iota(jnp.int32, (1, 8, 128), 1)
    inner = ((lane < 4) & (sub < 7)) | ((lane >= 124) & (sub > 0))
    edge = ((sub == 0) & (lane >= 8) & (lane <= 10)) | ((sub == 7) & (lane >= 5) & (lane <= 7))
    beside = jnp.where(lane < 64, pltpu.roll(values, 7, 1), pltpu.roll(values, 1, 1))
    return jnp.where(inner, beside, jnp.where(edge, pltpu.roll(values, 8, 2), 0.0))


def split_rows(values, left, at):
    rows = values.shape[0]
    for column, x in enumerate((values, seam(values))):
        x = x.reshape(rows * 8, 128)
        high = x.astype(BF16)
        left[pl.ds(at, rows * 8), pl.ds(128 * column, 128)] = high
        left[pl.ds(at, rows * 8), pl.ds(256 + 128 * column, 128)] = (x - high.astype(F32)).astype(BF16)


def multiply(left, rows, y_matrix):
    matrix = y_matrix[...]
    right = jnp.concatenate([matrix, matrix], axis=0)
    return jnp.dot(left[pl.ds(0, rows), :], right, preferred_element_type=F32)


def fetch(sems, *pairs):
    copies = [pltpu.make_async_copy(a, b, sems.at[k]) for k, (a, b) in enumerate(pairs)]
    for copy in copies:
        copy.start()
    for copy in copies:
        copy.wait()


def to_rows(flat, load_tile, row_tiles):
    for i in range(row_tiles):
        for j in range(8):
            flat[pl.ds((i * 8 + j) * 8, 8), :] = load_tile(i, j)


def row_of(flat, row):
    start = (row // 8) * 64 + row % 8
    return flat[pl.ds(start, 8, stride=8), :]


def planes_of(source, receiver):
    def loader(field, part, freq):
        return lambda i, j: field[part, freq, pl.ds(8 * i, 8), pl.ds(128 * j, 128)]

    return [
        loader(field, part, freq)
        for field in (source, receiver)
        for part in range(2)
        for freq in range(source.shape[1])
    ]


def slow_tile(planes, depth):
    columns = planes.shape[3]
    return lambda i, j: planes[
        128 * j // columns, depth, pl.ds(8 * i, 8), pl.ds(128 * j % columns, 128)
    ]


def pack_kernel(
    aperture_hbm, source_hbm, receiver_hbm, planes_hbm, ahead, behind,
    aperture, source, receiver, planes, sems, *flats,
):
    fetch(
        sems,
        (aperture_hbm, aperture),
        (source_hbm, source),
        (receiver_hbm, receiver),
        (planes_hbm.at[:, pl.ds(0, 1)], planes),
    )
    width = aperture[lax.axis_index("tile")]
    row_tiles = source.shape[2] // 8
    count = 4 * source.shape[1]
    loads = planes_of(source, receiver) + [slow_tile(planes, 0)]
    for plane, load in enumerate(loads):
        to_rows(flats[plane], load, row_tiles)
    for plane in range(count + 1):
        rows = HALO if plane < count else ORDER
        for k in range(rows):
            ahead[plane * HALO + k] = row_of(flats[plane], width - rows + k)
            behind[plane * HALO + k] = row_of(flats[plane], k)


def coefficients(weights, freq, slow_row, store):
    powers = weights.shape[1] // (2 * (ORDER + 1))
    for part in range(2 * (ORDER + 1)):
        value = weights[freq, part * powers + powers - 1]
        for power in range(powers - 2, -1, -1):
            value = value * slow_row + weights[freq, part * powers + power]
        store(part, value)


def sweep(freqs, fields, power, coefficient, write, partial, rows):
    def feed(held, value):
        kept = []
        for last in held:
            kept.append(value)
            value = value + last
        return kept, value

    for freq in range(freqs):
        for field in range(2):
            for part in range(2):
                p = (2 * field + part) * freqs + freq
                held = []
                for m in range(1, ORDER + 1):
                    chain = []
                    for k in range(2 * m):
                        value = power(p, m, ORDER - m + k)
                        chain, value = feed(chain, value)
                        chain.append(value)
                    held.append(chain)
                for o in range(rows):
                    kept, by_re, by_im = [], None, None
                    for m in range(ORDER + 1):
                        if m == 0:
                            value = fields(p, o)
                        else:
                            chain, value = feed(held[m - 1], power(p, m, o + ORDER + m))
                            kept.append(chain)
                        re = coefficient(freq, 2 * m, o) * value
                        im = coefficient(freq, 2 * m + 1, o) * value
                        by_re = re if by_re is None else by_re + re
                        by_im = im if by_im is None else by_im + im
                    held = kept
                    if part == 0:
                        partial[0, o] = by_re
                        partial[1, o] = by_im
                    elif field == 0:
                        write(p - freqs, o, partial[0, o] + by_im)
                        write(p, o, by_re - partial[1, o])
                    else:
                        write(p - freqs, o, partial[0, o] - by_im)
                        write(p, o, by_re + partial[1, o])


def image_row(freqs, load):
    total = None
    for k in range(2 * freqs):
        term = load(k) * load(2 * freqs + k)
        total = term if total is None else total + term
    return total


def power_of(ref, stride):
    def power(p, m, row):
        at = (p * stride + row) * 8
        at = at if isinstance(at, int) else pl.multiple_of(at, 8)
        return ref[pl.ds(at, 8), pl.ds(128 * (m - 1), 128)]

    return power


def own_kernel(
    frequency, order_table, filter_coeffs, source, receiver, planes, y_matrix,
    rows_out, powers_out, slow_out, weights_out, first_out, later_out,
    middle_out, middle_powers_out, last_out, first_image, last_image,
    flat, left, later_weights, partial,
):
    freqs, stored = source.shape[1:3]
    count = 4 * freqs
    row_tiles = stored // 8
    powers = filter_coeffs.shape[0]
    for plane, load in enumerate(planes_of(source, receiver)):
        to_rows(flat.at[plane], load, row_tiles)
        for r in range(stored):
            rows_out[plane, r] = row_of(flat.at[plane], r)
    for plane in range(count):
        split_rows(rows_out[plane], left, plane * stored * 8)
    powers_out[...] = multiply(left, count * stored * 8, y_matrix)

    for depth in range(NDEPTH):
        to_rows(flat.at[depth], slow_tile(planes, depth), row_tiles)
        for r in range(stored):
            slow_out[depth, r] = row_of(flat.at[depth], r)

    for depth, weights in enumerate((weights_out, later_weights)):
        for freq in range(freqs):
            omega = jnp.full((8, 128), frequency[freq], F32)
            active = [
                jnp.full((8, 128), jnp.where(order_table[depth, freq] >= n, 1.0, 0.0), F32)
                for n in range(ORDER + 1)
            ]
            for c in range(2):
                scale = None
                for j in range(powers):
                    scaled = [filter_coeffs[j, c, n] * active[n] for n in range(ORDER + 1)]
                    for m in range(ORDER + 1):
                        total = None
                        for n in range(m, ORDER + 1):
                            term = scaled[n] * float(SHIFTED[n][m])
                            total = term if total is None else total + term
                        if scale is not None:
                            total = total * scale
                        weights[freq, (m * 2 + c) * powers + j] = total
                    scale = omega if scale is None else scale * omega

    def tables(r, carry):
        for depth, (weights, out) in enumerate(((weights_out, first_out), (later_weights, later_out))):
            for freq in range(freqs):
                def store(part, value):
                    out[freq, part, r] = value

                coefficients(weights, freq, slow_out[depth, r], store)
        return carry

    lax.fori_loop(0, stored, tables, 0, unroll=2)

    inner = stored - 2 * ORDER

    def write_middle(p, o, value):
        middle_out[p, o] = value

    sweep(
        freqs,
        lambda p, o: rows_out[p, o + ORDER],
        power_of(powers_out, stored),
        lambda freq, part, o: first_out[freq, part, o + ORDER],
        write_middle,
        partial,
        inner,
    )
    for o in range(inner):
        first_image[o] = image_row(freqs, lambda p: middle_out[p, o])
    for plane in range(count):
        split_rows(middle_out[plane], left, plane * inner * 8)
    middle_powers_out[...] = multiply(left, count * inner * 8, y_matrix)

    def write_last(p, o, value):
        last_out[p, o] = value

    sweep(
        freqs,
        lambda p, o: middle_out[p, o + ORDER],
        power_of(middle_powers_out, inner),
        lambda freq, part, o: later_out[freq, part, o + HALO],
        write_last,
        partial,
        inner - 2 * ORDER,
    )
    for o in range(inner - 2 * ORDER):
        last_image[o] = image_row(freqs, lambda p: last_out[p, o])


def main_kernel(
    aperture, rows_in, powers_in, slow_in, weights, first_in, later,
    middle_in, middle_powers_in, last_in, first_image, last_image, y_matrix,
    from_before, from_after,
    image_out, receiver_out,
    flat, edges, left, edge_powers, slow, first, middle, middle_powers, last, images, partial,
):
    tile = lax.axis_index("tile")
    width = aperture[tile]
    count, stored = rows_in.shape[:2]
    freqs = count // 4
    row_tiles = stored // 8
    rows_one = stored + 2 * ORDER
    inner = stored - 2 * ORDER

    @pl.when(tile == 0)
    def _():
        for p in range(count):
            edges[p, HALO - 1] = jnp.zeros((8, 128), F32)
            for k in range(1, HALO):
                edges[p, HALO - 1 - k] = -rows_in[p, k - 1]
        slow[ORDER - 1] = slow_in[0, 0]
        for k in range(1, ORDER):
            slow[ORDER - 1 - k] = slow_in[0, k - 1]

    @pl.when(tile > 0)
    def _():
        for p in range(count):
            edges[p, pl.ds(0, HALO)] = from_before[pl.ds(p * HALO, HALO)]
        slow[pl.ds(0, ORDER)] = from_before[pl.ds(count * HALO, ORDER)]

    @pl.when(tile == lax.axis_size("tile") - 1)
    def _():
        for p in range(count):
            edges[p, HALO] = jnp.zeros((8, 128), F32)
            for k in range(1, HALO):
                edges[p, HALO + k] = -rows_in[p, width - k]
        slow[ORDER] = slow_in[0, width - 1]
        for k in range(1, ORDER):
            slow[ORDER + k] = slow_in[0, width - k]

    @pl.when(tile < lax.axis_size("tile") - 1)
    def _():
        for p in range(count):
            edges[p, pl.ds(HALO, HALO)] = from_after[pl.ds(p * HALO, HALO)]
        slow[pl.ds(ORDER, ORDER)] = from_after[pl.ds(count * HALO, ORDER)]

    for p in range(count):
        split_rows(edges[p], left, p * 2 * HALO * 8)
    edge_powers[...] = multiply(left, count * 2 * HALO * 8, y_matrix)
    for r in range(2 * ORDER):
        for freq in range(freqs):
            def store(part, value):
                first[freq, part, r] = value

            coefficients(weights, freq, slow[r], store)

    for p in range(count):
        middle[p, pl.ds(2 * ORDER, inner)] = middle_in[p]
    outer = power_of(edge_powers, 2 * HALO)
    own = power_of(powers_in, stored)

    def above(p, m, row):
        return outer(p, m, row) if row < HALO else own(p, m, row - HALO)

    def below(p, m, row):
        return own(p, m, row + width - HALO) if row < HALO else outer(p, m, row)

    def write_above(p, o, value):
        middle[p, o] = value

    def write_below(p, o, value):
        middle[p, o + width] = value

    sweep(
        freqs,
        lambda p, o: edges[p, o + ORDER] if o < ORDER else rows_in[p, o - ORDER],
        above,
        lambda freq, part, o: (
            first[freq, part, o] if o < ORDER else first_in[freq, part, o - ORDER]
        ),
        write_above,
        partial,
        2 * ORDER,
    )
    sweep(
        freqs,
        lambda p, o: rows_in[p, o + width - ORDER] if o < ORDER else edges[p, o + ORDER],
        below,
        lambda freq, part, o: (
            first_in[freq, part, o + width - ORDER] if o < ORDER else first[freq, part, o]
        ),
        write_below,
        partial,
        2 * ORDER,
    )
    for p in range(count):
        split_rows(middle[p, pl.ds(0, 2 * ORDER)], left, p * 4 * ORDER * 8)
        split_rows(middle[p, pl.ds(width, 2 * ORDER)], left, (p * 4 + 2) * ORDER * 8)
        middle_powers[pl.ds((p * rows_one + 2 * ORDER) * 8, inner * 8), :] = middle_powers_in[
            pl.ds(p * inner * 8, inner * 8), :
        ]
    edge_powers[...] = multiply(left, count * 4 * ORDER * 8, y_matrix)
    for p in range(count):
        size = 2 * ORDER * 8
        middle_powers[pl.ds(p * rows_one * 8, size), :] = edge_powers[pl.ds(2 * p * size, size), :]
        at = pl.multiple_of((p * rows_one + width) * 8, 8)
        middle_powers[pl.ds(at, size), :] = edge_powers[pl.ds((2 * p + 1) * size, size), :]
    for p in range(count):
        last[p, pl.ds(HALO, inner - 2 * ORDER)] = last_in[p]
    everywhere = power_of(middle_powers, rows_one)

    def write_first(p, o, value):
        last[p, o] = value

    def write_last(p, o, value):
        last[p, o + width - HALO] = value

    sweep(
        freqs,
        lambda p, o: middle[p, o + ORDER],
        everywhere,
        lambda freq, part, o: later[freq, part, o],
        write_first,
        partial,
        HALO,
    )
    sweep(
        freqs,
        lambda p, o: middle[p, o + width - ORDER],
        lambda p, m, row: everywhere(p, m, row + width - HALO),
        lambda freq, part, o: later[freq, part, o + width - HALO],
        write_last,
        partial,
        HALO,
    )

    images[0, pl.ds(ORDER, inner)] = first_image[...]
    images[1, pl.ds(HALO, inner - 2 * ORDER)] = last_image[...]
    for k in range(ORDER):
        images[0, k] = image_row(freqs, lambda p: middle[p, k + ORDER])
        images[0, width - ORDER + k] = image_row(freqs, lambda p: middle[p, width + k])
    for k in range(HALO):
        images[1, k] = image_row(freqs, lambda p: last[p, k])
        images[1, width - HALO + k] = image_row(freqs, lambda p: last[p, width - HALO + k])

    def put(slot, load_row, store_tile):
        for r in range(stored):
            at = (r // 8) * 64 + r % 8
            flat[slot, pl.ds(at, 8, stride=8), :] = jnp.where(r < width, load_row(r), 0.0)
        for i in range(row_tiles):
            for j in range(8):
                store_tile(i, j, flat[slot, pl.ds((i * 8 + j) * 8, 8), :])

    columns = image_out.shape[3]
    for depth in range(NDEPTH):
        def store_image(i, j, value):
            image_out[
                128 * j // columns, depth, pl.ds(8 * i, 8), pl.ds(128 * j % columns, 128)
            ] = value

        put(depth, lambda r: images[depth, r], store_image)
    for part in range(2):
        for freq in range(freqs):
            def store_receiver(i, j, value):
                receiver_out[part, freq, pl.ds(8 * i, 8), pl.ds(128 * j, 128)] = value

            p = (2 + part) * freqs + freq
            put(NDEPTH + part * freqs + freq, lambda r: last[p, r], store_receiver)


def passed_along(value, axis, steps):
    count = lax.axis_size(axis)
    initial, last = (max(0, -steps), min(count, count - steps))
    return lax.ppermute(value, axis, [(source, source + steps) for source in range(initial, last)])


def kernel(body, out_shape, in_specs, scratch, grant, name):
    return pl.pallas_call(
        body,
        out_shape=out_shape,
        in_specs=in_specs,
        out_specs=(VMEM,) * len(out_shape),
        scratch_shapes=scratch,
        compiler_params=pltpu.CompilerParams(vmem_limit_bytes=grant << 20),
        cost_estimate=pl.CostEstimate(flops=1000, bytes_accessed=1000, transcendentals=0),
        name=name,
    )


def shards(source_field, receiver_field, slowness, frequency, order_table, filter_coeffs, aperture):
    freqs, stored = source_field.shape[1:3]
    count = 4 * freqs
    parts = 2 * (ORDER + 1)
    rows_one = stored + 2 * ORDER
    inner = stored - 2 * ORDER
    wide = ORDER * 128

    def shape(*dims):
        return jax.ShapeDtypeStruct(dims, F32)

    def rows(*lead):
        return shape(*lead, 8, 128)

    def same(value):
        return pltpu.VMEM(value.shape, value.dtype)

    def scratch(*lead):
        return same(rows(*lead))

    planes = lax.all_gather(slowness, "freq", axis=0)
    halo = rows(count * HALO + ORDER)
    ahead, behind = kernel(
        pack_kernel,
        (halo, halo),
        [HBM] * 4,
        [
            pltpu.SMEM(aperture.shape, aperture.dtype),
            same(source_field),
            same(receiver_field),
            pltpu.VMEM((planes.shape[0], 1) + planes.shape[2:], F32),
            pltpu.SemaphoreType.DMA((4,)),
        ]
        + [pltpu.VMEM((stored * 8, 128), F32)] * (count + 1),
        60,
        "pack",
    )(aperture, source_field, receiver_field, planes)
    from_before = passed_along(ahead, "tile", 1)
    from_after = passed_along(behind, "tile", -1)

    y_matrix = jnp.asarray(y_weights(), BF16)
    coeffs = jnp.transpose(filter_coeffs, (2, 0, 1))
    weights = parts * coeffs.shape[0]
    own = kernel(
        own_kernel,
        (
            rows(count, stored),
            shape(count * stored * 8, wide),
            rows(NDEPTH, stored),
            rows(freqs, weights),
            rows(freqs, parts, stored),
            rows(freqs, parts, stored),
            rows(count, inner),
            shape(count * inner * 8, wide),
            rows(count, inner - 2 * ORDER),
            rows(inner),
            rows(inner - 2 * ORDER),
        ),
        [SMEM] * 3 + [VMEM] * 4,
        [
            pltpu.VMEM((count, stored * 8, 128), F32),
            pltpu.VMEM((count * stored * 8, 512), BF16),
            scratch(freqs, weights),
            scratch(2, inner),
        ],
        24,
        "own",
    )(frequency, order_table, coeffs, source_field, receiver_field, planes, y_matrix)
    image_parts, receiver_out = kernel(
        main_kernel,
        (shape(lax.axis_size("freq"), *slowness.shape), shape(*receiver_field.shape)),
        [SMEM] + [VMEM] * (len(own) + 3),
        [
            pltpu.VMEM((NDEPTH + 2 * freqs, stored * 8, 128), F32),
            scratch(count, 2 * HALO),
            pltpu.VMEM((count * 2 * HALO * 8, 512), BF16),
            pltpu.VMEM((count * 2 * HALO * 8, wide), F32),
            scratch(2 * ORDER),
            scratch(freqs, parts, 2 * ORDER),
            scratch(count, rows_one),
            pltpu.VMEM((count * rows_one * 8, wide), F32),
            scratch(count, stored),
            scratch(NDEPTH, stored),
            scratch(2, HALO),
        ],
        24,
        "migrate",
    )(aperture, *own, y_matrix, from_before, from_after)
    exchanged = lax.all_to_all(image_parts, "freq", 0, 0)
    return jnp.sum(exchanged, axis=0), receiver_out


def solution(mesh):
    placed = (
        P(None, "freq", "tile", None),
        P(None, "freq", "tile", None),
        P(None, "tile", "freq"),
        P("freq"),
        P(None, "freq"),
        P(),
        P(),
    )
    return jax.shard_map(
        shards,
        mesh=mesh,
        in_specs=placed,
        out_specs=(P(None, "tile", "freq"), P(None, "freq", "tile", None)),
        check_vma=False,
    )
```

```python
from math import comb

import jax
import jax.numpy as jnp
import numpy as np
from jax import lax
from jax.experimental import pallas as pl
from jax.experimental.pallas import tpu as pltpu
from jax.sharding import PartitionSpec as P

ORDER = 4
NDEPTH = 2
HALO = ORDER * NDEPTH
F32 = jnp.float32
BF16 = jnp.bfloat16
VMEM = pl.BlockSpec(memory_space=pltpu.VMEM)
SMEM = pl.BlockSpec(memory_space=pltpu.SMEM)

SHIFTED = ((1,), (-1, 2), (1, -8, 8), (-1, 18, -48, 32), (1, -32, 160, -256, 128))


def y_weights():
    out = np.zeros((256, ORDER * 128), np.float32)

    def add(k, column, sign):
        for m in range(1, ORDER + 1):
            for lane in range(max(0, column - m), min(128, column + m + 1)):
                out[k, (m - 1) * 128 + lane] += sign * comb(2 * m, m + lane - column) / 16.0**m

    for lane in range(128):
        add(lane, lane, 1)
    for lane in range(4):
        add(128 + lane, 128 + lane, 1)
        add(128 + 124 + lane, lane - 4, 1)
    for k in range(3):
        add(128 + 8 + k, -2 - k, -1)
        add(128 + 5 + k, 131 - k, -1)
    return out


def seam(values):
    lane = lax.broadcasted_iota(jnp.int32, (1, 8, 128), 2)
    sub = lax.broadcasted_iota(jnp.int32, (1, 8, 128), 1)
    inner = ((lane < 4) & (sub < 7)) | ((lane >= 124) & (sub > 0))
    edge = ((sub == 0) & (lane >= 8) & (lane <= 10)) | ((sub == 7) & (lane >= 5) & (lane <= 7))
    beside = jnp.where(lane < 64, pltpu.roll(values, 7, 1), pltpu.roll(values, 1, 1))
    return jnp.where(inner, beside, jnp.where(edge, pltpu.roll(values, 8, 2), 0.0))


def split_rows(values, left, at):
    rows = values.shape[0]
    for column, x in enumerate((values, seam(values))):
        x = x.reshape(rows * 8, 128)
        high = x.astype(BF16)
        left[pl.ds(at, rows * 8), pl.ds(128 * column, 128)] = high
        left[pl.ds(at, rows * 8), pl.ds(256 + 128 * column, 128)] = (x - high.astype(F32)).astype(BF16)


def multiply(left, rows, y_matrix):
    matrix = y_matrix[...]
    right = jnp.concatenate([matrix, matrix], axis=0)
    return jnp.dot(left[pl.ds(0, rows), :], right, preferred_element_type=F32)


def to_rows(flat, load_tile, row_tiles):
    for i in range(row_tiles):
        for j in range(8):
            flat[pl.ds((i * 8 + j) * 8, 8), :] = load_tile(i, j)


def row_of(flat, row):
    start = (row // 8) * 64 + row % 8
    return flat[pl.ds(start, 8, stride=8), :]


def planes_of(source, receiver):
    def loader(field, part, freq):
        return lambda i, j: field[part, freq, pl.ds(8 * i, 8), pl.ds(128 * j, 128)]

    return [
        loader(field, part, freq)
        for field in (source, receiver)
        for part in range(2)
        for freq in range(source.shape[1])
    ]


def slow_tile(planes, depth):
    columns = planes.shape[3]
    return lambda i, j: planes[
        128 * j // columns, depth, pl.ds(8 * i, 8), pl.ds(128 * j % columns, 128)
    ]


def ahead_kernel(aperture, source, receiver, planes, ahead, *flats):
    width = aperture[lax.axis_index("tile")]
    row_tiles = source.shape[2] // 8
    count = 4 * source.shape[1]
    for plane, load in enumerate(planes_of(source, receiver) + [slow_tile(planes, 0)]):
        to_rows(flats[plane], load, row_tiles)
    for plane in range(count + 1):
        rows = HALO if plane < count else ORDER
        for k in range(rows):
            ahead[plane * HALO + k] = row_of(flats[plane], width - rows + k)


def coefficients(weights, freq, slow_row, store):
    powers = weights.shape[1] // (2 * (ORDER + 1))
    for part in range(2 * (ORDER + 1)):
        value = weights[freq, part * powers + powers - 1]
        for power in range(powers - 2, -1, -1):
            value = value * slow_row + weights[freq, part * powers + power]
        store(part, value)


def sweep(freqs, fields, power, coefficient, write, partial, rows):
    def feed(held, value):
        kept = []
        for last in held:
            kept.append(value)
            value = value + last
        return kept, value

    for freq in range(freqs):
        for field in range(2):
            for part in range(2):
                p = (2 * field + part) * freqs + freq
                held = []
                for m in range(1, ORDER + 1):
                    chain = []
                    for k in range(2 * m):
                        value = power(p, m, ORDER - m + k)
                        chain, value = feed(chain, value)
                        chain.append(value)
                    held.append(chain)
                for o in range(rows):
                    kept, by_re, by_im = [], None, None
                    for m in range(ORDER + 1):
                        if m == 0:
                            value = fields(p, o)
                        else:
                            chain, value = feed(held[m - 1], power(p, m, o + ORDER + m))
                            kept.append(chain)
                        re = coefficient(freq, 2 * m, o) * value
                        im = coefficient(freq, 2 * m + 1, o) * value
                        by_re = re if by_re is None else by_re + re
                        by_im = im if by_im is None else by_im + im
                    held = kept
                    if part == 0:
                        partial[0, o] = by_re
                        partial[1, o] = by_im
                    elif field == 0:
                        write(p - freqs, o, partial[0, o] + by_im)
                        write(p, o, by_re - partial[1, o])
                    else:
                        write(p - freqs, o, partial[0, o] - by_im)
                        write(p, o, by_re + partial[1, o])


def image_row(freqs, load):
    total = None
    for k in range(2 * freqs):
        term = load(k) * load(2 * freqs + k)
        total = term if total is None else total + term
    return total


def power_of(ref, stride):
    def power(p, m, row):
        at = (p * stride + row) * 8
        at = at if isinstance(at, int) else pl.multiple_of(at, 8)
        return ref[pl.ds(at, 8), pl.ds(128 * (m - 1), 128)]

    return power


def rows_kernel(
    source, receiver, planes, y_matrix, behind, rows_out, powers_out, slow_out, flat, left
):
    freqs, stored = source.shape[1:3]
    count = 4 * freqs
    row_tiles = stored // 8
    for plane, load in enumerate(planes_of(source, receiver)):
        to_rows(flat.at[plane], load, row_tiles)
        for r in range(stored):
            rows_out[plane, r] = row_of(flat.at[plane], r)
    for depth in range(NDEPTH):
        to_rows(flat.at[depth], slow_tile(planes, depth), row_tiles)
        for r in range(stored):
            slow_out[depth, r] = row_of(flat.at[depth], r)
    for plane in range(count):
        behind[pl.ds(plane * HALO, HALO)] = rows_out[plane, pl.ds(0, HALO)]
    behind[pl.ds(count * HALO, ORDER)] = slow_out[0, pl.ds(0, ORDER)]
    for plane in range(count):
        split_rows(rows_out[plane], left, plane * stored * 8)
    powers_out[...] = multiply(left, count * stored * 8, y_matrix)


def own_kernel(
    frequency, order_table, filter_coeffs, rows_in, powers_in, slow_in, y_matrix,
    weights_out, first_out, later_out,
    middle_out, middle_powers_out, last_out, first_image, last_image,
    left, later_weights, partial,
):
    count, stored = rows_in.shape[:2]
    freqs = count // 4
    powers = filter_coeffs.shape[0]
    for depth, weights in enumerate((weights_out, later_weights)):
        for freq in range(freqs):
            omega = jnp.full((8, 128), frequency[freq], F32)
            active = [
                jnp.full((8, 128), jnp.where(order_table[depth, freq] >= n, 1.0, 0.0), F32)
                for n in range(ORDER + 1)
            ]
            for c in range(2):
                scale = None
                for j in range(powers):
                    scaled = [filter_coeffs[j, c, n] * active[n] for n in range(ORDER + 1)]
                    for m in range(ORDER + 1):
                        total = None
                        for n in range(m, ORDER + 1):
                            term = scaled[n] * float(SHIFTED[n][m])
                            total = term if total is None else total + term
                        if scale is not None:
                            total = total * scale
                        weights[freq, (m * 2 + c) * powers + j] = total
                    scale = omega if scale is None else scale * omega

    def tables(r, carry):
        for depth, (weights, out) in enumerate(((weights_out, first_out), (later_weights, later_out))):
            for freq in range(freqs):
                def store(part, value):
                    out[freq, part, r] = value

                coefficients(weights, freq, slow_in[depth, r], store)
        return carry

    lax.fori_loop(0, stored, tables, 0, unroll=2)

    inner = stored - 2 * ORDER

    def write_middle(p, o, value):
        middle_out[p, o] = value

    sweep(
        freqs,
        lambda p, o: rows_in[p, o + ORDER],
        power_of(powers_in, stored),
        lambda freq, part, o: first_out[freq, part, o + ORDER],
        write_middle,
        partial,
        inner,
    )
    for o in range(inner):
        first_image[o] = image_row(freqs, lambda p: middle_out[p, o])
    for plane in range(count):
        split_rows(middle_out[plane], left, plane * inner * 8)
    middle_powers_out[...] = multiply(left, count * inner * 8, y_matrix)

    def write_last(p, o, value):
        last_out[p, o] = value

    sweep(
        freqs,
        lambda p, o: middle_out[p, o + ORDER],
        power_of(middle_powers_out, inner),
        lambda freq, part, o: later_out[freq, part, o + HALO],
        write_last,
        partial,
        inner - 2 * ORDER,
    )
    for o in range(inner - 2 * ORDER):
        last_image[o] = image_row(freqs, lambda p: last_out[p, o])


def upper_kernel(
    rows_in, powers_in, slow_in, weights, first_in, later,
    middle_in, middle_powers_in, last_in, first_image, last_image, y_matrix, from_before,
    middle, middle_powers, last, images,
    edges, left, edge_powers, slow, first, partial,
):
    count, stored = rows_in.shape[:2]
    freqs = count // 4
    inner = stored - 2 * ORDER
    tile = lax.axis_index("tile")

    @pl.when(tile == 0)
    def _():
        for p in range(count):
            edges[p, HALO - 1] = jnp.zeros((8, 128), F32)
            for k in range(1, HALO):
                edges[p, HALO - 1 - k] = -rows_in[p, k - 1]
        slow[ORDER - 1] = slow_in[0, 0]
        for k in range(1, ORDER):
            slow[ORDER - 1 - k] = slow_in[0, k - 1]

    @pl.when(tile > 0)
    def _():
        for p in range(count):
            edges[p] = from_before[pl.ds(p * HALO, HALO)]
        slow[...] = from_before[pl.ds(count * HALO, ORDER)]

    for p in range(count):
        split_rows(edges[p], left, p * HALO * 8)
    edge_powers[...] = multiply(left, count * HALO * 8, y_matrix)
    for r in range(ORDER):
        for freq in range(freqs):
            def store(part, value):
                first[freq, part, r] = value

            coefficients(weights, freq, slow[r], store)

    outer = power_of(edge_powers, HALO)
    own = power_of(powers_in, stored)

    def write_middle(p, o, value):
        middle[p, o] = value

    sweep(
        freqs,
        lambda p, o: edges[p, o + ORDER] if o < ORDER else rows_in[p, o - ORDER],
        lambda p, m, row: outer(p, m, row) if row < HALO else own(p, m, row - HALO),
        lambda freq, part, o: (
            first[freq, part, o] if o < ORDER else first_in[freq, part, o - ORDER]
        ),
        write_middle,
        partial,
        2 * ORDER,
    )
    for p in range(count):
        middle[p, pl.ds(2 * ORDER, inner)] = middle_in[p]
        split_rows(middle[p, pl.ds(0, 2 * ORDER)], left, p * HALO * 8)
    edge_powers[...] = multiply(left, count * HALO * 8, y_matrix)
    for p in range(count):
        size = HALO * 8
        middle_powers[pl.ds(p * stored * 8, size), :] = edge_powers[pl.ds(p * size, size), :]
        middle_powers[pl.ds((p * stored + HALO) * 8, inner * 8), :] = middle_powers_in[
            pl.ds(p * inner * 8, inner * 8), :
        ]

    def write_last(p, o, value):
        last[p, o] = value

    sweep(
        freqs,
        lambda p, o: middle[p, o + ORDER],
        power_of(middle_powers, stored),
        lambda freq, part, o: later[freq, part, o],
        write_last,
        partial,
        HALO,
    )
    for p in range(count):
        last[p, pl.ds(HALO, inner - HALO)] = last_in[p]
    images[0, pl.ds(ORDER, inner)] = first_image[...]
    images[1, pl.ds(HALO, inner - HALO)] = last_image[...]
    for k in range(ORDER):
        images[0, k] = image_row(freqs, lambda p: middle[p, k + ORDER])
    for k in range(HALO):
        images[1, k] = image_row(freqs, lambda p: last[p, k])


def lower_kernel(
    aperture, rows_in, powers_in, slow_in, weights, first_in, later,
    middle_in, middle_powers_in, last_in, images_in, y_matrix, from_after,
    image_out, receiver_hbm,
    receiver_out, sem,
    flat, edges, left, edge_powers, slow, first, middle, last, images, partial,
):
    tile = lax.axis_index("tile")
    width = aperture[tile]
    count, stored = rows_in.shape[:2]
    freqs = count // 4
    row_tiles = stored // 8
    inner = stored - 2 * ORDER

    @pl.when(tile == lax.axis_size("tile") - 1)
    def _():
        for p in range(count):
            edges[p, 0] = jnp.zeros((8, 128), F32)
            for k in range(1, HALO):
                edges[p, k] = -rows_in[p, width - k]
        slow[0] = slow_in[0, width - 1]
        for k in range(1, ORDER):
            slow[k] = slow_in[0, width - k]

    @pl.when(tile < lax.axis_size("tile") - 1)
    def _():
        for p in range(count):
            edges[p] = from_after[pl.ds(p * HALO, HALO)]
        slow[...] = from_after[pl.ds(count * HALO, ORDER)]

    for p in range(count):
        split_rows(edges[p], left, p * HALO * 8)
    edge_powers[...] = multiply(left, count * HALO * 8, y_matrix)
    for r in range(ORDER):
        for freq in range(freqs):
            def store(part, value):
                first[freq, part, r] = value

            coefficients(weights, freq, slow[r], store)

    outer = power_of(edge_powers, HALO)
    own = power_of(powers_in, stored)
    done = power_of(middle_powers_in, stored)

    def write_middle(p, o, value):
        middle[p, o] = value

    sweep(
        freqs,
        lambda p, o: rows_in[p, o + width - ORDER] if o < ORDER else edges[p, o - ORDER],
        lambda p, m, row: (
            own(p, m, row + width - HALO) if row < HALO else outer(p, m, row - HALO)
        ),
        lambda freq, part, o: (
            first_in[freq, part, o + width - ORDER] if o < ORDER else first[freq, part, o - ORDER]
        ),
        write_middle,
        partial,
        2 * ORDER,
    )
    for p in range(count):
        split_rows(middle[p], left, p * HALO * 8)
    edge_powers[...] = multiply(left, count * HALO * 8, y_matrix)

    def write_last(p, o, value):
        last[p, o + width - HALO] = value

    for p in range(2 * freqs, count):
        last[p, pl.ds(0, inner)] = last_in[p]
    images[:, pl.ds(0, stored - ORDER)] = images_in[...]
    sweep(
        freqs,
        lambda p, o: middle_in[p, o + width - ORDER] if o < ORDER else middle[p, o - ORDER],
        lambda p, m, row: (
            done(p, m, row + width - HALO) if row < HALO else outer(p, m, row - HALO)
        ),
        lambda freq, part, o: later[freq, part, o + width - HALO],
        write_last,
        partial,
        HALO,
    )

    def put(slot, load_row, store_tile):
        for r in range(stored):
            at = (r // 8) * 64 + r % 8
            flat[slot, pl.ds(at, 8, stride=8), :] = jnp.where(r < width, load_row(r), 0.0)
        for i in range(row_tiles):
            for j in range(8):
                store_tile(i, j, flat[slot, pl.ds((i * 8 + j) * 8, 8), :])

    for part in range(2):
        for freq in range(freqs):
            def store_receiver(i, j, value):
                receiver_out[part, freq, pl.ds(8 * i, 8), pl.ds(128 * j, 128)] = value

            p = (2 + part) * freqs + freq
            put(NDEPTH + part * freqs + freq, lambda r: last[p, r], store_receiver)
    sent = pltpu.make_async_copy(receiver_out, receiver_hbm, sem)
    sent.start()

    for k in range(ORDER):
        images[0, width - ORDER + k] = image_row(freqs, lambda p: middle[p, k])
    for k in range(HALO):
        images[1, width - HALO + k] = image_row(freqs, lambda p: last[p, width - HALO + k])
    columns = image_out.shape[3]
    for depth in range(NDEPTH):
        def store_image(i, j, value):
            image_out[
                128 * j // columns, depth, pl.ds(8 * i, 8), pl.ds(128 * j % columns, 128)
            ] = value

        put(depth, lambda r: images[depth, r], store_image)
    sent.wait()


def passed_along(value, axis, steps):
    count = lax.axis_size(axis)
    initial, last = (max(0, -steps), min(count, count - steps))
    return lax.ppermute(value, axis, [(source, source + steps) for source in range(initial, last)])


def kernel(body, out_shape, in_specs, scratch, name):
    return pl.pallas_call(
        body,
        out_shape=out_shape,
        in_specs=in_specs,
        out_specs=(VMEM,) * len(out_shape),
        scratch_shapes=scratch,
        compiler_params=pltpu.CompilerParams(vmem_limit_bytes=24 << 20),
        cost_estimate=pl.CostEstimate(flops=1000, bytes_accessed=1000, transcendentals=0),
        name=name,
    )


def shards(source_field, receiver_field, slowness, frequency, order_table, filter_coeffs, aperture):
    freqs, stored = source_field.shape[1:3]
    count = 4 * freqs
    parts = 2 * (ORDER + 1)
    inner = stored - 2 * ORDER
    wide = ORDER * 128

    def shape(*dims):
        return jax.ShapeDtypeStruct(dims, F32)

    def rows(*lead):
        return shape(*lead, 8, 128)

    def same(value):
        return pltpu.VMEM(value.shape, value.dtype)

    def scratch(*lead):
        return same(rows(*lead))

    planes = lax.all_gather(slowness, "freq", axis=0)
    halo = rows(count * HALO + ORDER)
    flat = pltpu.VMEM((stored * 8, 128), F32)
    (ahead,) = kernel(
        ahead_kernel, (halo,), [SMEM] + [VMEM] * 3, [flat] * (count + 1), "ahead"
    )(aperture, source_field, receiver_field, planes)
    from_before = passed_along(ahead, "tile", 1)

    y_matrix = jnp.asarray(y_weights(), BF16)
    behind, own_rows, own_powers, slow = kernel(
        rows_kernel,
        (halo, rows(count, stored), shape(count * stored * 8, wide), rows(NDEPTH, stored)),
        [VMEM] * 4,
        [
            pltpu.VMEM((count, stored * 8, 128), F32),
            pltpu.VMEM((count * stored * 8, 512), BF16),
        ],
        "rows",
    )(source_field, receiver_field, planes, y_matrix)
    from_after = passed_along(behind, "tile", -1)

    coeffs = jnp.transpose(filter_coeffs, (2, 0, 1))
    terms = parts * coeffs.shape[0]
    weights, first, later, *inside = kernel(
        own_kernel,
        (
            rows(freqs, terms),
            rows(freqs, parts, stored),
            rows(freqs, parts, stored),
            rows(count, inner),
            shape(count * inner * 8, wide),
            rows(count, inner - HALO),
            rows(inner),
            rows(inner - HALO),
        ),
        [SMEM] * 3 + [VMEM] * 4,
        [
            pltpu.VMEM((count * inner * 8, 512), BF16),
            scratch(freqs, terms),
            scratch(2, inner),
        ],
        "own",
    )(frequency, order_table, coeffs, own_rows, own_powers, slow, y_matrix)
    edge = [
        scratch(count, HALO),
        pltpu.VMEM((count * HALO * 8, 512), BF16),
        pltpu.VMEM((count * HALO * 8, wide), F32),
        scratch(ORDER),
        scratch(freqs, parts, ORDER),
    ]
    tables = (own_rows, own_powers, slow, weights, first, later)
    upper = kernel(
        upper_kernel,
        (
            rows(count, stored),
            shape(count * stored * 8, wide),
            rows(count, inner),
            rows(NDEPTH, stored - ORDER),
        ),
        [VMEM] * (len(tables) + len(inside) + 2),
        edge + [scratch(2, HALO)],
        "upper",
    )(*tables, *inside, y_matrix, from_before)
    image_parts, receiver_out = pl.pallas_call(
        lower_kernel,
        out_shape=(
            shape(lax.axis_size("freq"), *slowness.shape),
            shape(*receiver_field.shape),
        ),
        in_specs=[SMEM] + [VMEM] * (len(tables) + len(upper) + 2),
        out_specs=(VMEM, pl.BlockSpec(memory_space=pl.ANY)),
        scratch_shapes=[
            same(receiver_field),
            pltpu.SemaphoreType.DMA,
            pltpu.VMEM((NDEPTH + 2 * freqs, stored * 8, 128), F32),
            *edge,
            scratch(count, HALO),
            scratch(count, stored),
            scratch(NDEPTH, stored),
            scratch(2, HALO),
        ],
        compiler_params=pltpu.CompilerParams(vmem_limit_bytes=24 << 20),
        cost_estimate=pl.CostEstimate(flops=1000, bytes_accessed=1000, transcendentals=0),
        name="lower",
    )(aperture, *tables, *upper, y_matrix, from_after)
    exchanged = lax.all_to_all(image_parts, "freq", 0, 0)
    return jnp.sum(exchanged, axis=0), receiver_out


def solution(mesh):
    placed = (
        P(None, "freq", "tile", None),
        P(None, "freq", "tile", None),
        P(None, "tile", "freq"),
        P("freq"),
        P(None, "freq"),
        P(),
        P(),
    )
    return jax.shard_map(
        shards,
        mesh=mesh,
        in_specs=placed,
        out_specs=(P(None, "tile", "freq"), P(None, "freq", "tile", None)),
        check_vma=False,
    )
```

```python
from math import comb

import jax
import jax.numpy as jnp
import numpy as np
from jax import lax
from jax.experimental import pallas as pl
from jax.experimental.pallas import tpu as pltpu
from jax.sharding import PartitionSpec as P

ORDER = 4
NDEPTH = 2
HALO = ORDER * NDEPTH
F32 = jnp.float32
BF16 = jnp.bfloat16
VMEM = pl.BlockSpec(memory_space=pltpu.VMEM)
SMEM = pl.BlockSpec(memory_space=pltpu.SMEM)

SHIFTED = ((1,), (-1, 2), (1, -8, 8), (-1, 18, -48, 32), (1, -32, 160, -256, 128))


def y_weights():
    out = np.zeros((256, ORDER * 128), np.float32)

    def add(k, column, sign):
        for m in range(1, ORDER + 1):
            for lane in range(max(0, column - m), min(128, column + m + 1)):
                out[k, (m - 1) * 128 + lane] += sign * comb(2 * m, m + lane - column) / 16.0**m

    for lane in range(128):
        add(lane, lane, 1)
    for lane in range(4):
        add(128 + lane, 128 + lane, 1)
        add(128 + 124 + lane, lane - 4, 1)
    for k in range(3):
        add(128 + 8 + k, -2 - k, -1)
        add(128 + 5 + k, 131 - k, -1)
    return out


def seam(values):
    lane = lax.broadcasted_iota(jnp.int32, (1, 8, 128), 2)
    sub = lax.broadcasted_iota(jnp.int32, (1, 8, 128), 1)
    inner = ((lane < 4) & (sub < 7)) | ((lane >= 124) & (sub > 0))
    edge = ((sub == 0) & (lane >= 8) & (lane <= 10)) | ((sub == 7) & (lane >= 5) & (lane <= 7))
    beside = jnp.where(lane < 64, pltpu.roll(values, 7, 1), pltpu.roll(values, 1, 1))
    return jnp.where(inner, beside, jnp.where(edge, pltpu.roll(values, 8, 2), 0.0))


def split_rows(values, left, at):
    rows = values.shape[0]
    for column, x in enumerate((values, seam(values))):
        x = x.reshape(rows * 8, 128)
        high = x.astype(BF16)
        left[pl.ds(at, rows * 8), pl.ds(128 * column, 128)] = high
        left[pl.ds(at, rows * 8), pl.ds(256 + 128 * column, 128)] = (x - high.astype(F32)).astype(BF16)


def multiply(left, rows, y_matrix):
    matrix = y_matrix[...]
    right = jnp.concatenate([matrix, matrix], axis=0)
    return jnp.dot(left[pl.ds(0, rows), :], right, preferred_element_type=F32)


def to_rows(flat, load_tile, row_tiles):
    for i in range(row_tiles):
        for j in range(8):
            flat[pl.ds((i * 8 + j) * 8, 8), :] = load_tile(i, j)


def row_of(flat, row):
    start = (row // 8) * 64 + row % 8
    return flat[pl.ds(start, 8, stride=8), :]


def planes_of(source, receiver):
    def loader(field, part, freq):
        return lambda i, j: field[part, freq, pl.ds(8 * i, 8), pl.ds(128 * j, 128)]

    return [
        loader(field, part, freq)
        for field in (source, receiver)
        for part in range(2)
        for freq in range(source.shape[1])
    ]


def slow_tile(planes, depth):
    columns = planes.shape[3]
    return lambda i, j: planes[
        128 * j // columns, depth, pl.ds(8 * i, 8), pl.ds(128 * j % columns, 128)
    ]


def ahead_kernel(aperture, source, receiver, planes, ahead, *flats):
    width = aperture[lax.axis_index("tile")]
    row_tiles = source.shape[2] // 8
    count = 4 * source.shape[1]
    for plane, load in enumerate(planes_of(source, receiver) + [slow_tile(planes, 0)]):
        to_rows(flats[plane], load, row_tiles)
    for plane in range(count + 1):
        rows = HALO if plane < count else ORDER
        for k in range(rows):
            ahead[plane * HALO + k] = row_of(flats[plane], width - rows + k)


def coefficients(weights, freq, slow_row, store):
    powers = weights.shape[1] // (2 * (ORDER + 1))
    for part in range(2 * (ORDER + 1)):
        value = weights[freq, part * powers + powers - 1]
        for power in range(powers - 2, -1, -1):
            value = value * slow_row + weights[freq, part * powers + power]
        store(part, value)


def sweep(freqs, fields, power, coefficient, write, partial, rows, which=(0, 1)):
    def feed(held, value):
        kept = []
        for last in held:
            kept.append(value)
            value = value + last
        return kept, value

    for freq in range(freqs):
        for field in which:
            for part in range(2):
                p = (2 * field + part) * freqs + freq
                held = []
                for m in range(1, ORDER + 1):
                    chain = []
                    for k in range(2 * m):
                        value = power(p, m, ORDER - m + k)
                        chain, value = feed(chain, value)
                        chain.append(value)
                    held.append(chain)
                for o in range(rows):
                    kept, by_re, by_im = [], None, None
                    for m in range(ORDER + 1):
                        if m == 0:
                            value = fields(p, o)
                        else:
                            chain, value = feed(held[m - 1], power(p, m, o + ORDER + m))
                            kept.append(chain)
                        re = coefficient(freq, 2 * m, o) * value
                        im = coefficient(freq, 2 * m + 1, o) * value
                        by_re = re if by_re is None else by_re + re
                        by_im = im if by_im is None else by_im + im
                    held = kept
                    if part == 0:
                        partial[0, o] = by_re
                        partial[1, o] = by_im
                    elif field == 0:
                        write(p - freqs, o, partial[0, o] + by_im)
                        write(p, o, by_re - partial[1, o])
                    else:
                        write(p - freqs, o, partial[0, o] - by_im)
                        write(p, o, by_re + partial[1, o])


def image_row(freqs, load):
    total = None
    for k in range(2 * freqs):
        term = load(k) * load(2 * freqs + k)
        total = term if total is None else total + term
    return total


def power_of(ref, stride):
    def power(p, m, row):
        at = (p * stride + row) * 8
        at = at if isinstance(at, int) else pl.multiple_of(at, 8)
        return ref[pl.ds(at, 8), pl.ds(128 * (m - 1), 128)]

    return power


def rows_kernel(
    source, receiver, planes, y_matrix, behind, rows_out, powers_out, slow_out, flat, left
):
    freqs, stored = source.shape[1:3]
    count = 4 * freqs
    row_tiles = stored // 8
    for plane, load in enumerate(planes_of(source, receiver)):
        to_rows(flat.at[plane], load, row_tiles)
        for r in range(stored):
            rows_out[plane, r] = row_of(flat.at[plane], r)
    for depth in range(NDEPTH):
        to_rows(flat.at[depth], slow_tile(planes, depth), row_tiles)
        for r in range(stored):
            slow_out[depth, r] = row_of(flat.at[depth], r)
    for plane in range(count):
        behind[pl.ds(plane * HALO, HALO)] = rows_out[plane, pl.ds(0, HALO)]
    behind[pl.ds(count * HALO, ORDER)] = slow_out[0, pl.ds(0, ORDER)]
    for plane in range(count):
        split_rows(rows_out[plane], left, plane * stored * 8)
    powers_out[...] = multiply(left, count * stored * 8, y_matrix)


def own_kernel(
    frequency, order_table, filter_coeffs, rows_in, powers_in, slow_in, y_matrix,
    weights_out, first_out, later_out,
    middle_out, middle_powers_out, last_out, first_image, last_image,
    left, later_weights, partial,
):
    count, stored = rows_in.shape[:2]
    freqs = count // 4
    powers = filter_coeffs.shape[0]
    for depth, weights in enumerate((weights_out, later_weights)):
        for freq in range(freqs):
            omega = jnp.full((8, 128), frequency[freq], F32)
            active = [
                jnp.full((8, 128), jnp.where(order_table[depth, freq] >= n, 1.0, 0.0), F32)
                for n in range(ORDER + 1)
            ]
            for c in range(2):
                scale = None
                for j in range(powers):
                    scaled = [filter_coeffs[j, c, n] * active[n] for n in range(ORDER + 1)]
                    for m in range(ORDER + 1):
                        total = None
                        for n in range(m, ORDER + 1):
                            term = scaled[n] * float(SHIFTED[n][m])
                            total = term if total is None else total + term
                        if scale is not None:
                            total = total * scale
                        weights[freq, (m * 2 + c) * powers + j] = total
                    scale = omega if scale is None else scale * omega

    def tables(r, carry):
        for depth, (weights, out) in enumerate(((weights_out, first_out), (later_weights, later_out))):
            for freq in range(freqs):
                def store(part, value):
                    out[freq, part, r] = value

                coefficients(weights, freq, slow_in[depth, r], store)
        return carry

    lax.fori_loop(0, stored, tables, 0, unroll=2)

    inner = stored - 2 * ORDER

    def write_middle(p, o, value):
        middle_out[p, o] = value

    sweep(
        freqs,
        lambda p, o: rows_in[p, o + ORDER],
        power_of(powers_in, stored),
        lambda freq, part, o: first_out[freq, part, o + ORDER],
        write_middle,
        partial,
        inner,
    )
    for o in range(inner):
        first_image[o] = image_row(freqs, lambda p: middle_out[p, o])
    for plane in range(count):
        split_rows(middle_out[plane], left, plane * inner * 8)
    middle_powers_out[...] = multiply(left, count * inner * 8, y_matrix)

    def write_last(p, o, value):
        last_out[p, o] = value

    sweep(
        freqs,
        lambda p, o: middle_out[p, o + ORDER],
        power_of(middle_powers_out, inner),
        lambda freq, part, o: later_out[freq, part, o + HALO],
        write_last,
        partial,
        inner - 2 * ORDER,
    )
    for o in range(inner - 2 * ORDER):
        last_image[o] = image_row(freqs, lambda p: last_out[p, o])


def upper_kernel(
    rows_in, powers_in, slow_in, weights, first_in, later,
    middle_in, middle_powers_in, last_in, first_image, last_image, y_matrix, from_before,
    middle, middle_powers, last, images,
    edges, left, edge_powers, slow, first, partial,
):
    count, stored = rows_in.shape[:2]
    freqs = count // 4
    inner = stored - 2 * ORDER
    tile = lax.axis_index("tile")

    @pl.when(tile == 0)
    def _():
        for p in range(count):
            edges[p, HALO - 1] = jnp.zeros((8, 128), F32)
            for k in range(1, HALO):
                edges[p, HALO - 1 - k] = -rows_in[p, k - 1]
        slow[ORDER - 1] = slow_in[0, 0]
        for k in range(1, ORDER):
            slow[ORDER - 1 - k] = slow_in[0, k - 1]

    @pl.when(tile > 0)
    def _():
        for p in range(count):
            edges[p] = from_before[pl.ds(p * HALO, HALO)]
        slow[...] = from_before[pl.ds(count * HALO, ORDER)]

    for p in range(count):
        split_rows(edges[p], left, p * HALO * 8)
    edge_powers[...] = multiply(left, count * HALO * 8, y_matrix)
    for r in range(ORDER):
        for freq in range(freqs):
            def store(part, value):
                first[freq, part, r] = value

            coefficients(weights, freq, slow[r], store)

    outer = power_of(edge_powers, HALO)
    own = power_of(powers_in, stored)

    def write_middle(p, o, value):
        middle[p, o] = value

    sweep(
        freqs,
        lambda p, o: edges[p, o + ORDER] if o < ORDER else rows_in[p, o - ORDER],
        lambda p, m, row: outer(p, m, row) if row < HALO else own(p, m, row - HALO),
        lambda freq, part, o: (
            first[freq, part, o] if o < ORDER else first_in[freq, part, o - ORDER]
        ),
        write_middle,
        partial,
        2 * ORDER,
    )
    for p in range(count):
        middle[p, pl.ds(2 * ORDER, inner)] = middle_in[p]
        split_rows(middle[p, pl.ds(0, 2 * ORDER)], left, p * HALO * 8)
    edge_powers[...] = multiply(left, count * HALO * 8, y_matrix)
    for p in range(count):
        size = HALO * 8
        middle_powers[pl.ds(p * stored * 8, size), :] = edge_powers[pl.ds(p * size, size), :]
        middle_powers[pl.ds((p * stored + HALO) * 8, inner * 8), :] = middle_powers_in[
            pl.ds(p * inner * 8, inner * 8), :
        ]

    def write_last(p, o, value):
        last[p, o] = value

    sweep(
        freqs,
        lambda p, o: middle[p, o + ORDER],
        power_of(middle_powers, stored),
        lambda freq, part, o: later[freq, part, o],
        write_last,
        partial,
        HALO,
    )
    for p in range(count):
        last[p, pl.ds(HALO, inner - HALO)] = last_in[p]
    images[0, pl.ds(ORDER, inner)] = first_image[...]
    images[1, pl.ds(HALO, inner - HALO)] = last_image[...]
    for k in range(ORDER):
        images[0, k] = image_row(freqs, lambda p: middle[p, k + ORDER])
    for k in range(HALO):
        images[1, k] = image_row(freqs, lambda p: last[p, k])


def lower_kernel(
    aperture, rows_in, powers_in, slow_in, weights, first_in, later,
    middle_in, middle_powers_in, last_in, images_in, y_matrix, from_after,
    image_out, receiver_hbm,
    receiver_out, sems,
    flat, edges, left, edge_powers, slow, first, middle, last, images, partial,
):
    tile = lax.axis_index("tile")
    width = aperture[tile]
    count, stored = rows_in.shape[:2]
    freqs = count // 4
    row_tiles = stored // 8
    inner = stored - 2 * ORDER

    @pl.when(tile == lax.axis_size("tile") - 1)
    def _():
        for p in range(count):
            edges[p, 0] = jnp.zeros((8, 128), F32)
            for k in range(1, HALO):
                edges[p, k] = -rows_in[p, width - k]
        slow[0] = slow_in[0, width - 1]
        for k in range(1, ORDER):
            slow[k] = slow_in[0, width - k]

    @pl.when(tile < lax.axis_size("tile") - 1)
    def _():
        for p in range(count):
            edges[p] = from_after[pl.ds(p * HALO, HALO)]
        slow[...] = from_after[pl.ds(count * HALO, ORDER)]

    for p in range(count):
        split_rows(edges[p], left, p * HALO * 8)
    edge_powers[...] = multiply(left, count * HALO * 8, y_matrix)
    for r in range(ORDER):
        for freq in range(freqs):
            def store(part, value):
                first[freq, part, r] = value

            coefficients(weights, freq, slow[r], store)

    outer = power_of(edge_powers, HALO)
    own = power_of(powers_in, stored)
    done = power_of(middle_powers_in, stored)

    def write_middle(p, o, value):
        middle[p, o] = value

    sweep(
        freqs,
        lambda p, o: rows_in[p, o + width - ORDER] if o < ORDER else edges[p, o - ORDER],
        lambda p, m, row: (
            own(p, m, row + width - HALO) if row < HALO else outer(p, m, row - HALO)
        ),
        lambda freq, part, o: (
            first_in[freq, part, o + width - ORDER] if o < ORDER else first[freq, part, o - ORDER]
        ),
        write_middle,
        partial,
        2 * ORDER,
    )
    for p in range(count):
        split_rows(middle[p], left, p * HALO * 8)
    edge_powers[...] = multiply(left, count * HALO * 8, y_matrix)

    def write_last(p, o, value):
        last[p, o + width - HALO] = value

    for p in range(2 * freqs, count):
        last[p, pl.ds(0, inner)] = last_in[p]
    images[:, pl.ds(0, stored - ORDER)] = images_in[...]

    def finish(which):
        sweep(
            freqs,
            lambda p, o: middle_in[p, o + width - ORDER] if o < ORDER else middle[p, o - ORDER],
            lambda p, m, row: (
                done(p, m, row + width - HALO) if row < HALO else outer(p, m, row - HALO)
            ),
            lambda freq, part, o: later[freq, part, o + width - HALO],
            write_last,
            partial,
            HALO,
            which,
        )

    def put(slot, load_row, store_tile):
        for r in range(stored):
            at = (r // 8) * 64 + r % 8
            flat[slot, pl.ds(at, 8, stride=8), :] = jnp.where(r < width, load_row(r), 0.0)
        for i in range(row_tiles):
            for j in range(8):
                store_tile(i, j, flat[slot, pl.ds((i * 8 + j) * 8, 8), :])

    finish((1,))
    sent = []
    for part in range(2):
        for freq in range(freqs):
            def store_receiver(i, j, value):
                receiver_out[part, freq, pl.ds(8 * i, 8), pl.ds(128 * j, 128)] = value

            p = (2 + part) * freqs + freq
            put(NDEPTH + part * freqs + freq, lambda r: last[p, r], store_receiver)
            sent.append(
                pltpu.make_async_copy(
                    receiver_out.at[part, freq],
                    receiver_hbm.at[part, freq],
                    sems.at[part * freqs + freq],
                )
            )
            sent[-1].start()
    finish((0,))

    for k in range(ORDER):
        images[0, width - ORDER + k] = image_row(freqs, lambda p: middle[p, k])
    for k in range(HALO):
        images[1, width - HALO + k] = image_row(freqs, lambda p: last[p, width - HALO + k])
    columns = image_out.shape[3]
    for depth in range(NDEPTH):
        def store_image(i, j, value):
            image_out[
                128 * j // columns, depth, pl.ds(8 * i, 8), pl.ds(128 * j % columns, 128)
            ] = value

        put(depth, lambda r: images[depth, r], store_image)
    for copy in sent:
        copy.wait()


def passed_along(value, axis, steps):
    count = lax.axis_size(axis)
    initial, last = (max(0, -steps), min(count, count - steps))
    return lax.ppermute(value, axis, [(source, source + steps) for source in range(initial, last)])


def kernel(body, out_shape, in_specs, scratch, name):
    return pl.pallas_call(
        body,
        out_shape=out_shape,
        in_specs=in_specs,
        out_specs=(VMEM,) * len(out_shape),
        scratch_shapes=scratch,
        compiler_params=pltpu.CompilerParams(vmem_limit_bytes=24 << 20),
        cost_estimate=pl.CostEstimate(flops=1000, bytes_accessed=1000, transcendentals=0),
        name=name,
    )


def shards(source_field, receiver_field, slowness, frequency, order_table, filter_coeffs, aperture):
    freqs, stored = source_field.shape[1:3]
    count = 4 * freqs
    parts = 2 * (ORDER + 1)
    inner = stored - 2 * ORDER
    wide = ORDER * 128

    def shape(*dims):
        return jax.ShapeDtypeStruct(dims, F32)

    def rows(*lead):
        return shape(*lead, 8, 128)

    def same(value):
        return pltpu.VMEM(value.shape, value.dtype)

    def scratch(*lead):
        return same(rows(*lead))

    planes = lax.all_gather(slowness, "freq", axis=0)
    halo = rows(count * HALO + ORDER)
    flat = pltpu.VMEM((stored * 8, 128), F32)
    (ahead,) = kernel(
        ahead_kernel, (halo,), [SMEM] + [VMEM] * 3, [flat] * (count + 1), "ahead"
    )(aperture, source_field, receiver_field, planes)
    from_before = passed_along(ahead, "tile", 1)

    y_matrix = jnp.asarray(y_weights(), BF16)
    behind, own_rows, own_powers, slow = kernel(
        rows_kernel,
        (halo, rows(count, stored), shape(count * stored * 8, wide), rows(NDEPTH, stored)),
        [VMEM] * 4,
        [
            pltpu.VMEM((count, stored * 8, 128), F32),
            pltpu.VMEM((count * stored * 8, 512), BF16),
        ],
        "rows",
    )(source_field, receiver_field, planes, y_matrix)
    from_after = passed_along(behind, "tile", -1)

    coeffs = jnp.transpose(filter_coeffs, (2, 0, 1))
    terms = parts * coeffs.shape[0]
    weights, first, later, *inside = kernel(
        own_kernel,
        (
            rows(freqs, terms),
            rows(freqs, parts, stored),
            rows(freqs, parts, stored),
            rows(count, inner),
            shape(count * inner * 8, wide),
            rows(count, inner - HALO),
            rows(inner),
            rows(inner - HALO),
        ),
        [SMEM] * 3 + [VMEM] * 4,
        [
            pltpu.VMEM((count * inner * 8, 512), BF16),
            scratch(freqs, terms),
            scratch(2, inner),
        ],
        "own",
    )(frequency, order_table, coeffs, own_rows, own_powers, slow, y_matrix)
    edge = [
        scratch(count, HALO),
        pltpu.VMEM((count * HALO * 8, 512), BF16),
        pltpu.VMEM((count * HALO * 8, wide), F32),
        scratch(ORDER),
        scratch(freqs, parts, ORDER),
    ]
    tables = (own_rows, own_powers, slow, weights, first, later)
    upper = kernel(
        upper_kernel,
        (
            rows(count, stored),
            shape(count * stored * 8, wide),
            rows(count, inner),
            rows(NDEPTH, stored - ORDER),
        ),
        [VMEM] * (len(tables) + len(inside) + 2),
        edge + [scratch(2, HALO)],
        "upper",
    )(*tables, *inside, y_matrix, from_before)
    image_parts, receiver_out = pl.pallas_call(
        lower_kernel,
        out_shape=(
            shape(lax.axis_size("freq"), *slowness.shape),
            shape(*receiver_field.shape),
        ),
        in_specs=[SMEM] + [VMEM] * (len(tables) + len(upper) + 2),
        out_specs=(VMEM, pl.BlockSpec(memory_space=pl.ANY)),
        scratch_shapes=[
            same(receiver_field),
            pltpu.SemaphoreType.DMA((2 * freqs,)),
            pltpu.VMEM((NDEPTH + 2 * freqs, stored * 8, 128), F32),
            *edge,
            scratch(count, HALO),
            scratch(count, stored),
            scratch(NDEPTH, stored),
            scratch(2, HALO),
        ],
        compiler_params=pltpu.CompilerParams(vmem_limit_bytes=24 << 20),
        cost_estimate=pl.CostEstimate(flops=1000, bytes_accessed=1000, transcendentals=0),
        name="lower",
    )(aperture, *tables, *upper, y_matrix, from_after)
    exchanged = lax.all_to_all(image_parts, "freq", 0, 0)
    return jnp.sum(exchanged, axis=0), receiver_out


def solution(mesh):
    placed = (
        P(None, "freq", "tile", None),
        P(None, "freq", "tile", None),
        P(None, "tile", "freq"),
        P("freq"),
        P(None, "freq"),
        P(),
        P(),
    )
    return jax.shard_map(
        shards,
        mesh=mesh,
        in_specs=placed,
        out_specs=(P(None, "tile", "freq"), P(None, "freq", "tile", None)),
        check_vma=False,
    )
```

```python
from math import comb

import jax
import jax.numpy as jnp
import numpy as np
from jax import lax
from jax.experimental import pallas as pl
from jax.experimental.pallas import tpu as pltpu
from jax.sharding import PartitionSpec as P

ORDER = 4
NDEPTH = 2
HALO = ORDER * NDEPTH
F32 = jnp.float32
BF16 = jnp.bfloat16
VMEM = pl.BlockSpec(memory_space=pltpu.VMEM)
SMEM = pl.BlockSpec(memory_space=pltpu.SMEM)

SHIFTED = ((1,), (-1, 2), (1, -8, 8), (-1, 18, -48, 32), (1, -32, 160, -256, 128))


def y_weights():
    out = np.zeros((256, ORDER * 128), np.float32)

    def add(k, column, sign):
        for m in range(1, ORDER + 1):
            for lane in range(max(0, column - m), min(128, column + m + 1)):
                out[k, (m - 1) * 128 + lane] += sign * comb(2 * m, m + lane - column) / 16.0**m

    for lane in range(128):
        add(lane, lane, 1)
    for lane in range(4):
        add(128 + lane, 128 + lane, 1)
        add(128 + 124 + lane, lane - 4, 1)
    for k in range(3):
        add(128 + 8 + k, -2 - k, -1)
        add(128 + 5 + k, 131 - k, -1)
    return out


def seam(values):
    lane = lax.broadcasted_iota(jnp.int32, (1, 8, 128), 2)
    sub = lax.broadcasted_iota(jnp.int32, (1, 8, 128), 1)
    inner = ((lane < 4) & (sub < 7)) | ((lane >= 124) & (sub > 0))
    edge = ((sub == 0) & (lane >= 8) & (lane <= 10)) | ((sub == 7) & (lane >= 5) & (lane <= 7))
    beside = jnp.where(lane < 64, pltpu.roll(values, 7, 1), pltpu.roll(values, 1, 1))
    return jnp.where(inner, beside, jnp.where(edge, pltpu.roll(values, 8, 2), 0.0))


def split_rows(values, left, at):
    rows = values.shape[0]
    for column, x in enumerate((values, seam(values))):
        x = x.reshape(rows * 8, 128)
        high = x.astype(BF16)
        left[pl.ds(at, rows * 8), pl.ds(128 * column, 128)] = high
        left[pl.ds(at, rows * 8), pl.ds(256 + 128 * column, 128)] = (x - high.astype(F32)).astype(BF16)


def multiply(left, rows, y_matrix):
    matrix = y_matrix[...]
    right = jnp.concatenate([matrix, matrix], axis=0)
    return jnp.dot(left[pl.ds(0, rows), :], right, preferred_element_type=F32)


def to_rows(flat, load_tile, row_tiles):
    for i in range(row_tiles):
        for j in range(8):
            flat[pl.ds((i * 8 + j) * 8, 8), :] = load_tile(i, j)


def row_of(flat, row):
    start = (row // 8) * 64 + row % 8
    return flat[pl.ds(start, 8, stride=8), :]


def planes_of(source, receiver):
    def loader(field, part, freq):
        return lambda i, j: field[part, freq, pl.ds(8 * i, 8), pl.ds(128 * j, 128)]

    return [
        loader(field, part, freq)
        for field in (source, receiver)
        for part in range(2)
        for freq in range(source.shape[1])
    ]


def slow_tile(planes, depth):
    columns = planes.shape[3]
    return lambda i, j: planes[
        128 * j // columns, depth, pl.ds(8 * i, 8), pl.ds(128 * j % columns, 128)
    ]


def slow_kernel(planes, out, flat):
    row_tiles = planes.shape[2] // 8
    for depth in range(NDEPTH):
        to_rows(flat.at[depth], slow_tile(planes, depth), row_tiles)
        for r in range(planes.shape[2]):
            out[depth, r] = row_of(flat.at[depth], r)


def ahead_kernel(aperture, source, receiver, slow, ahead, *flats):
    width = aperture[lax.axis_index("tile")]
    row_tiles = source.shape[2] // 8
    for plane, load in enumerate(planes_of(source, receiver)):
        to_rows(flats[plane], load, row_tiles)
        for k in range(HALO):
            ahead[plane * HALO + k] = row_of(flats[plane], width - HALO + k)
    end = 4 * source.shape[1] * HALO
    ahead[pl.ds(end, ORDER)] = slow[0, pl.ds(width - ORDER, ORDER)]


def coefficients(weights, freq, slow_row, store):
    powers = weights.shape[1] // (2 * (ORDER + 1))
    for part in range(2 * (ORDER + 1)):
        value = weights[freq, part * powers + powers - 1]
        for power in range(powers - 2, -1, -1):
            value = value * slow_row + weights[freq, part * powers + power]
        store(part, value)


def sweep(freqs, fields, power, coefficient, write, partial, rows, which=(0, 1)):
    def feed(held, value):
        kept = []
        for last in held:
            kept.append(value)
            value = value + last
        return kept, value

    for freq in range(freqs):
        for field in which:
            for part in range(2):
                p = (2 * field + part) * freqs + freq
                held = []
                for m in range(1, ORDER + 1):
                    chain = []
                    for k in range(2 * m):
                        value = power(p, m, ORDER - m + k)
                        chain, value = feed(chain, value)
                        chain.append(value)
                    held.append(chain)
                for o in range(rows):
                    kept, by_re, by_im = [], None, None
                    for m in range(ORDER + 1):
                        if m == 0:
                            value = fields(p, o)
                        else:
                            chain, value = feed(held[m - 1], power(p, m, o + ORDER + m))
                            kept.append(chain)
                        re = coefficient(freq, 2 * m, o) * value
                        im = coefficient(freq, 2 * m + 1, o) * value
                        by_re = re if by_re is None else by_re + re
                        by_im = im if by_im is None else by_im + im
                    held = kept
                    if part == 0:
                        partial[0, o] = by_re
                        partial[1, o] = by_im
                    elif field == 0:
                        write(p - freqs, o, partial[0, o] + by_im)
                        write(p, o, by_re - partial[1, o])
                    else:
                        write(p - freqs, o, partial[0, o] - by_im)
                        write(p, o, by_re + partial[1, o])


def image_row(freqs, load):
    total = None
    for k in range(2 * freqs):
        term = load(k) * load(2 * freqs + k)
        total = term if total is None else total + term
    return total


def power_of(ref, stride):
    def power(p, m, row):
        at = (p * stride + row) * 8
        at = at if isinstance(at, int) else pl.multiple_of(at, 8)
        return ref[pl.ds(at, 8), pl.ds(128 * (m - 1), 128)]

    return power


def rows_kernel(
    source, receiver, slow, y_matrix, behind, rows_out, powers_out, flat, left
):
    freqs, stored = source.shape[1:3]
    count = 4 * freqs
    row_tiles = stored // 8
    for plane, load in enumerate(planes_of(source, receiver)):
        to_rows(flat.at[plane], load, row_tiles)
        for r in range(stored):
            rows_out[plane, r] = row_of(flat.at[plane], r)
    for plane in range(count):
        behind[pl.ds(plane * HALO, HALO)] = rows_out[plane, pl.ds(0, HALO)]
    behind[pl.ds(count * HALO, ORDER)] = slow[0, pl.ds(0, ORDER)]
    for plane in range(count):
        split_rows(rows_out[plane], left, plane * stored * 8)
    powers_out[...] = multiply(left, count * stored * 8, y_matrix)


def own_kernel(
    frequency, order_table, filter_coeffs, rows_in, powers_in, slow_in, y_matrix,
    weights_out, first_out, later_out,
    middle_out, middle_powers_out, last_out, first_image, last_image,
    left, later_weights, partial,
):
    count, stored = rows_in.shape[:2]
    freqs = count // 4
    powers = filter_coeffs.shape[0]
    for depth, weights in enumerate((weights_out, later_weights)):
        for freq in range(freqs):
            omega = jnp.full((8, 128), frequency[freq], F32)
            active = [
                jnp.full((8, 128), jnp.where(order_table[depth, freq] >= n, 1.0, 0.0), F32)
                for n in range(ORDER + 1)
            ]
            for c in range(2):
                scale = None
                for j in range(powers):
                    scaled = [filter_coeffs[j, c, n] * active[n] for n in range(ORDER + 1)]
                    for m in range(ORDER + 1):
                        total = None
                        for n in range(m, ORDER + 1):
                            term = scaled[n] * float(SHIFTED[n][m])
                            total = term if total is None else total + term
                        if scale is not None:
                            total = total * scale
                        weights[freq, (m * 2 + c) * powers + j] = total
                    scale = omega if scale is None else scale * omega

    def tables(r, carry):
        for depth, (weights, out) in enumerate(((weights_out, first_out), (later_weights, later_out))):
            for freq in range(freqs):
                def store(part, value):
                    out[freq, part, r] = value

                coefficients(weights, freq, slow_in[depth, r], store)
        return carry

    lax.fori_loop(0, stored, tables, 0, unroll=2)

    inner = stored - 2 * ORDER

    def write_middle(p, o, value):
        middle_out[p, o] = value

    sweep(
        freqs,
        lambda p, o: rows_in[p, o + ORDER],
        power_of(powers_in, stored),
        lambda freq, part, o: first_out[freq, part, o + ORDER],
        write_middle,
        partial,
        inner,
    )
    for o in range(inner):
        first_image[o] = image_row(freqs, lambda p: middle_out[p, o])
    for plane in range(count):
        split_rows(middle_out[plane], left, plane * inner * 8)
    middle_powers_out[...] = multiply(left, count * inner * 8, y_matrix)

    def write_last(p, o, value):
        last_out[p, o] = value

    sweep(
        freqs,
        lambda p, o: middle_out[p, o + ORDER],
        power_of(middle_powers_out, inner),
        lambda freq, part, o: later_out[freq, part, o + HALO],
        write_last,
        partial,
        inner - 2 * ORDER,
    )
    for o in range(inner - 2 * ORDER):
        last_image[o] = image_row(freqs, lambda p: last_out[p, o])


def upper_kernel(
    rows_in, powers_in, slow_in, weights, first_in, later,
    middle_in, middle_powers_in, last_in, first_image, last_image, y_matrix, from_before,
    middle, middle_powers, last, images,
    edges, left, edge_powers, slow, first, partial,
):
    count, stored = rows_in.shape[:2]
    freqs = count // 4
    inner = stored - 2 * ORDER
    tile = lax.axis_index("tile")

    @pl.when(tile == 0)
    def _():
        for p in range(count):
            edges[p, HALO - 1] = jnp.zeros((8, 128), F32)
            for k in range(1, HALO):
                edges[p, HALO - 1 - k] = -rows_in[p, k - 1]
        slow[ORDER - 1] = slow_in[0, 0]
        for k in range(1, ORDER):
            slow[ORDER - 1 - k] = slow_in[0, k - 1]

    @pl.when(tile > 0)
    def _():
        for p in range(count):
            edges[p] = from_before[pl.ds(p * HALO, HALO)]
        slow[...] = from_before[pl.ds(count * HALO, ORDER)]

    for p in range(count):
        split_rows(edges[p], left, p * HALO * 8)
    edge_powers[...] = multiply(left, count * HALO * 8, y_matrix)
    for r in range(ORDER):
        for freq in range(freqs):
            def store(part, value):
                first[freq, part, r] = value

            coefficients(weights, freq, slow[r], store)

    outer = power_of(edge_powers, HALO)
    own = power_of(powers_in, stored)

    def write_middle(p, o, value):
        middle[p, o] = value

    sweep(
        freqs,
        lambda p, o: edges[p, o + ORDER] if o < ORDER else rows_in[p, o - ORDER],
        lambda p, m, row: outer(p, m, row) if row < HALO else own(p, m, row - HALO),
        lambda freq, part, o: (
            first[freq, part, o] if o < ORDER else first_in[freq, part, o - ORDER]
        ),
        write_middle,
        partial,
        2 * ORDER,
    )
    for p in range(count):
        middle[p, pl.ds(2 * ORDER, inner)] = middle_in[p]
        split_rows(middle[p, pl.ds(0, 2 * ORDER)], left, p * HALO * 8)
    edge_powers[...] = multiply(left, count * HALO * 8, y_matrix)
    for p in range(count):
        size = HALO * 8
        middle_powers[pl.ds(p * stored * 8, size), :] = edge_powers[pl.ds(p * size, size), :]
        middle_powers[pl.ds((p * stored + HALO) * 8, inner * 8), :] = middle_powers_in[
            pl.ds(p * inner * 8, inner * 8), :
        ]

    def write_last(p, o, value):
        last[p, o] = value

    sweep(
        freqs,
        lambda p, o: middle[p, o + ORDER],
        power_of(middle_powers, stored),
        lambda freq, part, o: later[freq, part, o],
        write_last,
        partial,
        HALO,
    )
    for p in range(count):
        last[p, pl.ds(HALO, inner - HALO)] = last_in[p]
    images[0, pl.ds(ORDER, inner)] = first_image[...]
    images[1, pl.ds(HALO, inner - HALO)] = last_image[...]
    for k in range(ORDER):
        images[0, k] = image_row(freqs, lambda p: middle[p, k + ORDER])
    for k in range(HALO):
        images[1, k] = image_row(freqs, lambda p: last[p, k])


def lower_kernel(
    aperture, rows_in, powers_in, slow_in, weights, first_in, later,
    middle_in, middle_powers_in, last_in, images_in, y_matrix, from_after,
    image_out, receiver_hbm,
    receiver_out, sems,
    flat, edges, left, edge_powers, slow, first, middle, last, images, partial,
):
    tile = lax.axis_index("tile")
    width = aperture[tile]
    count, stored = rows_in.shape[:2]
    freqs = count // 4
    row_tiles = stored // 8
    inner = stored - 2 * ORDER

    @pl.when(tile == lax.axis_size("tile") - 1)
    def _():
        for p in range(count):
            edges[p, 0] = jnp.zeros((8, 128), F32)
            for k in range(1, HALO):
                edges[p, k] = -rows_in[p, width - k]
        slow[0] = slow_in[0, width - 1]
        for k in range(1, ORDER):
            slow[k] = slow_in[0, width - k]

    @pl.when(tile < lax.axis_size("tile") - 1)
    def _():
        for p in range(count):
            edges[p] = from_after[pl.ds(p * HALO, HALO)]
        slow[...] = from_after[pl.ds(count * HALO, ORDER)]

    for p in range(count):
        split_rows(edges[p], left, p * HALO * 8)
    edge_powers[...] = multiply(left, count * HALO * 8, y_matrix)
    for r in range(ORDER):
        for freq in range(freqs):
            def store(part, value):
                first[freq, part, r] = value

            coefficients(weights, freq, slow[r], store)

    outer = power_of(edge_powers, HALO)
    own = power_of(powers_in, stored)
    done = power_of(middle_powers_in, stored)

    def write_middle(p, o, value):
        middle[p, o] = value

    sweep(
        freqs,
        lambda p, o: rows_in[p, o + width - ORDER] if o < ORDER else edges[p, o - ORDER],
        lambda p, m, row: (
            own(p, m, row + width - HALO) if row < HALO else outer(p, m, row - HALO)
        ),
        lambda freq, part, o: (
            first_in[freq, part, o + width - ORDER] if o < ORDER else first[freq, part, o - ORDER]
        ),
        write_middle,
        partial,
        2 * ORDER,
    )
    for p in range(count):
        split_rows(middle[p], left, p * HALO * 8)
    edge_powers[...] = multiply(left, count * HALO * 8, y_matrix)

    def write_last(p, o, value):
        last[p, o + width - HALO] = value

    for p in range(2 * freqs, count):
        last[p, pl.ds(0, inner)] = last_in[p]
    images[:, pl.ds(0, stored - ORDER)] = images_in[...]

    def finish(which):
        sweep(
            freqs,
            lambda p, o: middle_in[p, o + width - ORDER] if o < ORDER else middle[p, o - ORDER],
            lambda p, m, row: (
                done(p, m, row + width - HALO) if row < HALO else outer(p, m, row - HALO)
            ),
            lambda freq, part, o: later[freq, part, o + width - HALO],
            write_last,
            partial,
            HALO,
            which,
        )

    def put(slot, load_row, store_tile):
        for r in range(stored):
            at = (r // 8) * 64 + r % 8
            flat[slot, pl.ds(at, 8, stride=8), :] = jnp.where(r < width, load_row(r), 0.0)
        for i in range(row_tiles):
            for j in range(8):
                store_tile(i, j, flat[slot, pl.ds((i * 8 + j) * 8, 8), :])

    finish((1,))
    sent = []
    for part in range(2):
        for freq in range(freqs):
            def store_receiver(i, j, value):
                receiver_out[part, freq, pl.ds(8 * i, 8), pl.ds(128 * j, 128)] = value

            p = (2 + part) * freqs + freq
            put(NDEPTH + part * freqs + freq, lambda r: last[p, r], store_receiver)
            sent.append(
                pltpu.make_async_copy(
                    receiver_out.at[part, freq],
                    receiver_hbm.at[part, freq],
                    sems.at[part * freqs + freq],
                )
            )
            sent[-1].start()
    finish((0,))

    for k in range(ORDER):
        images[0, width - ORDER + k] = image_row(freqs, lambda p: middle[p, k])
    for k in range(HALO):
        images[1, width - HALO + k] = image_row(freqs, lambda p: last[p, width - HALO + k])
    columns = image_out.shape[3]
    for depth in range(NDEPTH):
        def store_image(i, j, value):
            image_out[
                128 * j // columns, depth, pl.ds(8 * i, 8), pl.ds(128 * j % columns, 128)
            ] = value

        put(depth, lambda r: images[depth, r], store_image)
    for copy in sent:
        copy.wait()


def passed_along(value, axis, steps):
    count = lax.axis_size(axis)
    initial, last = (max(0, -steps), min(count, count - steps))
    return lax.ppermute(value, axis, [(source, source + steps) for source in range(initial, last)])


def kernel(body, out_shape, in_specs, scratch, name, cost=1000):
    return pl.pallas_call(
        body,
        out_shape=out_shape,
        in_specs=in_specs,
        out_specs=(VMEM,) * len(out_shape),
        scratch_shapes=scratch,
        compiler_params=pltpu.CompilerParams(vmem_limit_bytes=24 << 20),
        cost_estimate=pl.CostEstimate(flops=cost, bytes_accessed=cost, transcendentals=0),
        name=name,
    )


def shards(source_field, receiver_field, slowness, frequency, order_table, filter_coeffs, aperture):
    freqs, stored = source_field.shape[1:3]
    count = 4 * freqs
    parts = 2 * (ORDER + 1)
    inner = stored - 2 * ORDER
    wide = ORDER * 128

    def shape(*dims):
        return jax.ShapeDtypeStruct(dims, F32)

    def rows(*lead):
        return shape(*lead, 8, 128)

    def same(value):
        return pltpu.VMEM(value.shape, value.dtype)

    def scratch(*lead):
        return same(rows(*lead))

    planes = lax.all_gather(slowness, "freq", axis=0)
    halo = rows(count * HALO + ORDER)
    flat = pltpu.VMEM((stored * 8, 128), F32)
    (slow,) = kernel(
        slow_kernel,
        (rows(NDEPTH, stored),),
        [VMEM],
        [pltpu.VMEM((NDEPTH, stored * 8, 128), F32)],
        "slow",
        1 << 30,
    )(planes)
    (ahead,) = kernel(
        ahead_kernel, (halo,), [SMEM] + [VMEM] * 3, [flat] * count, "ahead"
    )(aperture, source_field, receiver_field, slow)
    from_before = passed_along(ahead, "tile", 1)

    y_matrix = jnp.asarray(y_weights(), BF16)
    behind, own_rows, own_powers = kernel(
        rows_kernel,
        (halo, rows(count, stored), shape(count * stored * 8, wide)),
        [VMEM] * 4,
        [
            pltpu.VMEM((count, stored * 8, 128), F32),
            pltpu.VMEM((count * stored * 8, 512), BF16),
        ],
        "rows",
    )(source_field, receiver_field, slow, y_matrix)
    from_after = passed_along(behind, "tile", -1)

    coeffs = jnp.transpose(filter_coeffs, (2, 0, 1))
    terms = parts * coeffs.shape[0]
    weights, first, later, *inside = kernel(
        own_kernel,
        (
            rows(freqs, terms),
            rows(freqs, parts, stored),
            rows(freqs, parts, stored),
            rows(count, inner),
            shape(count * inner * 8, wide),
            rows(count, inner - HALO),
            rows(inner),
            rows(inner - HALO),
        ),
        [SMEM] * 3 + [VMEM] * 4,
        [
            pltpu.VMEM((count * inner * 8, 512), BF16),
            scratch(freqs, terms),
            scratch(2, inner),
        ],
        "own",
    )(frequency, order_table, coeffs, own_rows, own_powers, slow, y_matrix)
    edge = [
        scratch(count, HALO),
        pltpu.VMEM((count * HALO * 8, 512), BF16),
        pltpu.VMEM((count * HALO * 8, wide), F32),
        scratch(ORDER),
        scratch(freqs, parts, ORDER),
    ]
    tables = (own_rows, own_powers, slow, weights, first, later)
    upper = kernel(
        upper_kernel,
        (
            rows(count, stored),
            shape(count * stored * 8, wide),
            rows(count, inner),
            rows(NDEPTH, stored - ORDER),
        ),
        [VMEM] * (len(tables) + len(inside) + 2),
        edge + [scratch(2, HALO)],
        "upper",
    )(*tables, *inside, y_matrix, from_before)
    image_parts, receiver_out = pl.pallas_call(
        lower_kernel,
        out_shape=(
            shape(lax.axis_size("freq"), *slowness.shape),
            shape(*receiver_field.shape),
        ),
        in_specs=[SMEM] + [VMEM] * (len(tables) + len(upper) + 2),
        out_specs=(VMEM, pl.BlockSpec(memory_space=pl.ANY)),
        scratch_shapes=[
            same(receiver_field),
            pltpu.SemaphoreType.DMA((2 * freqs,)),
            pltpu.VMEM((NDEPTH + 2 * freqs, stored * 8, 128), F32),
            *edge,
            scratch(count, HALO),
            scratch(count, stored),
            scratch(NDEPTH, stored),
            scratch(2, HALO),
        ],
        compiler_params=pltpu.CompilerParams(vmem_limit_bytes=24 << 20),
        cost_estimate=pl.CostEstimate(flops=1000, bytes_accessed=1000, transcendentals=0),
        name="lower",
    )(aperture, *tables, *upper, y_matrix, from_after)
    exchanged = lax.all_to_all(image_parts, "freq", 0, 0)
    return jnp.sum(exchanged, axis=0), receiver_out


def solution(mesh):
    placed = (
        P(None, "freq", "tile", None),
        P(None, "freq", "tile", None),
        P(None, "tile", "freq"),
        P("freq"),
        P(None, "freq"),
        P(),
        P(),
    )
    return jax.shard_map(
        shards,
        mesh=mesh,
        in_specs=placed,
        out_specs=(P(None, "tile", "freq"), P(None, "freq", "tile", None)),
        check_vma=False,
    )
```

```python
from math import comb

import jax
import jax.numpy as jnp
import numpy as np
from jax import lax
from jax.experimental import pallas as pl
from jax.experimental.pallas import tpu as pltpu
from jax.sharding import PartitionSpec as P

ORDER = 4
NDEPTH = 2
HALO = ORDER * NDEPTH
F32 = jnp.float32
BF16 = jnp.bfloat16
VMEM = pl.BlockSpec(memory_space=pltpu.VMEM)
SMEM = pl.BlockSpec(memory_space=pltpu.SMEM)

SHIFTED = ((1,), (-1, 2), (1, -8, 8), (-1, 18, -48, 32), (1, -32, 160, -256, 128))


def y_weights():
    out = np.zeros((256, ORDER * 128), np.float32)

    def add(k, column, sign):
        for m in range(1, ORDER + 1):
            for lane in range(max(0, column - m), min(128, column + m + 1)):
                out[k, (m - 1) * 128 + lane] += sign * comb(2 * m, m + lane - column) / 16.0**m

    for lane in range(128):
        add(lane, lane, 1)
    for lane in range(4):
        add(128 + lane, 128 + lane, 1)
        add(128 + 124 + lane, lane - 4, 1)
    for k in range(3):
        add(128 + 8 + k, -2 - k, -1)
        add(128 + 5 + k, 131 - k, -1)
    return out


def seam(values):
    lane = lax.broadcasted_iota(jnp.int32, (1, 8, 128), 2)
    sub = lax.broadcasted_iota(jnp.int32, (1, 8, 128), 1)
    inner = ((lane < 4) & (sub < 7)) | ((lane >= 124) & (sub > 0))
    edge = ((sub == 0) & (lane >= 8) & (lane <= 10)) | ((sub == 7) & (lane >= 5) & (lane <= 7))
    beside = jnp.where(lane < 64, pltpu.roll(values, 7, 1), pltpu.roll(values, 1, 1))
    return jnp.where(inner, beside, jnp.where(edge, pltpu.roll(values, 8, 2), 0.0))


def split_rows(values, left, at):
    rows = values.shape[0]
    for column, x in enumerate((values, seam(values))):
        x = x.reshape(rows * 8, 128)
        high = x.astype(BF16)
        left[pl.ds(at, rows * 8), pl.ds(128 * column, 128)] = high
        left[pl.ds(at, rows * 8), pl.ds(256 + 128 * column, 128)] = (x - high.astype(F32)).astype(BF16)


def multiply(left, rows, y_matrix):
    matrix = y_matrix[...]
    right = jnp.concatenate([matrix, matrix], axis=0)
    return jnp.dot(left[pl.ds(0, rows), :], right, preferred_element_type=F32)


def to_rows(flat, load_tile, row_tiles):
    for i in range(row_tiles):
        for j in range(8):
            flat[pl.ds((i * 8 + j) * 8, 8), :] = load_tile(i, j)


def row_of(flat, row):
    start = (row // 8) * 64 + row % 8
    return flat[pl.ds(start, 8, stride=8), :]


def planes_of(source, receiver):
    def loader(field, part, freq):
        return lambda i, j: field[part, freq, pl.ds(8 * i, 8), pl.ds(128 * j, 128)]

    return [
        loader(field, part, freq)
        for field in (source, receiver)
        for part in range(2)
        for freq in range(source.shape[1])
    ]


def slow_tile(planes, depth):
    columns = planes.shape[3]
    return lambda i, j: planes[
        128 * j // columns, depth, pl.ds(8 * i, 8), pl.ds(128 * j % columns, 128)
    ]


def slow_kernel(planes, out, flat):
    row_tiles = planes.shape[2] // 8
    for depth in range(NDEPTH):
        to_rows(flat.at[depth], slow_tile(planes, depth), row_tiles)
        for r in range(planes.shape[2]):
            out[depth, r] = row_of(flat.at[depth], r)


def ahead_kernel(aperture, source, receiver, slow, ahead, *flats):
    width = aperture[lax.axis_index("tile")]
    row_tiles = source.shape[2] // 8
    for plane, load in enumerate(planes_of(source, receiver)):
        to_rows(flats[plane], load, row_tiles)
        for k in range(HALO):
            ahead[plane * HALO + k] = row_of(flats[plane], width - HALO + k)
    end = 4 * source.shape[1] * HALO
    ahead[pl.ds(end, ORDER)] = slow[0, pl.ds(width - ORDER, ORDER)]


def coefficients(weights, freq, slow_row, store):
    powers = weights.shape[1] // (2 * (ORDER + 1))
    for part in range(2 * (ORDER + 1)):
        value = weights[freq, part * powers + powers - 1]
        for power in range(powers - 2, -1, -1):
            value = value * slow_row + weights[freq, part * powers + power]
        store(part, value)


def sweep(freqs, fields, power, coefficient, write, partial, rows, which=(0, 1)):
    def feed(held, value):
        kept = []
        for last in held:
            kept.append(value)
            value = value + last
        return kept, value

    for freq in range(freqs):
        for field in which:
            for part in range(2):
                p = (2 * field + part) * freqs + freq
                held = []
                for m in range(1, ORDER + 1):
                    chain = []
                    for k in range(2 * m):
                        value = power(p, m, ORDER - m + k)
                        chain, value = feed(chain, value)
                        chain.append(value)
                    held.append(chain)
                for o in range(rows):
                    kept, by_re, by_im = [], None, None
                    for m in range(ORDER + 1):
                        if m == 0:
                            value = fields(p, o)
                        else:
                            chain, value = feed(held[m - 1], power(p, m, o + ORDER + m))
                            kept.append(chain)
                        re = coefficient(freq, 2 * m, o) * value
                        im = coefficient(freq, 2 * m + 1, o) * value
                        by_re = re if by_re is None else by_re + re
                        by_im = im if by_im is None else by_im + im
                    held = kept
                    if part == 0:
                        partial[0, o] = by_re
                        partial[1, o] = by_im
                    elif field == 0:
                        write(p - freqs, o, partial[0, o] + by_im)
                        write(p, o, by_re - partial[1, o])
                    else:
                        write(p - freqs, o, partial[0, o] - by_im)
                        write(p, o, by_re + partial[1, o])


def image_row(freqs, load):
    total = None
    for k in range(2 * freqs):
        term = load(k) * load(2 * freqs + k)
        total = term if total is None else total + term
    return total


def power_of(ref, stride):
    def power(p, m, row):
        at = (p * stride + row) * 8
        at = at if isinstance(at, int) else pl.multiple_of(at, 8)
        return ref[pl.ds(at, 8), pl.ds(128 * (m - 1), 128)]

    return power


def rows_kernel(
    source, receiver, y_matrix, rows_out, powers_out, flat, left
):
    freqs, stored = source.shape[1:3]
    count = 4 * freqs
    row_tiles = stored // 8
    for plane, load in enumerate(planes_of(source, receiver)):
        to_rows(flat.at[plane], load, row_tiles)
        for r in range(stored):
            rows_out[plane, r] = row_of(flat.at[plane], r)
    for plane in range(count):
        split_rows(rows_out[plane], left, plane * stored * 8)
    powers_out[...] = multiply(left, count * stored * 8, y_matrix)


def own_kernel(
    frequency, order_table, filter_coeffs, rows_in, powers_in, slow_in, y_matrix,
    behind, weights_out, first_out, later_out,
    middle_out, middle_powers_out, last_out, first_image, last_image,
    left, later_weights, partial,
):
    count, stored = rows_in.shape[:2]
    freqs = count // 4
    for plane in range(count):
        behind[pl.ds(plane * HALO, HALO)] = rows_in[plane, pl.ds(0, HALO)]
    behind[pl.ds(count * HALO, ORDER)] = slow_in[0, pl.ds(0, ORDER)]
    powers = filter_coeffs.shape[0]
    for depth, weights in enumerate((weights_out, later_weights)):
        for freq in range(freqs):
            omega = jnp.full((8, 128), frequency[freq], F32)
            active = [
                jnp.full((8, 128), jnp.where(order_table[depth, freq] >= n, 1.0, 0.0), F32)
                for n in range(ORDER + 1)
            ]
            for c in range(2):
                scale = None
                for j in range(powers):
                    scaled = [filter_coeffs[j, c, n] * active[n] for n in range(ORDER + 1)]
                    for m in range(ORDER + 1):
                        total = None
                        for n in range(m, ORDER + 1):
                            term = scaled[n] * float(SHIFTED[n][m])
                            total = term if total is None else total + term
                        if scale is not None:
                            total = total * scale
                        weights[freq, (m * 2 + c) * powers + j] = total
                    scale = omega if scale is None else scale * omega

    def tables(r, carry):
        for depth, (weights, out) in enumerate(((weights_out, first_out), (later_weights, later_out))):
            for freq in range(freqs):
                def store(part, value):
                    out[freq, part, r] = value

                coefficients(weights, freq, slow_in[depth, r], store)
        return carry

    lax.fori_loop(0, stored, tables, 0, unroll=2)

    inner = stored - 2 * ORDER

    def write_middle(p, o, value):
        middle_out[p, o] = value

    sweep(
        freqs,
        lambda p, o: rows_in[p, o + ORDER],
        power_of(powers_in, stored),
        lambda freq, part, o: first_out[freq, part, o + ORDER],
        write_middle,
        partial,
        inner,
    )
    for o in range(inner):
        first_image[o] = image_row(freqs, lambda p: middle_out[p, o])
    for plane in range(count):
        split_rows(middle_out[plane], left, plane * inner * 8)
    middle_powers_out[...] = multiply(left, count * inner * 8, y_matrix)

    def write_last(p, o, value):
        last_out[p, o] = value

    sweep(
        freqs,
        lambda p, o: middle_out[p, o + ORDER],
        power_of(middle_powers_out, inner),
        lambda freq, part, o: later_out[freq, part, o + HALO],
        write_last,
        partial,
        inner - 2 * ORDER,
    )
    for o in range(inner - 2 * ORDER):
        last_image[o] = image_row(freqs, lambda p: last_out[p, o])


def upper_kernel(
    rows_in, powers_in, slow_in, weights, first_in, later,
    middle_in, middle_powers_in, last_in, first_image, last_image, y_matrix, from_before,
    middle, middle_powers, last, images,
    edges, left, edge_powers, slow, first, partial,
):
    count, stored = rows_in.shape[:2]
    freqs = count // 4
    inner = stored - 2 * ORDER
    tile = lax.axis_index("tile")

    @pl.when(tile == 0)
    def _():
        for p in range(count):
            edges[p, HALO - 1] = jnp.zeros((8, 128), F32)
            for k in range(1, HALO):
                edges[p, HALO - 1 - k] = -rows_in[p, k - 1]
        slow[ORDER - 1] = slow_in[0, 0]
        for k in range(1, ORDER):
            slow[ORDER - 1 - k] = slow_in[0, k - 1]

    @pl.when(tile > 0)
    def _():
        for p in range(count):
            edges[p] = from_before[pl.ds(p * HALO, HALO)]
        slow[...] = from_before[pl.ds(count * HALO, ORDER)]

    for p in range(count):
        split_rows(edges[p], left, p * HALO * 8)
    edge_powers[...] = multiply(left, count * HALO * 8, y_matrix)
    for r in range(ORDER):
        for freq in range(freqs):
            def store(part, value):
                first[freq, part, r] = value

            coefficients(weights, freq, slow[r], store)

    outer = power_of(edge_powers, HALO)
    own = power_of(powers_in, stored)

    def write_middle(p, o, value):
        middle[p, o] = value

    sweep(
        freqs,
        lambda p, o: edges[p, o + ORDER] if o < ORDER else rows_in[p, o - ORDER],
        lambda p, m, row: outer(p, m, row) if row < HALO else own(p, m, row - HALO),
        lambda freq, part, o: (
            first[freq, part, o] if o < ORDER else first_in[freq, part, o - ORDER]
        ),
        write_middle,
        partial,
        2 * ORDER,
    )
    for p in range(count):
        middle[p, pl.ds(2 * ORDER, inner)] = middle_in[p]
        split_rows(middle[p, pl.ds(0, 2 * ORDER)], left, p * HALO * 8)
    edge_powers[...] = multiply(left, count * HALO * 8, y_matrix)
    for p in range(count):
        size = HALO * 8
        middle_powers[pl.ds(p * stored * 8, size), :] = edge_powers[pl.ds(p * size, size), :]
        middle_powers[pl.ds((p * stored + HALO) * 8, inner * 8), :] = middle_powers_in[
            pl.ds(p * inner * 8, inner * 8), :
        ]

    def write_last(p, o, value):
        last[p, o] = value

    sweep(
        freqs,
        lambda p, o: middle[p, o + ORDER],
        power_of(middle_powers, stored),
        lambda freq, part, o: later[freq, part, o],
        write_last,
        partial,
        HALO,
    )
    for p in range(count):
        last[p, pl.ds(HALO, inner - HALO)] = last_in[p]
    images[0, pl.ds(ORDER, inner)] = first_image[...]
    images[1, pl.ds(HALO, inner - HALO)] = last_image[...]
    for k in range(ORDER):
        images[0, k] = image_row(freqs, lambda p: middle[p, k + ORDER])
    for k in range(HALO):
        images[1, k] = image_row(freqs, lambda p: last[p, k])


def lower_kernel(
    aperture, rows_in, powers_in, slow_in, weights, first_in, later,
    middle_in, middle_powers_in, last_in, images_in, y_matrix, from_after,
    image_out, receiver_hbm,
    receiver_out, sems,
    flat, edges, left, edge_powers, slow, first, middle, last, images, partial,
):
    tile = lax.axis_index("tile")
    width = aperture[tile]
    count, stored = rows_in.shape[:2]
    freqs = count // 4
    row_tiles = stored // 8
    inner = stored - 2 * ORDER

    @pl.when(tile == lax.axis_size("tile") - 1)
    def _():
        for p in range(count):
            edges[p, 0] = jnp.zeros((8, 128), F32)
            for k in range(1, HALO):
                edges[p, k] = -rows_in[p, width - k]
        slow[0] = slow_in[0, width - 1]
        for k in range(1, ORDER):
            slow[k] = slow_in[0, width - k]

    @pl.when(tile < lax.axis_size("tile") - 1)
    def _():
        for p in range(count):
            edges[p] = from_after[pl.ds(p * HALO, HALO)]
        slow[...] = from_after[pl.ds(count * HALO, ORDER)]

    for p in range(count):
        split_rows(edges[p], left, p * HALO * 8)
    edge_powers[...] = multiply(left, count * HALO * 8, y_matrix)
    for r in range(ORDER):
        for freq in range(freqs):
            def store(part, value):
                first[freq, part, r] = value

            coefficients(weights, freq, slow[r], store)

    outer = power_of(edge_powers, HALO)
    own = power_of(powers_in, stored)
    done = power_of(middle_powers_in, stored)

    def write_middle(p, o, value):
        middle[p, o] = value

    sweep(
        freqs,
        lambda p, o: rows_in[p, o + width - ORDER] if o < ORDER else edges[p, o - ORDER],
        lambda p, m, row: (
            own(p, m, row + width - HALO) if row < HALO else outer(p, m, row - HALO)
        ),
        lambda freq, part, o: (
            first_in[freq, part, o + width - ORDER] if o < ORDER else first[freq, part, o - ORDER]
        ),
        write_middle,
        partial,
        2 * ORDER,
    )
    for p in range(count):
        split_rows(middle[p], left, p * HALO * 8)
    edge_powers[...] = multiply(left, count * HALO * 8, y_matrix)

    def write_last(p, o, value):
        last[p, o + width - HALO] = value

    for p in range(2 * freqs, count):
        last[p, pl.ds(0, inner)] = last_in[p]
    images[:, pl.ds(0, stored - ORDER)] = images_in[...]

    def finish(which):
        sweep(
            freqs,
            lambda p, o: middle_in[p, o + width - ORDER] if o < ORDER else middle[p, o - ORDER],
            lambda p, m, row: (
                done(p, m, row + width - HALO) if row < HALO else outer(p, m, row - HALO)
            ),
            lambda freq, part, o: later[freq, part, o + width - HALO],
            write_last,
            partial,
            HALO,
            which,
        )

    def put(slot, load_row, store_tile):
        for r in range(stored):
            at = (r // 8) * 64 + r % 8
            flat[slot, pl.ds(at, 8, stride=8), :] = jnp.where(r < width, load_row(r), 0.0)
        for i in range(row_tiles):
            for j in range(8):
                store_tile(i, j, flat[slot, pl.ds((i * 8 + j) * 8, 8), :])

    finish((1,))
    sent = []
    for part in range(2):
        for freq in range(freqs):
            def store_receiver(i, j, value):
                receiver_out[part, freq, pl.ds(8 * i, 8), pl.ds(128 * j, 128)] = value

            p = (2 + part) * freqs + freq
            put(NDEPTH + part * freqs + freq, lambda r: last[p, r], store_receiver)
            sent.append(
                pltpu.make_async_copy(
                    receiver_out.at[part, freq],
                    receiver_hbm.at[part, freq],
                    sems.at[part * freqs + freq],
                )
            )
            sent[-1].start()
    finish((0,))

    for k in range(ORDER):
        images[0, width - ORDER + k] = image_row(freqs, lambda p: middle[p, k])
    for k in range(HALO):
        images[1, width - HALO + k] = image_row(freqs, lambda p: last[p, width - HALO + k])
    columns = image_out.shape[3]
    for depth in range(NDEPTH):
        def store_image(i, j, value):
            image_out[
                128 * j // columns, depth, pl.ds(8 * i, 8), pl.ds(128 * j % columns, 128)
            ] = value

        put(depth, lambda r: images[depth, r], store_image)
    for copy in sent:
        copy.wait()


def passed_along(value, axis, steps):
    count = lax.axis_size(axis)
    initial, last = (max(0, -steps), min(count, count - steps))
    return lax.ppermute(value, axis, [(source, source + steps) for source in range(initial, last)])


def kernel(body, out_shape, in_specs, scratch, name, cost=1000):
    return pl.pallas_call(
        body,
        out_shape=out_shape,
        in_specs=in_specs,
        out_specs=(VMEM,) * len(out_shape),
        scratch_shapes=scratch,
        compiler_params=pltpu.CompilerParams(vmem_limit_bytes=24 << 20),
        cost_estimate=pl.CostEstimate(flops=cost, bytes_accessed=cost, transcendentals=0),
        name=name,
    )


def shards(source_field, receiver_field, slowness, frequency, order_table, filter_coeffs, aperture):
    freqs, stored = source_field.shape[1:3]
    count = 4 * freqs
    parts = 2 * (ORDER + 1)
    inner = stored - 2 * ORDER
    wide = ORDER * 128

    def shape(*dims):
        return jax.ShapeDtypeStruct(dims, F32)

    def rows(*lead):
        return shape(*lead, 8, 128)

    def same(value):
        return pltpu.VMEM(value.shape, value.dtype)

    def scratch(*lead):
        return same(rows(*lead))

    planes = lax.all_gather(slowness, "freq", axis=0)
    halo = rows(count * HALO + ORDER)
    flat = pltpu.VMEM((stored * 8, 128), F32)
    (slow,) = kernel(
        slow_kernel,
        (rows(NDEPTH, stored),),
        [VMEM],
        [pltpu.VMEM((NDEPTH, stored * 8, 128), F32)],
        "slow",
        1 << 30,
    )(planes)
    (ahead,) = kernel(
        ahead_kernel, (halo,), [SMEM] + [VMEM] * 3, [flat] * count, "ahead"
    )(aperture, source_field, receiver_field, slow)
    from_before = passed_along(ahead, "tile", 1)

    y_matrix = jnp.asarray(y_weights(), BF16)
    own_rows, own_powers = kernel(
        rows_kernel,
        (rows(count, stored), shape(count * stored * 8, wide)),
        [VMEM] * 3,
        [
            pltpu.VMEM((count, stored * 8, 128), F32),
            pltpu.VMEM((count * stored * 8, 512), BF16),
        ],
        "rows",
    )(source_field, receiver_field, y_matrix)

    coeffs = jnp.transpose(filter_coeffs, (2, 0, 1))
    terms = parts * coeffs.shape[0]
    behind, weights, first, later, *inside = kernel(
        own_kernel,
        (
            halo,
            rows(freqs, terms),
            rows(freqs, parts, stored),
            rows(freqs, parts, stored),
            rows(count, inner),
            shape(count * inner * 8, wide),
            rows(count, inner - HALO),
            rows(inner),
            rows(inner - HALO),
        ),
        [SMEM] * 3 + [VMEM] * 4,
        [
            pltpu.VMEM((count * inner * 8, 512), BF16),
            scratch(freqs, terms),
            scratch(2, inner),
        ],
        "own",
    )(frequency, order_table, coeffs, own_rows, own_powers, slow, y_matrix)
    from_after = passed_along(behind, "tile", -1)
    edge = [
        scratch(count, HALO),
        pltpu.VMEM((count * HALO * 8, 512), BF16),
        pltpu.VMEM((count * HALO * 8, wide), F32),
        scratch(ORDER),
        scratch(freqs, parts, ORDER),
    ]
    tables = (own_rows, own_powers, slow, weights, first, later)
    upper = kernel(
        upper_kernel,
        (
            rows(count, stored),
            shape(count * stored * 8, wide),
            rows(count, inner),
            rows(NDEPTH, stored - ORDER),
        ),
        [VMEM] * (len(tables) + len(inside) + 2),
        edge + [scratch(2, HALO)],
        "upper",
    )(*tables, *inside, y_matrix, from_before)
    image_parts, receiver_out = pl.pallas_call(
        lower_kernel,
        out_shape=(
            shape(lax.axis_size("freq"), *slowness.shape),
            shape(*receiver_field.shape),
        ),
        in_specs=[SMEM] + [VMEM] * (len(tables) + len(upper) + 2),
        out_specs=(VMEM, pl.BlockSpec(memory_space=pl.ANY)),
        scratch_shapes=[
            same(receiver_field),
            pltpu.SemaphoreType.DMA((2 * freqs,)),
            pltpu.VMEM((NDEPTH + 2 * freqs, stored * 8, 128), F32),
            *edge,
            scratch(count, HALO),
            scratch(count, stored),
            scratch(NDEPTH, stored),
            scratch(2, HALO),
        ],
        compiler_params=pltpu.CompilerParams(vmem_limit_bytes=24 << 20),
        cost_estimate=pl.CostEstimate(flops=1000, bytes_accessed=1000, transcendentals=0),
        name="lower",
    )(aperture, *tables, *upper, y_matrix, from_after)
    exchanged = lax.all_to_all(image_parts, "freq", 0, 0)
    return jnp.sum(exchanged, axis=0), receiver_out


def solution(mesh):
    placed = (
        P(None, "freq", "tile", None),
        P(None, "freq", "tile", None),
        P(None, "tile", "freq"),
        P("freq"),
        P(None, "freq"),
        P(),
        P(),
    )
    return jax.shard_map(
        shards,
        mesh=mesh,
        in_specs=placed,
        out_specs=(P(None, "tile", "freq"), P(None, "freq", "tile", None)),
        check_vma=False,
    )
```

```python
from math import comb

import jax
import jax.numpy as jnp
import numpy as np
from jax import lax
from jax.experimental import pallas as pl
from jax.experimental.pallas import tpu as pltpu
from jax.sharding import PartitionSpec as P

ORDER = 4
NDEPTH = 2
HALO = ORDER * NDEPTH
F32 = jnp.float32
BF16 = jnp.bfloat16
VMEM = pl.BlockSpec(memory_space=pltpu.VMEM)
SMEM = pl.BlockSpec(memory_space=pltpu.SMEM)

SHIFTED = ((1,), (-1, 2), (1, -8, 8), (-1, 18, -48, 32), (1, -32, 160, -256, 128))


def y_weights():
    out = np.zeros((256, ORDER * 128), np.float32)

    def add(k, column, sign):
        for m in range(1, ORDER + 1):
            for lane in range(max(0, column - m), min(128, column + m + 1)):
                out[k, (m - 1) * 128 + lane] += sign * comb(2 * m, m + lane - column) / 16.0**m

    for lane in range(128):
        add(lane, lane, 1)
    for lane in range(4):
        add(128 + lane, 128 + lane, 1)
        add(128 + 124 + lane, lane - 4, 1)
    for k in range(3):
        add(128 + 8 + k, -2 - k, -1)
        add(128 + 5 + k, 131 - k, -1)
    return out


def seam(values):
    lane = lax.broadcasted_iota(jnp.int32, (1, 8, 128), 2)
    sub = lax.broadcasted_iota(jnp.int32, (1, 8, 128), 1)
    inner = ((lane < 4) & (sub < 7)) | ((lane >= 124) & (sub > 0))
    edge = ((sub == 0) & (lane >= 8) & (lane <= 10)) | ((sub == 7) & (lane >= 5) & (lane <= 7))
    beside = jnp.where(lane < 64, pltpu.roll(values, 7, 1), pltpu.roll(values, 1, 1))
    return jnp.where(inner, beside, jnp.where(edge, pltpu.roll(values, 8, 2), 0.0))


def split_rows(values, left, at):
    rows = values.shape[0]
    for column, x in enumerate((values, seam(values))):
        x = x.reshape(rows * 8, 128)
        high = x.astype(BF16)
        left[pl.ds(at, rows * 8), pl.ds(128 * column, 128)] = high
        left[pl.ds(at, rows * 8), pl.ds(256 + 128 * column, 128)] = (x - high.astype(F32)).astype(BF16)


def multiply(left, rows, y_matrix):
    matrix = y_matrix[...]
    right = jnp.concatenate([matrix, matrix], axis=0)
    return jnp.dot(left[pl.ds(0, rows), :], right, preferred_element_type=F32)


def to_rows(flat, load_tile, row_tiles):
    for i in range(row_tiles):
        for j in range(8):
            flat[pl.ds((i * 8 + j) * 8, 8), :] = load_tile(i, j)


def row_of(flat, row):
    start = (row // 8) * 64 + row % 8
    return flat[pl.ds(start, 8, stride=8), :]


def planes_of(source, receiver):
    def loader(field, part, freq):
        return lambda i, j: field[part, freq, pl.ds(8 * i, 8), pl.ds(128 * j, 128)]

    return [
        loader(field, part, freq)
        for field in (source, receiver)
        for part in range(2)
        for freq in range(source.shape[1])
    ]


def slow_tile(planes, depth):
    columns = planes.shape[3]
    return lambda i, j: planes[
        128 * j // columns, depth, pl.ds(8 * i, 8), pl.ds(128 * j % columns, 128)
    ]


def slow_kernel(planes, out, flat):
    row_tiles = planes.shape[2] // 8
    for depth in range(NDEPTH):
        to_rows(flat.at[depth], slow_tile(planes, depth), row_tiles)
        for r in range(planes.shape[2]):
            out[depth, r] = row_of(flat.at[depth], r)


def ahead_kernel(aperture, source, receiver, slow, ahead, *flats):
    width = aperture[lax.axis_index("tile")]
    row_tiles = source.shape[2] // 8
    for plane, load in enumerate(planes_of(source, receiver)):
        to_rows(flats[plane], load, row_tiles)
        for k in range(HALO):
            ahead[plane * HALO + k] = row_of(flats[plane], width - HALO + k)
    end = 4 * source.shape[1] * HALO
    ahead[pl.ds(end, ORDER)] = slow[0, pl.ds(width - ORDER, ORDER)]


def coefficients(weights, freq, slow_row, store):
    powers = weights.shape[1] // (2 * (ORDER + 1))
    for part in range(2 * (ORDER + 1)):
        value = weights[freq, part * powers + powers - 1]
        for power in range(powers - 2, -1, -1):
            value = value * slow_row + weights[freq, part * powers + power]
        store(part, value)


def sweep(freqs, fields, power, coefficient, write, partial, rows, which=(0, 1)):
    def feed(held, value):
        kept = []
        for last in held:
            kept.append(value)
            value = value + last
        return kept, value

    for freq in range(freqs):
        for field in which:
            for part in range(2):
                p = (2 * field + part) * freqs + freq
                held = []
                for m in range(1, ORDER + 1):
                    chain = []
                    for k in range(2 * m):
                        value = power(p, m, ORDER - m + k)
                        chain, value = feed(chain, value)
                        chain.append(value)
                    held.append(chain)
                for o in range(rows):
                    kept, by_re, by_im = [], None, None
                    for m in range(ORDER + 1):
                        if m == 0:
                            value = fields(p, o)
                        else:
                            chain, value = feed(held[m - 1], power(p, m, o + ORDER + m))
                            kept.append(chain)
                        re = coefficient(freq, 2 * m, o) * value
                        im = coefficient(freq, 2 * m + 1, o) * value
                        by_re = re if by_re is None else by_re + re
                        by_im = im if by_im is None else by_im + im
                    held = kept
                    if part == 0:
                        partial[0, o] = by_re
                        partial[1, o] = by_im
                    elif field == 0:
                        write(p - freqs, o, partial[0, o] + by_im)
                        write(p, o, by_re - partial[1, o])
                    else:
                        write(p - freqs, o, partial[0, o] - by_im)
                        write(p, o, by_re + partial[1, o])


def image_row(freqs, load):
    total = None
    for k in range(2 * freqs):
        term = load(k) * load(2 * freqs + k)
        total = term if total is None else total + term
    return total


def power_of(ref, stride):
    def power(p, m, row):
        at = (p * stride + row) * 8
        at = at if isinstance(at, int) else pl.multiple_of(at, 8)
        return ref[pl.ds(at, 8), pl.ds(128 * (m - 1), 128)]

    return power


def rows_kernel(
    frequency, order_table, filter_coeffs, source, receiver, slow, y_matrix,
    behind, rows_out, powers_out, weights_out, first_out, later_out,
    flat, left, later_weights,
):
    powers = filter_coeffs.shape[0]
    freqs, stored = source.shape[1:3]
    count = 4 * freqs
    row_tiles = stored // 8
    for plane, load in enumerate(planes_of(source, receiver)):
        to_rows(flat.at[plane], load, row_tiles)
        for r in range(stored):
            rows_out[plane, r] = row_of(flat.at[plane], r)
    for plane in range(count):
        behind[pl.ds(plane * HALO, HALO)] = rows_out[plane, pl.ds(0, HALO)]
    behind[pl.ds(count * HALO, ORDER)] = slow[0, pl.ds(0, ORDER)]
    for plane in range(count):
        split_rows(rows_out[plane], left, plane * stored * 8)
    powers_out[...] = multiply(left, count * stored * 8, y_matrix)

    for depth, weights in enumerate((weights_out, later_weights)):
        for freq in range(freqs):
            omega = jnp.full((8, 128), frequency[freq], F32)
            active = [
                jnp.full((8, 128), jnp.where(order_table[depth, freq] >= n, 1.0, 0.0), F32)
                for n in range(ORDER + 1)
            ]
            for c in range(2):
                scale = None
                for j in range(powers):
                    scaled = [filter_coeffs[j, c, n] * active[n] for n in range(ORDER + 1)]
                    for m in range(ORDER + 1):
                        total = None
                        for n in range(m, ORDER + 1):
                            term = scaled[n] * float(SHIFTED[n][m])
                            total = term if total is None else total + term
                        if scale is not None:
                            total = total * scale
                        weights[freq, (m * 2 + c) * powers + j] = total
                    scale = omega if scale is None else scale * omega

    def tables(r, carry):
        for depth, (weights, out) in enumerate(((weights_out, first_out), (later_weights, later_out))):
            for freq in range(freqs):
                def store(part, value):
                    out[freq, part, r] = value

                coefficients(weights, freq, slow[depth, r], store)
        return carry

    lax.fori_loop(0, stored, tables, 0, unroll=2)


def own_kernel(
    rows_in, powers_in, first_in, later_in, y_matrix,
    middle_out, middle_powers_out, last_out, first_image, last_image,
    left, partial,
):
    count, stored = rows_in.shape[:2]
    freqs = count // 4
    inner = stored - 2 * ORDER

    def write_middle(p, o, value):
        middle_out[p, o] = value

    sweep(
        freqs,
        lambda p, o: rows_in[p, o + ORDER],
        power_of(powers_in, stored),
        lambda freq, part, o: first_in[freq, part, o + ORDER],
        write_middle,
        partial,
        inner,
    )
    for o in range(inner):
        first_image[o] = image_row(freqs, lambda p: middle_out[p, o])
    for plane in range(count):
        split_rows(middle_out[plane], left, plane * inner * 8)
    middle_powers_out[...] = multiply(left, count * inner * 8, y_matrix)

    def write_last(p, o, value):
        last_out[p, o] = value

    sweep(
        freqs,
        lambda p, o: middle_out[p, o + ORDER],
        power_of(middle_powers_out, inner),
        lambda freq, part, o: later_in[freq, part, o + HALO],
        write_last,
        partial,
        inner - 2 * ORDER,
    )
    for o in range(inner - 2 * ORDER):
        last_image[o] = image_row(freqs, lambda p: last_out[p, o])


def upper_kernel(
    rows_in, powers_in, slow_in, weights, first_in, later,
    middle_in, middle_powers_in, last_in, first_image, last_image, y_matrix, from_before,
    middle, middle_powers, last, images,
    edges, left, edge_powers, slow, first, partial,
):
    count, stored = rows_in.shape[:2]
    freqs = count // 4
    inner = stored - 2 * ORDER
    tile = lax.axis_index("tile")

    @pl.when(tile == 0)
    def _():
        for p in range(count):
            edges[p, HALO - 1] = jnp.zeros((8, 128), F32)
            for k in range(1, HALO):
                edges[p, HALO - 1 - k] = -rows_in[p, k - 1]
        slow[ORDER - 1] = slow_in[0, 0]
        for k in range(1, ORDER):
            slow[ORDER - 1 - k] = slow_in[0, k - 1]

    @pl.when(tile > 0)
    def _():
        for p in range(count):
            edges[p] = from_before[pl.ds(p * HALO, HALO)]
        slow[...] = from_before[pl.ds(count * HALO, ORDER)]

    for p in range(count):
        split_rows(edges[p], left, p * HALO * 8)
    edge_powers[...] = multiply(left, count * HALO * 8, y_matrix)
    for r in range(ORDER):
        for freq in range(freqs):
            def store(part, value):
                first[freq, part, r] = value

            coefficients(weights, freq, slow[r], store)

    outer = power_of(edge_powers, HALO)
    own = power_of(powers_in, stored)

    def write_middle(p, o, value):
        middle[p, o] = value

    sweep(
        freqs,
        lambda p, o: edges[p, o + ORDER] if o < ORDER else rows_in[p, o - ORDER],
        lambda p, m, row: outer(p, m, row) if row < HALO else own(p, m, row - HALO),
        lambda freq, part, o: (
            first[freq, part, o] if o < ORDER else first_in[freq, part, o - ORDER]
        ),
        write_middle,
        partial,
        2 * ORDER,
    )
    for p in range(count):
        middle[p, pl.ds(2 * ORDER, inner)] = middle_in[p]
        split_rows(middle[p, pl.ds(0, 2 * ORDER)], left, p * HALO * 8)
    edge_powers[...] = multiply(left, count * HALO * 8, y_matrix)
    for p in range(count):
        size = HALO * 8
        middle_powers[pl.ds(p * stored * 8, size), :] = edge_powers[pl.ds(p * size, size), :]
        middle_powers[pl.ds((p * stored + HALO) * 8, inner * 8), :] = middle_powers_in[
            pl.ds(p * inner * 8, inner * 8), :
        ]

    def write_last(p, o, value):
        last[p, o] = value

    sweep(
        freqs,
        lambda p, o: middle[p, o + ORDER],
        power_of(middle_powers, stored),
        lambda freq, part, o: later[freq, part, o],
        write_last,
        partial,
        HALO,
    )
    for p in range(count):
        last[p, pl.ds(HALO, inner - HALO)] = last_in[p]
    images[0, pl.ds(ORDER, inner)] = first_image[...]
    images[1, pl.ds(HALO, inner - HALO)] = last_image[...]
    for k in range(ORDER):
        images[0, k] = image_row(freqs, lambda p: middle[p, k + ORDER])
    for k in range(HALO):
        images[1, k] = image_row(freqs, lambda p: last[p, k])


def lower_kernel(
    aperture, rows_in, powers_in, slow_in, weights, first_in, later,
    middle_in, middle_powers_in, last_in, images_in, y_matrix, from_after,
    image_out, receiver_hbm,
    receiver_out, sems,
    flat, edges, left, edge_powers, slow, first, middle, last, images, partial,
):
    tile = lax.axis_index("tile")
    width = aperture[tile]
    count, stored = rows_in.shape[:2]
    freqs = count // 4
    row_tiles = stored // 8
    inner = stored - 2 * ORDER

    @pl.when(tile == lax.axis_size("tile") - 1)
    def _():
        for p in range(count):
            edges[p, 0] = jnp.zeros((8, 128), F32)
            for k in range(1, HALO):
                edges[p, k] = -rows_in[p, width - k]
        slow[0] = slow_in[0, width - 1]
        for k in range(1, ORDER):
            slow[k] = slow_in[0, width - k]

    @pl.when(tile < lax.axis_size("tile") - 1)
    def _():
        for p in range(count):
            edges[p] = from_after[pl.ds(p * HALO, HALO)]
        slow[...] = from_after[pl.ds(count * HALO, ORDER)]

    for p in range(count):
        split_rows(edges[p], left, p * HALO * 8)
    edge_powers[...] = multiply(left, count * HALO * 8, y_matrix)
    for r in range(ORDER):
        for freq in range(freqs):
            def store(part, value):
                first[freq, part, r] = value

            coefficients(weights, freq, slow[r], store)

    outer = power_of(edge_powers, HALO)
    own = power_of(powers_in, stored)
    done = power_of(middle_powers_in, stored)

    def write_middle(p, o, value):
        middle[p, o] = value

    sweep(
        freqs,
        lambda p, o: rows_in[p, o + width - ORDER] if o < ORDER else edges[p, o - ORDER],
        lambda p, m, row: (
            own(p, m, row + width - HALO) if row < HALO else outer(p, m, row - HALO)
        ),
        lambda freq, part, o: (
            first_in[freq, part, o + width - ORDER] if o < ORDER else first[freq, part, o - ORDER]
        ),
        write_middle,
        partial,
        2 * ORDER,
    )
    for p in range(count):
        split_rows(middle[p], left, p * HALO * 8)
    edge_powers[...] = multiply(left, count * HALO * 8, y_matrix)

    def write_last(p, o, value):
        last[p, o + width - HALO] = value

    for p in range(2 * freqs, count):
        last[p, pl.ds(0, inner)] = last_in[p]
    images[:, pl.ds(0, stored - ORDER)] = images_in[...]

    def finish(which):
        sweep(
            freqs,
            lambda p, o: middle_in[p, o + width - ORDER] if o < ORDER else middle[p, o - ORDER],
            lambda p, m, row: (
                done(p, m, row + width - HALO) if row < HALO else outer(p, m, row - HALO)
            ),
            lambda freq, part, o: later[freq, part, o + width - HALO],
            write_last,
            partial,
            HALO,
            which,
        )

    def put(slot, load_row, store_tile):
        for r in range(stored):
            at = (r // 8) * 64 + r % 8
            flat[slot, pl.ds(at, 8, stride=8), :] = jnp.where(r < width, load_row(r), 0.0)
        for i in range(row_tiles):
            for j in range(8):
                store_tile(i, j, flat[slot, pl.ds((i * 8 + j) * 8, 8), :])

    finish((1,))
    sent = []
    for part in range(2):
        for freq in range(freqs):
            def store_receiver(i, j, value):
                receiver_out[part, freq, pl.ds(8 * i, 8), pl.ds(128 * j, 128)] = value

            p = (2 + part) * freqs + freq
            put(NDEPTH + part * freqs + freq, lambda r: last[p, r], store_receiver)
            sent.append(
                pltpu.make_async_copy(
                    receiver_out.at[part, freq],
                    receiver_hbm.at[part, freq],
                    sems.at[part * freqs + freq],
                )
            )
            sent[-1].start()
    finish((0,))

    for k in range(ORDER):
        images[0, width - ORDER + k] = image_row(freqs, lambda p: middle[p, k])
    for k in range(HALO):
        images[1, width - HALO + k] = image_row(freqs, lambda p: last[p, width - HALO + k])
    columns = image_out.shape[3]
    for depth in range(NDEPTH):
        def store_image(i, j, value):
            image_out[
                128 * j // columns, depth, pl.ds(8 * i, 8), pl.ds(128 * j % columns, 128)
            ] = value

        put(depth, lambda r: images[depth, r], store_image)
    for copy in sent:
        copy.wait()


def passed_along(value, axis, steps):
    count = lax.axis_size(axis)
    initial, last = (max(0, -steps), min(count, count - steps))
    return lax.ppermute(value, axis, [(source, source + steps) for source in range(initial, last)])


def kernel(body, out_shape, in_specs, scratch, name, cost=1000):
    return pl.pallas_call(
        body,
        out_shape=out_shape,
        in_specs=in_specs,
        out_specs=(VMEM,) * len(out_shape),
        scratch_shapes=scratch,
        compiler_params=pltpu.CompilerParams(vmem_limit_bytes=24 << 20),
        cost_estimate=pl.CostEstimate(flops=cost, bytes_accessed=cost, transcendentals=0),
        name=name,
    )


def shards(source_field, receiver_field, slowness, frequency, order_table, filter_coeffs, aperture):
    freqs, stored = source_field.shape[1:3]
    count = 4 * freqs
    parts = 2 * (ORDER + 1)
    inner = stored - 2 * ORDER
    wide = ORDER * 128

    def shape(*dims):
        return jax.ShapeDtypeStruct(dims, F32)

    def rows(*lead):
        return shape(*lead, 8, 128)

    def same(value):
        return pltpu.VMEM(value.shape, value.dtype)

    def scratch(*lead):
        return same(rows(*lead))

    planes = lax.all_gather(slowness, "freq", axis=0)
    halo = rows(count * HALO + ORDER)
    flat = pltpu.VMEM((stored * 8, 128), F32)
    (slow,) = kernel(
        slow_kernel,
        (rows(NDEPTH, stored),),
        [VMEM],
        [pltpu.VMEM((NDEPTH, stored * 8, 128), F32)],
        "slow",
        1 << 30,
    )(planes)
    (ahead,) = kernel(
        ahead_kernel, (halo,), [SMEM] + [VMEM] * 3, [flat] * count, "ahead"
    )(aperture, source_field, receiver_field, slow)
    from_before = passed_along(ahead, "tile", 1)

    y_matrix = jnp.asarray(y_weights(), BF16)
    coeffs = jnp.transpose(filter_coeffs, (2, 0, 1))
    terms = parts * coeffs.shape[0]
    behind, own_rows, own_powers, weights, first, later = kernel(
        rows_kernel,
        (
            halo,
            rows(count, stored),
            shape(count * stored * 8, wide),
            rows(freqs, terms),
            rows(freqs, parts, stored),
            rows(freqs, parts, stored),
        ),
        [SMEM] * 3 + [VMEM] * 4,
        [
            pltpu.VMEM((count, stored * 8, 128), F32),
            pltpu.VMEM((count * stored * 8, 512), BF16),
            scratch(freqs, terms),
        ],
        "rows",
    )(frequency, order_table, coeffs, source_field, receiver_field, slow, y_matrix)
    from_after = passed_along(behind, "tile", -1)

    inside = kernel(
        own_kernel,
        (
            rows(count, inner),
            shape(count * inner * 8, wide),
            rows(count, inner - HALO),
            rows(inner),
            rows(inner - HALO),
        ),
        [VMEM] * 5,
        [pltpu.VMEM((count * inner * 8, 512), BF16), scratch(2, inner)],
        "own",
    )(own_rows, own_powers, first, later, y_matrix)
    edge = [
        scratch(count, HALO),
        pltpu.VMEM((count * HALO * 8, 512), BF16),
        pltpu.VMEM((count * HALO * 8, wide), F32),
        scratch(ORDER),
        scratch(freqs, parts, ORDER),
    ]
    tables = (own_rows, own_powers, slow, weights, first, later)
    upper = kernel(
        upper_kernel,
        (
            rows(count, stored),
            shape(count * stored * 8, wide),
            rows(count, inner),
            rows(NDEPTH, stored - ORDER),
        ),
        [VMEM] * (len(tables) + len(inside) + 2),
        edge + [scratch(2, HALO)],
        "upper",
    )(*tables, *inside, y_matrix, from_before)
    image_parts, receiver_out = pl.pallas_call(
        lower_kernel,
        out_shape=(
            shape(lax.axis_size("freq"), *slowness.shape),
            shape(*receiver_field.shape),
        ),
        in_specs=[SMEM] + [VMEM] * (len(tables) + len(upper) + 2),
        out_specs=(VMEM, pl.BlockSpec(memory_space=pl.ANY)),
        scratch_shapes=[
            same(receiver_field),
            pltpu.SemaphoreType.DMA((2 * freqs,)),
            pltpu.VMEM((NDEPTH + 2 * freqs, stored * 8, 128), F32),
            *edge,
            scratch(count, HALO),
            scratch(count, stored),
            scratch(NDEPTH, stored),
            scratch(2, HALO),
        ],
        compiler_params=pltpu.CompilerParams(vmem_limit_bytes=24 << 20),
        cost_estimate=pl.CostEstimate(flops=1000, bytes_accessed=1000, transcendentals=0),
        name="lower",
    )(aperture, *tables, *upper, y_matrix, from_after)
    exchanged = lax.all_to_all(image_parts, "freq", 0, 0)
    return jnp.sum(exchanged, axis=0), receiver_out


def solution(mesh):
    placed = (
        P(None, "freq", "tile", None),
        P(None, "freq", "tile", None),
        P(None, "tile", "freq"),
        P("freq"),
        P(None, "freq"),
        P(),
        P(),
    )
    return jax.shard_map(
        shards,
        mesh=mesh,
        in_specs=placed,
        out_specs=(P(None, "tile", "freq"), P(None, "freq", "tile", None)),
        check_vma=False,
    )
```

```python
import functools
from math import comb

import jax
import jax.numpy as jnp
import numpy as np
from jax import lax
from jax.experimental import pallas as pl
from jax.experimental.pallas import tpu as pltpu
from jax.sharding import PartitionSpec as P

ORDER = 4
NDEPTH = 2
HALO = ORDER * NDEPTH
F32 = jnp.float32
BF16 = jnp.bfloat16
VMEM = pl.BlockSpec(memory_space=pltpu.VMEM)
SMEM = pl.BlockSpec(memory_space=pltpu.SMEM)

SHIFTED = ((1,), (-1, 2), (1, -8, 8), (-1, 18, -48, 32), (1, -32, 160, -256, 128))


def y_weights():
    out = np.zeros((256, ORDER * 128), np.float32)

    def add(k, column, sign):
        for m in range(1, ORDER + 1):
            for lane in range(max(0, column - m), min(128, column + m + 1)):
                out[k, (m - 1) * 128 + lane] += sign * comb(2 * m, m + lane - column) / 16.0**m

    for lane in range(128):
        add(lane, lane, 1)
    for lane in range(4):
        add(128 + lane, 128 + lane, 1)
        add(128 + 124 + lane, lane - 4, 1)
    for k in range(3):
        add(128 + 8 + k, -2 - k, -1)
        add(128 + 5 + k, 131 - k, -1)
    return out


def seam(values):
    lane = lax.broadcasted_iota(jnp.int32, (1, 8, 128), 2)
    sub = lax.broadcasted_iota(jnp.int32, (1, 8, 128), 1)
    inner = ((lane < 4) & (sub < 7)) | ((lane >= 124) & (sub > 0))
    edge = ((sub == 0) & (lane >= 8) & (lane <= 10)) | ((sub == 7) & (lane >= 5) & (lane <= 7))
    beside = jnp.where(lane < 64, pltpu.roll(values, 7, 1), pltpu.roll(values, 1, 1))
    return jnp.where(inner, beside, jnp.where(edge, pltpu.roll(values, 8, 2), 0.0))


def split_rows(values, left, at):
    rows = values.shape[0]
    for column, x in enumerate((values, seam(values))):
        x = x.reshape(rows * 8, 128)
        high = x.astype(BF16)
        left[pl.ds(at, rows * 8), pl.ds(128 * column, 128)] = high
        left[pl.ds(at, rows * 8), pl.ds(256 + 128 * column, 128)] = (x - high.astype(F32)).astype(BF16)


def multiply(left, rows, y_matrix):
    matrix = y_matrix[...]
    right = jnp.concatenate([matrix, matrix], axis=0)
    return jnp.dot(left[pl.ds(0, rows), :], right, preferred_element_type=F32)


def to_rows(flat, load_tile, row_tiles):
    for i in range(row_tiles):
        for j in range(8):
            flat[pl.ds((i * 8 + j) * 8, 8), :] = load_tile(i, j)


def row_of(flat, row):
    start = (row // 8) * 64 + row % 8
    return flat[pl.ds(start, 8, stride=8), :]


def planes_of(source, receiver):
    def loader(field, part, freq):
        return lambda i, j: field[part, freq, pl.ds(8 * i, 8), pl.ds(128 * j, 128)]

    return [
        loader(field, part, freq)
        for field in (source, receiver)
        for part in range(2)
        for freq in range(source.shape[1])
    ]


def slow_tile(planes, depth):
    columns = planes.shape[3]
    return lambda i, j: planes[
        128 * j // columns, depth, pl.ds(8 * i, 8), pl.ds(128 * j % columns, 128)
    ]


def slow_kernel(planes, out, flat):
    row_tiles = planes.shape[2] // 8
    for depth in range(NDEPTH):
        to_rows(flat.at[depth], slow_tile(planes, depth), row_tiles)
        for r in range(planes.shape[2]):
            out[depth, r] = row_of(flat.at[depth], r)


def ahead_kernel(aperture, source, receiver, slow, ahead, *flats):
    width = aperture[lax.axis_index("tile")]
    row_tiles = source.shape[2] // 8
    for plane, load in enumerate(planes_of(source, receiver)):
        to_rows(flats[plane], load, row_tiles)
        for k in range(HALO):
            ahead[plane * HALO + k] = row_of(flats[plane], width - HALO + k)
    end = 4 * source.shape[1] * HALO
    ahead[pl.ds(end, ORDER)] = slow[0, pl.ds(width - ORDER, ORDER)]


def coefficients(weights, freq, slow_row, store):
    powers = weights.shape[1] // (2 * (ORDER + 1))
    for part in range(2 * (ORDER + 1)):
        value = weights[freq, part * powers + powers - 1]
        for power in range(powers - 2, -1, -1):
            value = value * slow_row + weights[freq, part * powers + power]
        store(part, value)


def sweep(freqs, fields, power, coefficient, write, partial, rows, which=(0, 1)):
    def feed(held, value):
        kept = []
        for last in held:
            kept.append(value)
            value = value + last
        return kept, value

    for freq in range(freqs):
        for field in which:
            for part in range(2):
                p = (2 * field + part) * freqs + freq
                held = []
                for m in range(1, ORDER + 1):
                    chain = []
                    for k in range(2 * m):
                        value = power(p, m, ORDER - m + k)
                        chain, value = feed(chain, value)
                        chain.append(value)
                    held.append(chain)
                for o in range(rows):
                    kept, by_re, by_im = [], None, None
                    for m in range(ORDER + 1):
                        if m == 0:
                            value = fields(p, o)
                        else:
                            chain, value = feed(held[m - 1], power(p, m, o + ORDER + m))
                            kept.append(chain)
                        re = coefficient(freq, 2 * m, o) * value
                        im = coefficient(freq, 2 * m + 1, o) * value
                        by_re = re if by_re is None else by_re + re
                        by_im = im if by_im is None else by_im + im
                    held = kept
                    if part == 0:
                        partial[0, o] = by_re
                        partial[1, o] = by_im
                    elif field == 0:
                        write(p - freqs, o, partial[0, o] + by_im)
                        write(p, o, by_re - partial[1, o])
                    else:
                        write(p - freqs, o, partial[0, o] - by_im)
                        write(p, o, by_re + partial[1, o])


def image_row(freqs, load):
    total = None
    for k in range(2 * freqs):
        term = load(k) * load(2 * freqs + k)
        total = term if total is None else total + term
    return total


def power_of(ref, stride):
    def power(p, m, row):
        at = (p * stride + row) * 8
        at = at if isinstance(at, int) else pl.multiple_of(at, 8)
        return ref[pl.ds(at, 8), pl.ds(128 * (m - 1), 128)]

    return power


def rows_kernel(
    frequency, order_table, filter_coeffs, source, receiver, slow, y_matrix, *others
):
    powers = filter_coeffs.shape[0]
    behind, others = others[: source.shape[1]], others[source.shape[1] :]
    rows_out, powers_out, weights_out, first_out, later_out, flat, left, later_weights = others
    freqs, stored = source.shape[1:3]
    count = 4 * freqs
    row_tiles = stored // 8
    for plane, load in enumerate(planes_of(source, receiver)):
        to_rows(flat.at[plane], load, row_tiles)
        for r in range(stored):
            rows_out[plane, r] = row_of(flat.at[plane], r)
    for plane in range(count):
        behind[plane % freqs][pl.ds(plane // freqs * HALO, HALO)] = rows_out[plane, pl.ds(0, HALO)]
    behind[0][pl.ds(4 * HALO, ORDER)] = slow[0, pl.ds(0, ORDER)]
    for plane in range(count):
        split_rows(rows_out[plane], left, plane * stored * 8)
    powers_out[...] = multiply(left, count * stored * 8, y_matrix)

    for depth, weights in enumerate((weights_out, later_weights)):
        for freq in range(freqs):
            omega = jnp.full((8, 128), frequency[freq], F32)
            active = [
                jnp.full((8, 128), jnp.where(order_table[depth, freq] >= n, 1.0, 0.0), F32)
                for n in range(ORDER + 1)
            ]
            for c in range(2):
                scale = None
                for j in range(powers):
                    scaled = [filter_coeffs[j, c, n] * active[n] for n in range(ORDER + 1)]
                    for m in range(ORDER + 1):
                        total = None
                        for n in range(m, ORDER + 1):
                            term = scaled[n] * float(SHIFTED[n][m])
                            total = term if total is None else total + term
                        if scale is not None:
                            total = total * scale
                        weights[freq, (m * 2 + c) * powers + j] = total
                    scale = omega if scale is None else scale * omega

    def tables(r, carry):
        for depth, (weights, out) in enumerate(((weights_out, first_out), (later_weights, later_out))):
            for freq in range(freqs):
                def store(part, value):
                    out[freq, part, r] = value

                coefficients(weights, freq, slow[depth, r], store)
        return carry

    lax.fori_loop(0, stored, tables, 0, unroll=2)


def own_kernel(
    rows_in, powers_in, first_in, later_in, y_matrix,
    middle_out, middle_powers_out, last_out, first_image, last_image,
    left, partial,
):
    count, stored = rows_in.shape[:2]
    freqs = count // 4
    inner = stored - 2 * ORDER

    def write_middle(p, o, value):
        middle_out[p, o] = value

    sweep(
        freqs,
        lambda p, o: rows_in[p, o + ORDER],
        power_of(powers_in, stored),
        lambda freq, part, o: first_in[freq, part, o + ORDER],
        write_middle,
        partial,
        inner,
    )
    for o in range(inner):
        first_image[o] = image_row(freqs, lambda p: middle_out[p, o])
    for plane in range(count):
        split_rows(middle_out[plane], left, plane * inner * 8)
    middle_powers_out[...] = multiply(left, count * inner * 8, y_matrix)

    def write_last(p, o, value):
        last_out[p, o] = value

    sweep(
        freqs,
        lambda p, o: middle_out[p, o + ORDER],
        power_of(middle_powers_out, inner),
        lambda freq, part, o: later_in[freq, part, o + HALO],
        write_last,
        partial,
        inner - 2 * ORDER,
    )
    for o in range(inner - 2 * ORDER):
        last_image[o] = image_row(freqs, lambda p: last_out[p, o])


def upper_kernel(
    rows_in, powers_in, slow_in, weights, first_in, later,
    middle_in, middle_powers_in, last_in, first_image, last_image, y_matrix, from_before,
    middle, middle_powers, last, images,
    edges, left, edge_powers, slow, first, partial,
):
    count, stored = rows_in.shape[:2]
    freqs = count // 4
    inner = stored - 2 * ORDER
    tile = lax.axis_index("tile")

    @pl.when(tile == 0)
    def _():
        for p in range(count):
            edges[p, HALO - 1] = jnp.zeros((8, 128), F32)
            for k in range(1, HALO):
                edges[p, HALO - 1 - k] = -rows_in[p, k - 1]
        slow[ORDER - 1] = slow_in[0, 0]
        for k in range(1, ORDER):
            slow[ORDER - 1 - k] = slow_in[0, k - 1]

    @pl.when(tile > 0)
    def _():
        for p in range(count):
            edges[p] = from_before[pl.ds(p * HALO, HALO)]
        slow[...] = from_before[pl.ds(count * HALO, ORDER)]

    for p in range(count):
        split_rows(edges[p], left, p * HALO * 8)
    edge_powers[...] = multiply(left, count * HALO * 8, y_matrix)
    for r in range(ORDER):
        for freq in range(freqs):
            def store(part, value):
                first[freq, part, r] = value

            coefficients(weights, freq, slow[r], store)

    outer = power_of(edge_powers, HALO)
    own = power_of(powers_in, stored)

    def write_middle(p, o, value):
        middle[p, o] = value

    sweep(
        freqs,
        lambda p, o: edges[p, o + ORDER] if o < ORDER else rows_in[p, o - ORDER],
        lambda p, m, row: outer(p, m, row) if row < HALO else own(p, m, row - HALO),
        lambda freq, part, o: (
            first[freq, part, o] if o < ORDER else first_in[freq, part, o - ORDER]
        ),
        write_middle,
        partial,
        2 * ORDER,
    )
    for p in range(count):
        middle[p, pl.ds(2 * ORDER, inner)] = middle_in[p]
        split_rows(middle[p, pl.ds(0, 2 * ORDER)], left, p * HALO * 8)
    edge_powers[...] = multiply(left, count * HALO * 8, y_matrix)
    for p in range(count):
        size = HALO * 8
        middle_powers[pl.ds(p * stored * 8, size), :] = edge_powers[pl.ds(p * size, size), :]
        middle_powers[pl.ds((p * stored + HALO) * 8, inner * 8), :] = middle_powers_in[
            pl.ds(p * inner * 8, inner * 8), :
        ]

    def write_last(p, o, value):
        last[p, o] = value

    sweep(
        freqs,
        lambda p, o: middle[p, o + ORDER],
        power_of(middle_powers, stored),
        lambda freq, part, o: later[freq, part, o],
        write_last,
        partial,
        HALO,
    )
    for p in range(count):
        last[p, pl.ds(HALO, inner - HALO)] = last_in[p]
    images[0, pl.ds(ORDER, inner)] = first_image[...]
    images[1, pl.ds(HALO, inner - HALO)] = last_image[...]
    for k in range(ORDER):
        images[0, k] = image_row(freqs, lambda p: middle[p, k + ORDER])
    for k in range(HALO):
        images[1, k] = image_row(freqs, lambda p: last[p, k])


def lower_rows(
    freq, width, last_tile, own, after, slow, edges, left, edge_powers, first, middle, last, partial
):
    rows_in, powers_in, weights, first_in, later, middle_in, middle_powers_in, y_matrix = own
    count, stored = rows_in.shape[:2]
    freqs = count // 4

    @pl.when(last_tile)
    def _():
        for k in range(4):
            edges[k, 0] = jnp.zeros((8, 128), F32)
            for r in range(1, HALO):
                edges[k, r] = -rows_in[k * freqs + freq, width - r]

    @pl.when(jnp.logical_not(last_tile))
    def _():
        for k in range(4):
            edges[k] = after[pl.ds(k * HALO, HALO)]

    for k in range(4):
        split_rows(edges[k], left, k * HALO * 8)
    edge_powers[...] = multiply(left, 4 * HALO * 8, y_matrix)
    for r in range(ORDER):
        def store(part, value):
            first[part, r] = value

        coefficients(weights, freq, slow[r], store)

    outer = power_of(edge_powers, HALO)
    inside = power_of(powers_in, stored)
    done = power_of(middle_powers_in, stored)

    def write_middle(k, o, value):
        middle[k, o] = value

    def write_last(k, o, value):
        last[k, o] = value

    sweep(
        1,
        lambda k, o: (
            rows_in[k * freqs + freq, o + width - ORDER] if o < ORDER else edges[k, o - ORDER]
        ),
        lambda k, m, row: (
            inside(k * freqs + freq, m, row + width - HALO)
            if row < HALO
            else outer(k, m, row - HALO)
        ),
        lambda _, part, o: (
            first_in[freq, part, o + width - ORDER] if o < ORDER else first[part, o - ORDER]
        ),
        write_middle,
        partial,
        2 * ORDER,
    )
    for k in range(4):
        split_rows(middle[k], left, k * HALO * 8)
    edge_powers[...] = multiply(left, 4 * HALO * 8, y_matrix)
    sweep(
        1,
        lambda k, o: (
            middle_in[k * freqs + freq, o + width - ORDER] if o < ORDER else middle[k, o - ORDER]
        ),
        lambda k, m, row: (
            done(k * freqs + freq, m, row + width - HALO)
            if row < HALO
            else outer(k, m, row - HALO)
        ),
        lambda _, part, o: later[freq, part, o + width - HALO],
        write_last,
        partial,
        HALO,
    )


def lower_kernel(freq, aperture, slow_in, *refs):
    own, refs = refs[:8], refs[8:]
    tile = lax.axis_index("tile")
    width = aperture[tile]
    last_tile = tile == lax.axis_size("tile") - 1
    if freq == 0:
        after, receiver_rows, images, slow, *scratch = refs

        @pl.when(last_tile)
        def _():
            slow[0] = slow_in[0, width - 1]
            for k in range(1, ORDER):
                slow[k] = slow_in[0, width - k]

        @pl.when(jnp.logical_not(last_tile))
        def _():
            slow[...] = after[pl.ds(4 * HALO, ORDER)]
    else:
        after, slow, receiver_rows, images, *scratch = refs
    lower_rows(freq, width, last_tile, own, after, slow, *scratch)
    middle, last = scratch[4:6]
    receiver_rows[...] = last[pl.ds(2, 2)]
    for k in range(ORDER):
        images[k] = image_row(1, lambda p: middle[p, k])
    for k in range(HALO):
        images[ORDER + k] = image_row(1, lambda p: last[p, k])


def final_kernel(freq, aperture, slow, *refs):
    own, refs = refs[:8], refs[8:]
    after, last_in, images_in, *refs = refs
    others, refs = refs[: 2 * freq], refs[2 * freq :]
    image_out, receiver_hbm, receiver_out, sems, flat, rows, images, *scratch = refs
    tile = lax.axis_index("tile")
    width = aperture[tile]
    lower_rows(freq, width, tile == lax.axis_size("tile") - 1, own, after, slow, *scratch)
    middle, last = scratch[4:6]
    count, inner = last_in.shape[:2]
    freqs = count // 4
    stored = own[0].shape[1]
    row_tiles = stored // 8

    def put(slot, load_row, store_tile):
        for r in range(stored):
            at = (r // 8) * 64 + r % 8
            flat[slot, pl.ds(at, 8, stride=8), :] = jnp.where(r < width, load_row(r), 0.0)
        for i in range(row_tiles):
            for j in range(8):
                store_tile(i, j, flat[slot, pl.ds((i * 8 + j) * 8, 8), :])

    sent = []
    for part in range(2):
        for at in range(freqs):
            def store_receiver(i, j, value):
                receiver_out[part, at, pl.ds(8 * i, 8), pl.ds(128 * j, 128)] = value

            p = part * freqs + at
            rows[p, pl.ds(0, inner)] = last_in[2 * freqs + p]
            rows[p, pl.ds(width - HALO, HALO)] = last[2 + part] if at == freq else others[2 * at][part]
            put(NDEPTH + p, lambda r: rows[p, r], store_receiver)
            sent.append(
                pltpu.make_async_copy(
                    receiver_out.at[part, at], receiver_hbm.at[part, at], sems.at[p]
                )
            )
            sent[-1].start()

    images[:, pl.ds(0, stored - ORDER)] = images_in[...]
    for k in range(ORDER + HALO):
        if k < ORDER:
            total = image_row(1, lambda p: middle[p, k])
        else:
            total = image_row(1, lambda p: last[p, k - ORDER])
        for at in range(freq):
            total = total + others[2 * at + 1][k]
        if k < ORDER:
            images[0, width - ORDER + k] = total
        else:
            images[1, width - HALO + k - ORDER] = total
    columns = image_out.shape[3]
    for depth in range(NDEPTH):
        def store_image(i, j, value):
            image_out[
                128 * j // columns, depth, pl.ds(8 * i, 8), pl.ds(128 * j % columns, 128)
            ] = value

        put(depth, lambda r: images[depth, r], store_image)
    for copy in sent:
        copy.wait()


def passed_along(value, axis, steps):
    count = lax.axis_size(axis)
    initial, last = (max(0, -steps), min(count, count - steps))
    return lax.ppermute(value, axis, [(source, source + steps) for source in range(initial, last)])


def kernel(body, out_shape, in_specs, scratch, name, cost=1000):
    return pl.pallas_call(
        body,
        out_shape=out_shape,
        in_specs=in_specs,
        out_specs=(VMEM,) * len(out_shape),
        scratch_shapes=scratch,
        compiler_params=pltpu.CompilerParams(vmem_limit_bytes=24 << 20),
        cost_estimate=pl.CostEstimate(flops=cost, bytes_accessed=cost, transcendentals=0),
        name=name,
    )


def shards(source_field, receiver_field, slowness, frequency, order_table, filter_coeffs, aperture):
    freqs, stored = source_field.shape[1:3]
    count = 4 * freqs
    parts = 2 * (ORDER + 1)
    inner = stored - 2 * ORDER
    wide = ORDER * 128

    def shape(*dims):
        return jax.ShapeDtypeStruct(dims, F32)

    def rows(*lead):
        return shape(*lead, 8, 128)

    def same(value):
        return pltpu.VMEM(value.shape, value.dtype)

    def scratch(*lead):
        return same(rows(*lead))

    planes = lax.all_gather(slowness, "freq", axis=0)
    halo = rows(count * HALO + ORDER)
    flat = pltpu.VMEM((stored * 8, 128), F32)
    (slow,) = kernel(
        slow_kernel,
        (rows(NDEPTH, stored),),
        [VMEM],
        [pltpu.VMEM((NDEPTH, stored * 8, 128), F32)],
        "slow",
        1 << 30,
    )(planes)
    (ahead,) = kernel(
        ahead_kernel, (halo,), [SMEM] + [VMEM] * 3, [flat] * count, "ahead"
    )(aperture, source_field, receiver_field, slow)
    from_before = passed_along(ahead, "tile", 1)

    y_matrix = jnp.asarray(y_weights(), BF16)
    coeffs = jnp.transpose(filter_coeffs, (2, 0, 1))
    terms = parts * coeffs.shape[0]
    *behind, own_rows, own_powers, weights, first, later = kernel(
        rows_kernel,
        (
            rows(4 * HALO + ORDER),
            *[rows(4 * HALO)] * (freqs - 1),
            rows(count, stored),
            shape(count * stored * 8, wide),
            rows(freqs, terms),
            rows(freqs, parts, stored),
            rows(freqs, parts, stored),
        ),
        [SMEM] * 3 + [VMEM] * 4,
        [
            pltpu.VMEM((count, stored * 8, 128), F32),
            pltpu.VMEM((count * stored * 8, 512), BF16),
            scratch(freqs, terms),
        ],
        "rows",
    )(frequency, order_table, coeffs, source_field, receiver_field, slow, y_matrix)
    from_after = [passed_along(value, "tile", -1) for value in behind]

    inside = kernel(
        own_kernel,
        (
            rows(count, inner),
            shape(count * inner * 8, wide),
            rows(count, inner - HALO),
            rows(inner),
            rows(inner - HALO),
        ),
        [VMEM] * 5,
        [pltpu.VMEM((count * inner * 8, 512), BF16), scratch(2, inner)],
        "own",
    )(own_rows, own_powers, first, later, y_matrix)
    edge = [
        scratch(count, HALO),
        pltpu.VMEM((count * HALO * 8, 512), BF16),
        pltpu.VMEM((count * HALO * 8, wide), F32),
        scratch(ORDER),
        scratch(freqs, parts, ORDER),
    ]
    tables = (own_rows, own_powers, slow, weights, first, later)
    upper = kernel(
        upper_kernel,
        (
            rows(count, stored),
            shape(count * stored * 8, wide),
            rows(count, inner),
            rows(NDEPTH, stored - ORDER),
        ),
        [VMEM] * (len(tables) + len(inside) + 2),
        edge + [scratch(2, HALO)],
        "upper",
    )(*tables, *inside, y_matrix, from_before)
    own = (own_rows, own_powers, weights, first, later, *upper[:2], y_matrix)
    edge = [
        scratch(4, HALO),
        pltpu.VMEM((4 * HALO * 8, 512), BF16),
        pltpu.VMEM((4 * HALO * 8, wide), F32),
        scratch(parts, ORDER),
        scratch(4, HALO),
        scratch(4, HALO),
        scratch(2, HALO),
    ]
    others = []
    for freq in range(freqs - 1):
        operands = (aperture, slow, *own, from_after[freq])
        results = (rows(2, HALO), rows(ORDER + HALO))
        if freq == 0:
            results = (*results, rows(ORDER))
        else:
            operands = (*operands, slow_after)
        out = kernel(
            functools.partial(lower_kernel, freq),
            results,
            [SMEM] + [VMEM] * (len(operands) - 1),
            edge,
            "lower",
        )(*operands)
        others += out[:2]
        if freq == 0:
            slow_after = out[2]
    operands = (aperture, slow_after, *own, from_after[-1], *upper[2:], *others)
    image_parts, receiver_out = pl.pallas_call(
        functools.partial(final_kernel, freqs - 1),
        out_shape=(
            shape(lax.axis_size("freq"), *slowness.shape),
            shape(*receiver_field.shape),
        ),
        in_specs=[SMEM] + [VMEM] * (len(operands) - 1),
        out_specs=(VMEM, pl.BlockSpec(memory_space=pl.ANY)),
        scratch_shapes=[
            same(receiver_field),
            pltpu.SemaphoreType.DMA((2 * freqs,)),
            pltpu.VMEM((NDEPTH + 2 * freqs, stored * 8, 128), F32),
            scratch(2 * freqs, stored),
            scratch(NDEPTH, stored),
            *edge,
        ],
        compiler_params=pltpu.CompilerParams(vmem_limit_bytes=24 << 20),
        cost_estimate=pl.CostEstimate(flops=1000, bytes_accessed=1000, transcendentals=0),
        name="final",
    )(*operands)
    exchanged = lax.all_to_all(image_parts, "freq", 0, 0)
    return jnp.sum(exchanged, axis=0), receiver_out


def solution(mesh):
    placed = (
        P(None, "freq", "tile", None),
        P(None, "freq", "tile", None),
        P(None, "tile", "freq"),
        P("freq"),
        P(None, "freq"),
        P(),
        P(),
    )
    return jax.shard_map(
        shards,
        mesh=mesh,
        in_specs=placed,
        out_specs=(P(None, "tile", "freq"), P(None, "freq", "tile", None)),
        check_vma=False,
    )
```

```python
import functools
from math import comb

import jax
import jax.numpy as jnp
import numpy as np
from jax import lax
from jax.experimental import pallas as pl
from jax.experimental.pallas import tpu as pltpu
from jax.sharding import PartitionSpec as P

ORDER = 4
NDEPTH = 2
HALO = ORDER * NDEPTH
F32 = jnp.float32
BF16 = jnp.bfloat16
VMEM = pl.BlockSpec(memory_space=pltpu.VMEM)
SMEM = pl.BlockSpec(memory_space=pltpu.SMEM)

SHIFTED = ((1,), (-1, 2), (1, -8, 8), (-1, 18, -48, 32), (1, -32, 160, -256, 128))


def y_weights():
    out = np.zeros((256, ORDER * 128), np.float32)

    def add(k, column, sign):
        for m in range(1, ORDER + 1):
            for lane in range(max(0, column - m), min(128, column + m + 1)):
                out[k, (m - 1) * 128 + lane] += sign * comb(2 * m, m + lane - column) / 16.0**m

    for lane in range(128):
        add(lane, lane, 1)
    for lane in range(4):
        add(128 + lane, 128 + lane, 1)
        add(128 + 124 + lane, lane - 4, 1)
    for k in range(3):
        add(128 + 8 + k, -2 - k, -1)
        add(128 + 5 + k, 131 - k, -1)
    return out


def seam(values):
    lane = lax.broadcasted_iota(jnp.int32, (1, 8, 128), 2)
    sub = lax.broadcasted_iota(jnp.int32, (1, 8, 128), 1)
    inner = ((lane < 4) & (sub < 7)) | ((lane >= 124) & (sub > 0))
    edge = ((sub == 0) & (lane >= 8) & (lane <= 10)) | ((sub == 7) & (lane >= 5) & (lane <= 7))
    beside = jnp.where(lane < 64, pltpu.roll(values, 7, 1), pltpu.roll(values, 1, 1))
    return jnp.where(inner, beside, jnp.where(edge, pltpu.roll(values, 8, 2), 0.0))


def split_rows(values, left, at):
    rows = values.shape[0]
    for column, x in enumerate((values, seam(values))):
        x = x.reshape(rows * 8, 128)
        high = x.astype(BF16)
        left[pl.ds(at, rows * 8), pl.ds(128 * column, 128)] = high
        left[pl.ds(at, rows * 8), pl.ds(256 + 128 * column, 128)] = (x - high.astype(F32)).astype(BF16)


def multiply(left, rows, y_matrix):
    matrix = y_matrix[...]
    right = jnp.concatenate([matrix, matrix], axis=0)
    return jnp.dot(left[pl.ds(0, rows), :], right, preferred_element_type=F32)


def to_rows(flat, load_tile, row_tiles):
    for i in range(row_tiles):
        for j in range(8):
            flat[pl.ds((i * 8 + j) * 8, 8), :] = load_tile(i, j)


def row_of(flat, row):
    start = (row // 8) * 64 + row % 8
    return flat[pl.ds(start, 8, stride=8), :]


def planes_of(source, receiver):
    def loader(field, part, freq):
        return lambda i, j: field[part, freq, pl.ds(8 * i, 8), pl.ds(128 * j, 128)]

    return [
        loader(field, part, freq)
        for field in (source, receiver)
        for part in range(2)
        for freq in range(source.shape[1])
    ]


def slow_tile(planes, depth):
    columns = planes.shape[3]
    return lambda i, j: planes[
        128 * j // columns, depth, pl.ds(8 * i, 8), pl.ds(128 * j % columns, 128)
    ]


def slow_kernel(planes, out, flat):
    row_tiles = planes.shape[2] // 8
    for depth in range(NDEPTH):
        to_rows(flat.at[depth], slow_tile(planes, depth), row_tiles)
        for r in range(planes.shape[2]):
            out[depth, r] = row_of(flat.at[depth], r)


def ahead_kernel(aperture, source, receiver, slow, ahead, *flats):
    width = aperture[lax.axis_index("tile")]
    row_tiles = source.shape[2] // 8
    for plane, load in enumerate(planes_of(source, receiver)):
        to_rows(flats[plane], load, row_tiles)
        for k in range(HALO):
            ahead[plane * HALO + k] = row_of(flats[plane], width - HALO + k)
    end = 4 * source.shape[1] * HALO
    ahead[pl.ds(end, ORDER)] = slow[0, pl.ds(width - ORDER, ORDER)]


def coefficients(weights, freq, slow_row, store):
    powers = weights.shape[1] // (2 * (ORDER + 1))
    for part in range(2 * (ORDER + 1)):
        value = weights[freq, part * powers + powers - 1]
        for power in range(powers - 2, -1, -1):
            value = value * slow_row + weights[freq, part * powers + power]
        store(part, value)


def sweep(freqs, fields, power, coefficient, write, partial, rows, which=(0, 1)):
    def feed(held, value):
        kept = []
        for last in held:
            kept.append(value)
            value = value + last
        return kept, value

    for freq in range(freqs):
        for field in which:
            for part in range(2):
                p = (2 * field + part) * freqs + freq
                held = []
                for m in range(1, ORDER + 1):
                    chain = []
                    for k in range(2 * m):
                        value = power(p, m, ORDER - m + k)
                        chain, value = feed(chain, value)
                        chain.append(value)
                    held.append(chain)
                for o in range(rows):
                    kept, by_re, by_im = [], None, None
                    for m in range(ORDER + 1):
                        if m == 0:
                            value = fields(p, o)
                        else:
                            chain, value = feed(held[m - 1], power(p, m, o + ORDER + m))
                            kept.append(chain)
                        re = coefficient(freq, 2 * m, o) * value
                        im = coefficient(freq, 2 * m + 1, o) * value
                        by_re = re if by_re is None else by_re + re
                        by_im = im if by_im is None else by_im + im
                    held = kept
                    if part == 0:
                        partial[0, o] = by_re
                        partial[1, o] = by_im
                    elif field == 0:
                        write(p - freqs, o, partial[0, o] + by_im)
                        write(p, o, by_re - partial[1, o])
                    else:
                        write(p - freqs, o, partial[0, o] - by_im)
                        write(p, o, by_re + partial[1, o])


def image_row(freqs, load):
    total = None
    for k in range(2 * freqs):
        term = load(k) * load(2 * freqs + k)
        total = term if total is None else total + term
    return total


def power_of(ref, stride):
    def power(p, m, row):
        at = (p * stride + row) * 8
        at = at if isinstance(at, int) else pl.multiple_of(at, 8)
        return ref[pl.ds(at, 8), pl.ds(128 * (m - 1), 128)]

    return power


def rows_kernel(
    frequency, order_table, filter_coeffs, source, receiver, slow, y_matrix, *others
):
    powers = filter_coeffs.shape[0]
    behind, others = others[: source.shape[1]], others[source.shape[1] :]
    rows_out, powers_out, weights_out, first_out, later_out, flat, left, later_weights = others
    freqs, stored = source.shape[1:3]
    count = 4 * freqs
    row_tiles = stored // 8
    for plane, load in enumerate(planes_of(source, receiver)):
        to_rows(flat.at[plane], load, row_tiles)
        for r in range(stored):
            rows_out[plane, r] = row_of(flat.at[plane], r)
    for plane in range(count):
        behind[plane % freqs][pl.ds(plane // freqs * HALO, HALO)] = rows_out[plane, pl.ds(0, HALO)]
    behind[0][pl.ds(4 * HALO, ORDER)] = slow[0, pl.ds(0, ORDER)]
    for plane in range(count):
        split_rows(rows_out[plane], left, plane * stored * 8)
    powers_out[...] = multiply(left, count * stored * 8, y_matrix)

    for depth, weights in enumerate((weights_out, later_weights)):
        for freq in range(freqs):
            omega = jnp.full((8, 128), frequency[freq], F32)
            active = [
                jnp.full((8, 128), jnp.where(order_table[depth, freq] >= n, 1.0, 0.0), F32)
                for n in range(ORDER + 1)
            ]
            for c in range(2):
                scale = None
                for j in range(powers):
                    scaled = [filter_coeffs[j, c, n] * active[n] for n in range(ORDER + 1)]
                    for m in range(ORDER + 1):
                        total = None
                        for n in range(m, ORDER + 1):
                            term = scaled[n] * float(SHIFTED[n][m])
                            total = term if total is None else total + term
                        if scale is not None:
                            total = total * scale
                        weights[freq, (m * 2 + c) * powers + j] = total
                    scale = omega if scale is None else scale * omega

    def tables(r, carry):
        for depth, (weights, out) in enumerate(((weights_out, first_out), (later_weights, later_out))):
            for freq in range(freqs):
                def store(part, value):
                    out[freq, part, r] = value

                coefficients(weights, freq, slow[depth, r], store)
        return carry

    lax.fori_loop(0, stored, tables, 0, unroll=2)


def own_kernel(
    rows_in, powers_in, first_in, later_in, y_matrix,
    middle_out, middle_powers_out, last_out, first_image, last_image,
    left, partial,
):
    count, stored = rows_in.shape[:2]
    freqs = count // 4
    inner = stored - 2 * ORDER

    def write_middle(p, o, value):
        middle_out[p, o] = value

    sweep(
        freqs,
        lambda p, o: rows_in[p, o + ORDER],
        power_of(powers_in, stored),
        lambda freq, part, o: first_in[freq, part, o + ORDER],
        write_middle,
        partial,
        inner,
    )
    for o in range(inner):
        first_image[o] = image_row(freqs, lambda p: middle_out[p, o])
    for plane in range(count):
        split_rows(middle_out[plane], left, plane * inner * 8)
    middle_powers_out[...] = multiply(left, count * inner * 8, y_matrix)

    def write_last(p, o, value):
        last_out[p, o] = value

    sweep(
        freqs,
        lambda p, o: middle_out[p, o + ORDER],
        power_of(middle_powers_out, inner),
        lambda freq, part, o: later_in[freq, part, o + HALO],
        write_last,
        partial,
        inner - 2 * ORDER,
    )
    for o in range(inner - 2 * ORDER):
        last_image[o] = image_row(freqs, lambda p: last_out[p, o])


def upper_kernel(
    rows_in, powers_in, slow_in, weights, first_in, later,
    middle_in, middle_powers_in, last_in, first_image, last_image, y_matrix, from_before,
    middle, middle_powers, last, images,
    edges, left, edge_powers, slow, first, partial,
):
    count, stored = rows_in.shape[:2]
    freqs = count // 4
    inner = stored - 2 * ORDER
    tile = lax.axis_index("tile")

    @pl.when(tile == 0)
    def _():
        for p in range(count):
            edges[p, HALO - 1] = jnp.zeros((8, 128), F32)
            for k in range(1, HALO):
                edges[p, HALO - 1 - k] = -rows_in[p, k - 1]
        slow[ORDER - 1] = slow_in[0, 0]
        for k in range(1, ORDER):
            slow[ORDER - 1 - k] = slow_in[0, k - 1]

    @pl.when(tile > 0)
    def _():
        for p in range(count):
            edges[p] = from_before[pl.ds(p * HALO, HALO)]
        slow[...] = from_before[pl.ds(count * HALO, ORDER)]

    for p in range(count):
        split_rows(edges[p], left, p * HALO * 8)
    edge_powers[...] = multiply(left, count * HALO * 8, y_matrix)
    for r in range(ORDER):
        for freq in range(freqs):
            def store(part, value):
                first[freq, part, r] = value

            coefficients(weights, freq, slow[r], store)

    outer = power_of(edge_powers, HALO)
    own = power_of(powers_in, stored)

    def write_middle(p, o, value):
        middle[p, o] = value

    sweep(
        freqs,
        lambda p, o: edges[p, o + ORDER] if o < ORDER else rows_in[p, o - ORDER],
        lambda p, m, row: outer(p, m, row) if row < HALO else own(p, m, row - HALO),
        lambda freq, part, o: (
            first[freq, part, o] if o < ORDER else first_in[freq, part, o - ORDER]
        ),
        write_middle,
        partial,
        2 * ORDER,
    )
    for p in range(count):
        middle[p, pl.ds(2 * ORDER, inner)] = middle_in[p]
        split_rows(middle[p, pl.ds(0, 2 * ORDER)], left, p * HALO * 8)
    edge_powers[...] = multiply(left, count * HALO * 8, y_matrix)
    for p in range(count):
        size = HALO * 8
        middle_powers[pl.ds(p * stored * 8, size), :] = edge_powers[pl.ds(p * size, size), :]
        middle_powers[pl.ds((p * stored + HALO) * 8, inner * 8), :] = middle_powers_in[
            pl.ds(p * inner * 8, inner * 8), :
        ]

    def write_last(p, o, value):
        last[p, o] = value

    sweep(
        freqs,
        lambda p, o: middle[p, o + ORDER],
        power_of(middle_powers, stored),
        lambda freq, part, o: later[freq, part, o],
        write_last,
        partial,
        HALO,
    )
    for p in range(count):
        last[p, pl.ds(HALO, inner - HALO)] = last_in[p]
    images[0, pl.ds(ORDER, inner)] = first_image[...]
    images[1, pl.ds(HALO, inner - HALO)] = last_image[...]
    for k in range(ORDER):
        images[0, k] = image_row(freqs, lambda p: middle[p, k + ORDER])
    for k in range(HALO):
        images[1, k] = image_row(freqs, lambda p: last[p, k])


def lower_rows(
    freq, width, last_tile, own, after, slow, edges, left, edge_powers, first, middle, last, partial
):
    rows_in, powers_in, weights, first_in, later, middle_in, middle_powers_in, y_matrix = own
    count, stored = rows_in.shape[:2]
    freqs = count // 4

    @pl.when(last_tile)
    def _():
        for k in range(4):
            edges[k, 0] = jnp.zeros((8, 128), F32)
            for r in range(1, HALO):
                edges[k, r] = -rows_in[k * freqs + freq, width - r]

    @pl.when(jnp.logical_not(last_tile))
    def _():
        for k in range(4):
            edges[k] = after[pl.ds(k * HALO, HALO)]

    for k in range(4):
        split_rows(edges[k], left, k * HALO * 8)
    edge_powers[...] = multiply(left, 4 * HALO * 8, y_matrix)
    for r in range(ORDER):
        def store(part, value):
            first[part, r] = value

        coefficients(weights, freq, slow[r], store)

    outer = power_of(edge_powers, HALO)
    inside = power_of(powers_in, stored)
    done = power_of(middle_powers_in, stored)

    def write_middle(k, o, value):
        middle[k, o] = value

    def write_last(k, o, value):
        last[k, o] = value

    sweep(
        1,
        lambda k, o: (
            rows_in[k * freqs + freq, o + width - ORDER] if o < ORDER else edges[k, o - ORDER]
        ),
        lambda k, m, row: (
            inside(k * freqs + freq, m, row + width - HALO)
            if row < HALO
            else outer(k, m, row - HALO)
        ),
        lambda _, part, o: (
            first_in[freq, part, o + width - ORDER] if o < ORDER else first[part, o - ORDER]
        ),
        write_middle,
        partial,
        2 * ORDER,
    )
    for k in range(4):
        split_rows(middle[k], left, k * HALO * 8)
    edge_powers[...] = multiply(left, 4 * HALO * 8, y_matrix)
    sweep(
        1,
        lambda k, o: (
            middle_in[k * freqs + freq, o + width - ORDER] if o < ORDER else middle[k, o - ORDER]
        ),
        lambda k, m, row: (
            done(k * freqs + freq, m, row + width - HALO)
            if row < HALO
            else outer(k, m, row - HALO)
        ),
        lambda _, part, o: later[freq, part, o + width - HALO],
        write_last,
        partial,
        HALO,
    )


def lower_kernel(freq, aperture, slow_in, *refs):
    own, refs = refs[:8], refs[8:]
    tile = lax.axis_index("tile")
    width = aperture[tile]
    last_tile = tile == lax.axis_size("tile") - 1
    if freq == 0:
        after, receiver_rows, images, slow, *scratch = refs

        @pl.when(last_tile)
        def _():
            slow[0] = slow_in[0, width - 1]
            for k in range(1, ORDER):
                slow[k] = slow_in[0, width - k]

        @pl.when(jnp.logical_not(last_tile))
        def _():
            slow[...] = after[pl.ds(4 * HALO, ORDER)]
    else:
        after, slow, receiver_rows, images, *scratch = refs
    lower_rows(freq, width, last_tile, own, after, slow, *scratch)
    middle, last = scratch[4:6]
    receiver_rows[...] = last[pl.ds(2, 2)]
    for k in range(ORDER):
        images[k] = image_row(1, lambda p: middle[p, k])
    for k in range(HALO):
        images[ORDER + k] = image_row(1, lambda p: last[p, k])


def final_kernel(freq, aperture, slow, *refs):
    own, refs = refs[:8], refs[8:]
    after, last_in, images_in, *refs = refs
    others, refs = refs[: 2 * freq], refs[2 * freq :]
    image_out, receiver_hbm, receiver_out, sems, flat, rows, images, *scratch = refs
    tile = lax.axis_index("tile")
    width = aperture[tile]
    middle, last = scratch[4:6]
    count, inner = last_in.shape[:2]
    freqs = count // 4
    stored = own[0].shape[1]
    row_tiles = stored // 8

    def put(slot, load_row, store_tile):
        for r in range(stored):
            at = (r // 8) * 64 + r % 8
            flat[slot, pl.ds(at, 8, stride=8), :] = jnp.where(r < width, load_row(r), 0.0)
        for i in range(row_tiles):
            for j in range(8):
                store_tile(i, j, flat[slot, pl.ds((i * 8 + j) * 8, 8), :])

    sent = []

    def send(at, load_last):
        for part in range(2):
            def store_receiver(i, j, value):
                receiver_out[part, at, pl.ds(8 * i, 8), pl.ds(128 * j, 128)] = value

            p = part * freqs + at
            rows[p, pl.ds(0, inner)] = last_in[2 * freqs + p]
            rows[p, pl.ds(width - HALO, HALO)] = load_last(part)
            put(NDEPTH + p, lambda r: rows[p, r], store_receiver)
            sent.append(
                pltpu.make_async_copy(
                    receiver_out.at[part, at], receiver_hbm.at[part, at], sems.at[p]
                )
            )
            sent[-1].start()

    for at in range(freq):
        send(at, lambda part: others[2 * at][part])
    lower_rows(freq, width, tile == lax.axis_size("tile") - 1, own, after, slow, *scratch)
    send(freq, lambda part: last[2 + part])

    images[:, pl.ds(0, stored - ORDER)] = images_in[...]
    for k in range(ORDER + HALO):
        if k < ORDER:
            total = image_row(1, lambda p: middle[p, k])
        else:
            total = image_row(1, lambda p: last[p, k - ORDER])
        for at in range(freq):
            total = total + others[2 * at + 1][k]
        if k < ORDER:
            images[0, width - ORDER + k] = total
        else:
            images[1, width - HALO + k - ORDER] = total
    columns = image_out.shape[3]
    for depth in range(NDEPTH):
        def store_image(i, j, value):
            image_out[
                128 * j // columns, depth, pl.ds(8 * i, 8), pl.ds(128 * j % columns, 128)
            ] = value

        put(depth, lambda r: images[depth, r], store_image)
    for copy in sent:
        copy.wait()


def passed_along(value, axis, steps):
    count = lax.axis_size(axis)
    initial, last = (max(0, -steps), min(count, count - steps))
    return lax.ppermute(value, axis, [(source, source + steps) for source in range(initial, last)])


def kernel(body, out_shape, in_specs, scratch, name, cost=1000):
    return pl.pallas_call(
        body,
        out_shape=out_shape,
        in_specs=in_specs,
        out_specs=(VMEM,) * len(out_shape),
        scratch_shapes=scratch,
        compiler_params=pltpu.CompilerParams(vmem_limit_bytes=24 << 20),
        cost_estimate=pl.CostEstimate(flops=cost, bytes_accessed=cost, transcendentals=0),
        name=name,
    )


def shards(source_field, receiver_field, slowness, frequency, order_table, filter_coeffs, aperture):
    freqs, stored = source_field.shape[1:3]
    count = 4 * freqs
    parts = 2 * (ORDER + 1)
    inner = stored - 2 * ORDER
    wide = ORDER * 128

    def shape(*dims):
        return jax.ShapeDtypeStruct(dims, F32)

    def rows(*lead):
        return shape(*lead, 8, 128)

    def same(value):
        return pltpu.VMEM(value.shape, value.dtype)

    def scratch(*lead):
        return same(rows(*lead))

    planes = lax.all_gather(slowness, "freq", axis=0)
    halo = rows(count * HALO + ORDER)
    flat = pltpu.VMEM((stored * 8, 128), F32)
    (slow,) = kernel(
        slow_kernel,
        (rows(NDEPTH, stored),),
        [VMEM],
        [pltpu.VMEM((NDEPTH, stored * 8, 128), F32)],
        "slow",
        1 << 30,
    )(planes)
    (ahead,) = kernel(
        ahead_kernel, (halo,), [SMEM] + [VMEM] * 3, [flat] * count, "ahead"
    )(aperture, source_field, receiver_field, slow)
    from_before = passed_along(ahead, "tile", 1)

    y_matrix = jnp.asarray(y_weights(), BF16)
    coeffs = jnp.transpose(filter_coeffs, (2, 0, 1))
    terms = parts * coeffs.shape[0]
    *behind, own_rows, own_powers, weights, first, later = kernel(
        rows_kernel,
        (
            rows(4 * HALO + ORDER),
            *[rows(4 * HALO)] * (freqs - 1),
            rows(count, stored),
            shape(count * stored * 8, wide),
            rows(freqs, terms),
            rows(freqs, parts, stored),
            rows(freqs, parts, stored),
        ),
        [SMEM] * 3 + [VMEM] * 4,
        [
            pltpu.VMEM((count, stored * 8, 128), F32),
            pltpu.VMEM((count * stored * 8, 512), BF16),
            scratch(freqs, terms),
        ],
        "rows",
    )(frequency, order_table, coeffs, source_field, receiver_field, slow, y_matrix)
    from_after = [passed_along(value, "tile", -1) for value in behind]

    inside = kernel(
        own_kernel,
        (
            rows(count, inner),
            shape(count * inner * 8, wide),
            rows(count, inner - HALO),
            rows(inner),
            rows(inner - HALO),
        ),
        [VMEM] * 5,
        [pltpu.VMEM((count * inner * 8, 512), BF16), scratch(2, inner)],
        "own",
    )(own_rows, own_powers, first, later, y_matrix)
    edge = [
        scratch(count, HALO),
        pltpu.VMEM((count * HALO * 8, 512), BF16),
        pltpu.VMEM((count * HALO * 8, wide), F32),
        scratch(ORDER),
        scratch(freqs, parts, ORDER),
    ]
    tables = (own_rows, own_powers, slow, weights, first, later)
    upper = kernel(
        upper_kernel,
        (
            rows(count, stored),
            shape(count * stored * 8, wide),
            rows(count, inner),
            rows(NDEPTH, stored - ORDER),
        ),
        [VMEM] * (len(tables) + len(inside) + 2),
        edge + [scratch(2, HALO)],
        "upper",
    )(*tables, *inside, y_matrix, from_before)
    own = (own_rows, own_powers, weights, first, later, *upper[:2], y_matrix)
    edge = [
        scratch(4, HALO),
        pltpu.VMEM((4 * HALO * 8, 512), BF16),
        pltpu.VMEM((4 * HALO * 8, wide), F32),
        scratch(parts, ORDER),
        scratch(4, HALO),
        scratch(4, HALO),
        scratch(2, HALO),
    ]
    others = []
    for freq in range(freqs - 1):
        operands = (aperture, slow, *own, from_after[freq])
        results = (rows(2, HALO), rows(ORDER + HALO))
        if freq == 0:
            results = (*results, rows(ORDER))
        else:
            operands = (*operands, slow_after)
        out = kernel(
            functools.partial(lower_kernel, freq),
            results,
            [SMEM] + [VMEM] * (len(operands) - 1),
            edge,
            "lower",
        )(*operands)
        others += out[:2]
        if freq == 0:
            slow_after = out[2]
    operands = (aperture, slow_after, *own, from_after[-1], *upper[2:], *others)
    image_parts, receiver_out = pl.pallas_call(
        functools.partial(final_kernel, freqs - 1),
        out_shape=(
            shape(lax.axis_size("freq"), *slowness.shape),
            shape(*receiver_field.shape),
        ),
        in_specs=[SMEM] + [VMEM] * (len(operands) - 1),
        out_specs=(VMEM, pl.BlockSpec(memory_space=pl.ANY)),
        scratch_shapes=[
            same(receiver_field),
            pltpu.SemaphoreType.DMA((2 * freqs,)),
            pltpu.VMEM((NDEPTH + 2 * freqs, stored * 8, 128), F32),
            scratch(2 * freqs, stored),
            scratch(NDEPTH, stored),
            *edge,
        ],
        compiler_params=pltpu.CompilerParams(vmem_limit_bytes=24 << 20),
        cost_estimate=pl.CostEstimate(flops=1000, bytes_accessed=1000, transcendentals=0),
        name="final",
    )(*operands)
    exchanged = lax.all_to_all(image_parts, "freq", 0, 0)
    return jnp.sum(exchanged, axis=0), receiver_out


def solution(mesh):
    placed = (
        P(None, "freq", "tile", None),
        P(None, "freq", "tile", None),
        P(None, "tile", "freq"),
        P("freq"),
        P(None, "freq"),
        P(),
        P(),
    )
    return jax.shard_map(
        shards,
        mesh=mesh,
        in_specs=placed,
        out_specs=(P(None, "tile", "freq"), P(None, "freq", "tile", None)),
        check_vma=False,
    )
```
